256 devices in a mesh: gx: 32 (over z, x), gz: 8 (over y, core).
Axes of the slice: x: 4, y: 4, z: 8, core: 2. Of those that a mesh axis runs over, the one named last changes fastest.
Arguments:
- eta: float32 [1024, 512], P('gx'), may hold values from -0.6 to 0.6
- phis: float32 [1024, 512], P('gx'), may hold values from -3 to 3
- particles: float32 [8, 64, 4, 16, 128], P(None, 'gx', None, 'gz'), as said below
- cell_count: int32 [64, 4, 16], P('gx', None, 'gz'), may hold values from 16 to 128, as said below
- pair_cells: int32 [32, 8, 2, 96], P('gx', 'gz'), may hold values from 0 to 63, as said below
- pair_count: int32 [32, 8, 1], P('gx', 'gz'), may hold values from 24 to 96, as said below
Outputs:
- w_surface: float32 [1024, 512], P('gx')
- density_rate: float32 [64, 4, 16, 128], P('gx', None, 'gz')
The draws below stay inside these ranges and needn't reach their ends.
Inputs may be any that keep to these rules, and one draw needn't show every extreme that they name: `particles`: positions lie inside their cell, cells being cubes of side 2 placed at 2 times their global index; densities lie in 0.8 to 1.2, masses in 0.05 to 0.09. `cell_count`: each device's first cell holds 128 live particles. `pair_cells`: entry 0 is an own cell index, entry 1 a neighbourhood cell index within one cell of it along every dimension; used pairs of one device are distinct. `pair_count`: the first device's list is full.
All inputs are finite; a program needn't handle non-finite values.
Results may differ from the reference program's by a relative error of at most 0.0003.
Values sent between devices are 32-bit elements; how exact they have to be, the bound alone decides.
No kernel may reach another device: no remote copies, remote signals or barrier semaphores. Data moves between devices by JAX's collectives and lax.ppermute only.
A program may use at most 64 MiB of HBM per device.

```python
import jax
import jax.numpy as jnp
from jax import lax

NXH = 1024
NYH = 512
TILE = 128
CXD = 2
CY = 4
CZD = 2
PAIRS = 96
RELAX_SLABS = 64
SLABS_X = 32
SLABS_Z = 8
NXC = 64
NZC = 16
N_GX = 32
N_GZ = 8


def draw_particles(key, part):
    shape_all = (NXC, CY, NZC, TILE)
    key_list = jax.random.split(jax.random.fold_in(key, 3), 8)
    cell_x = lax.broadcasted_iota(jnp.int32, shape_all, 0).astype(jnp.float32)
    cell_y = lax.broadcasted_iota(jnp.int32, shape_all, 1).astype(jnp.float32)
    cell_z = lax.broadcasted_iota(jnp.int32, shape_all, 2).astype(jnp.float32)
    pos_x = (cell_x + jax.random.uniform(key_list[0], shape_all, jnp.float32, 0.02, 0.98)) * 2.0
    pos_y = (cell_y + jax.random.uniform(key_list[1], shape_all, jnp.float32, 0.02, 0.98)) * 2.0
    pos_z = (cell_z + jax.random.uniform(key_list[2], shape_all, jnp.float32, 0.02, 0.98)) * 2.0
    vel_u = jax.random.normal(key_list[3], shape_all, jnp.float32)
    vel_v = jax.random.normal(key_list[4], shape_all, jnp.float32)
    vel_w = jax.random.normal(key_list[5], shape_all, jnp.float32)
    density = jax.random.uniform(key_list[6], shape_all, jnp.float32, 0.8, 1.2)
    masses = jax.random.uniform(key_list[7], shape_all, jnp.float32, 0.05, 0.09)
    return jnp.stack([pos_x, pos_y, pos_z, vel_u, vel_v, vel_w, density, masses], 0)


def draw_cell_count(key, part):
    shape_all = (NXC, CY, NZC)
    counts = jax.random.randint(jax.random.fold_in(key, 5), shape_all, 16, TILE + 1)
    index_x = lax.broadcasted_iota(jnp.int32, shape_all, 0)
    index_y = lax.broadcasted_iota(jnp.int32, shape_all, 1)
    index_z = lax.broadcasted_iota(jnp.int32, shape_all, 2)
    corner = (index_x % CXD == 0) & (index_y == 0) & (index_z % CZD == 0)
    return jnp.where(corner, TILE, counts).astype(jnp.int32)


def pair_lists(key):
    cell_total = CXD * CY * CZD
    candidate_ids = jnp.arange(cell_total * 27, dtype=jnp.int32)
    own_cell = candidate_ids // 27
    offset_ids = candidate_ids % 27
    own_x = own_cell // (CY * CZD)
    own_y = own_cell // CZD % CY
    own_z = own_cell % CZD
    step_x = offset_ids // 9 - 1
    step_y = offset_ids // 3 % 3 - 1
    step_z = offset_ids % 3 - 1
    near_y = own_y + step_y
    inside_y = (near_y >= 0) & (near_y < CY)
    other_cell = (own_x + 1 + step_x) * CY * (CZD + 2) + jnp.clip(near_y, 0, CY - 1) * (CZD + 2) + own_z + 1 + step_z

    def device_list(device_key):
        score_ids = jax.random.randint(device_key, candidate_ids.shape, 0, 1 << 17) * 4096 + candidate_ids
        score_ids = jnp.where(inside_y, score_ids, -1)
        unused_values, chosen = lax.top_k(score_ids, PAIRS)
        return jnp.stack([own_cell[chosen], other_cell[chosen]], 0)
    device_keys = jax.random.split(jax.random.fold_in(key, 11), SLABS_X * SLABS_Z)
    pair_table = jax.vmap(device_list)(device_keys).reshape(SLABS_X, SLABS_Z, 2, PAIRS)
    counts = jax.random.randint(jax.random.fold_in(key, 12), (SLABS_X, SLABS_Z, 1), PAIRS // 4, PAIRS + 1)
    counts = counts.at[0, 0, 0].set(PAIRS)
    return (pair_table.astype(jnp.int32), counts.astype(jnp.int32))


def draw_pair_cells(key, part):
    return pair_lists(key)[0]


def draw_pair_count(key, part):
    return pair_lists(key)[1]


def shard_levels(key, dims, shards, smallest, high):
    loudness = 1.0
    for dim, parts in shards:
        heights = jax.random.uniform(jax.random.fold_in(jax.random.fold_in(key, 6), dim), (parts,), jnp.float32, smallest / len(shards), high / len(shards))
        loudness = loudness * jnp.repeat(jnp.exp(heights), dims[dim] // parts).reshape((-1,) + (1,) * (len(dims) - 1 - dim))
    return loudness


def scatter_about(key, extent, width, most, pieces=(), kind=jnp.bfloat16):
    entries = jax.random.normal(key, extent, jnp.float32) * width
    if len(pieces) > 0:
        entries = shard_levels(key, extent, pieces, -0.22, 0.18) * entries
    return jnp.clip(entries, min=-most, max=most).astype(kind)


def setup_inputs(seed: int = 0) -> dict:
    keys = jax.random.split(jax.random.key(seed), 7)
    eta = scatter_about(keys[0], (NXH, NYH), 0.1, 0.6, ((0, 32),), jnp.float32)
    phis = scatter_about(keys[1], (NXH, NYH), 0.5, 3.0, ((0, 32),), jnp.float32)
    particles = draw_particles(jax.random.fold_in(keys[6], 71), 0)
    cell_count = draw_cell_count(jax.random.fold_in(keys[6], 71), 0)
    pair_cells = draw_pair_cells(jax.random.fold_in(keys[6], 71), 0)
    pair_count = draw_pair_count(jax.random.fold_in(keys[6], 71), 0)
    return dict(eta=eta, phis=phis, particles=particles, cell_count=cell_count, pair_cells=pair_cells, pair_count=pair_count)


TWO_PI = 6.283185307179586
DELTA_COEF = 0.1
SOUND_SPEED = 10.0
KERNEL_COEF = -5.0 * 21.0 / (16.0 * 3.141592653589793)
FIRST_KINDS = (('power', 1), ('power', 2), ('power', 3), ('slope_x', 1), ('slope_y', 1))
SECOND_KINDS = (('power', 1), ('power', 2))
THIRD_KINDS = (('power', 1),)

def wave_number(position, length):
    signed = jnp.where(position < length // 2, position, position - length)
    return signed.astype(jnp.float32) * (TWO_PI / length)

def spectral(field, wave_x, wave_y, wave_abs, kind_list):
    spectrum = jnp.fft.fft2(field)
    results = []
    for kind_name, exponent in kind_list:
        if kind_name == 'power':
            results.append(jnp.real(jnp.fft.ifft2(spectrum * wave_abs ** exponent)))
        elif kind_name == 'slope_x':
            results.append(-jnp.imag(jnp.fft.ifft2(spectrum * wave_x)))
        else:
            results.append(-jnp.imag(jnp.fft.ifft2(spectrum * wave_y)))
    return [result.astype(jnp.float32) for result in results]

def pair_terms(own_tiles, other_tiles):
    gap_x = own_tiles[0][:, :, None] - other_tiles[0][:, None, :]
    gap_y = own_tiles[1][:, :, None] - other_tiles[1][:, None, :]
    gap_z = own_tiles[2][:, :, None] - other_tiles[2][:, None, :]
    radius = jnp.sqrt(gap_x * gap_x + gap_y * gap_y + gap_z * gap_z)
    reach = jnp.maximum(1.0 - 0.5 * radius, 0.0)
    kernel_slope = KERNEL_COEF * reach * reach * reach
    approach = (own_tiles[3][:, :, None] - other_tiles[3][:, None, :]) * gap_x
    approach = approach + (own_tiles[4][:, :, None] - other_tiles[4][:, None, :]) * gap_y
    approach = approach + (own_tiles[5][:, :, None] - other_tiles[5][:, None, :]) * gap_z
    continuity = other_tiles[7][:, None, :] * approach
    diffusion = -2.0 * DELTA_COEF * SOUND_SPEED * (other_tiles[6][:, None, :] - own_tiles[6][:, :, None]) * other_tiles[8][:, None, :]
    return lax.optimization_barrier(jnp.sum(kernel_slope * (continuity + diffusion), axis=2))

def reference(eta, phis, particles, cell_count, pair_cells, pair_count):
    wave_x = wave_number(jnp.arange(NXH, dtype=jnp.int32), NXH)[:, None]
    wave_y = wave_number(jnp.arange(NYH, dtype=jnp.int32), NYH)[None, :]
    wave_abs = jnp.sqrt(wave_x * wave_x + wave_y * wave_y)
    first = spectral(phis, wave_x, wave_y, wave_abs, FIRST_KINDS)
    phi_second = -eta * first[0]
    second = spectral(phi_second, wave_x, wave_y, wave_abs, SECOND_KINDS)
    phi_third = -eta * second[0] - 0.5 * eta * eta * first[1]
    third = spectral(phi_third, wave_x, wave_y, wave_abs, THIRD_KINDS)
    vertical = first[0] + second[0] + eta * first[1] + third[0] + eta * second[1] + 0.5 * eta * eta * first[2]
    scale_x = NXH // N_GX / (2.0 * CXD)
    scale_y = NYH / (2.0 * CY)
    hos_x = particles[0] * scale_x
    hos_y = particles[1] * scale_y
    low_x = jnp.floor(hos_x)
    low_y = jnp.floor(hos_y)
    frac_x = hos_x - low_x
    frac_y = hos_y - low_y
    index_x = low_x.astype(jnp.int32) % NXH
    index_y = low_y.astype(jnp.int32) % NYH
    next_x = (index_x + 1) % NXH
    next_y = (index_y + 1) % NYH

    def bilinear(field):
        lower = (1.0 - frac_y) * field[index_x, index_y] + frac_y * field[index_x, next_y]
        upper = (1.0 - frac_y) * field[next_x, index_y] + frac_y * field[next_x, next_y]
        return (1.0 - frac_x) * lower + frac_x * upper
    targets = jnp.stack([bilinear(first[3]), bilinear(first[4]), bilinear(vertical)], 0)
    top_height = 2.0 * CZD * N_GZ
    depth_factor = jnp.exp((particles[2] - top_height) / top_height)
    relax_reach = 2.0 * RELAX_SLABS * CXD
    closeness = jnp.clip(1.0 - particles[0] / relax_reach, 0.0, 1.0)
    relax_weight = closeness * closeness
    velocity = particles[3:6] + relax_weight * (targets * depth_factor - particles[3:6])
    slot_live = jnp.arange(TILE, dtype=jnp.int32) < cell_count[..., None]
    mass_live = jnp.where(slot_live, particles[7], 0.0)
    volume_live = jnp.where(slot_live, particles[7] / particles[6], 0.0)
    channels = jnp.concatenate([particles[0:3], velocity, particles[6:7], mass_live[None], volume_live[None]], 0)
    padded = jnp.pad(channels, ((0, 0), (1, 1), (0, 0), (1, 1), (0, 0)))

    def device_rate(device):
        slab = device // N_GZ
        layer = device % N_GZ
        zero_index = jnp.zeros((), jnp.int32)
        block_cells = lax.dynamic_slice(padded, (zero_index, slab * CXD, zero_index, layer * CZD, zero_index), (9, CXD + 2, CY, CZD + 2, TILE))
        halo_grid = block_cells.reshape(9, (CXD + 2) * CY * (CZD + 2), TILE)
        pair_list = pair_cells[slab, layer]
        used_count = pair_count[slab, layer, 0]
        own_cell = pair_list[0]
        other_cell = pair_list[1]
        own_x = own_cell // (CY * CZD)
        own_y = own_cell // CZD % CY
        own_z = own_cell % CZD
        own_halo = (own_x + 1) * CY * (CZD + 2) + own_y * (CZD + 2) + own_z + 1
        own_tiles = jnp.take(halo_grid, own_halo, axis=1)
        other_tiles = jnp.take(halo_grid, other_cell, axis=1)
        pair_used = jnp.arange(PAIRS, dtype=jnp.int32) < used_count
        terms = pair_terms(own_tiles, other_tiles) * pair_used[:, None]
        rate_sum = jnp.zeros((CXD * CY * CZD, TILE), jnp.float32).at[own_cell].add(terms)
        return rate_sum.reshape(CXD, CY, CZD, TILE)
    rates = lax.map(device_rate, jnp.arange(N_GX * N_GZ, dtype=jnp.int32))
    rates = rates.reshape(N_GX, N_GZ, CXD, CY, CZD, TILE).transpose(0, 2, 3, 1, 4, 5)
    rates = rates.reshape(NXC, CY, NZC, TILE)
    density_rate = jnp.where(slot_live, rates, 0.0)
    return (vertical, density_rate)
```

```python
import functools

import jax
import jax.numpy as jnp
import ml_dtypes
import numpy as np
from jax import lax
from jax.experimental import pallas as pl
from jax.experimental.pallas import tpu as pltpu
from jax.sharding import PartitionSpec as P

TWO_PI = 6.283185307179586
KERNEL_COEF = -5.0 * 21.0 / (16.0 * 3.141592653589793)
NX = 1024
NY = 512
HALF = 512
ROWS = 72
F32 = jnp.float32
BF16 = jnp.bfloat16
NN = (((1,), (0,)), ((), ()))
NT = (((1,), (1,)), ((), ()))
VM = pl.BlockSpec(memory_space=pltpu.VMEM)
SM = pl.BlockSpec(memory_space=pltpu.SMEM)


def parts_of(table):
    high = table.astype(ml_dtypes.bfloat16)
    low = (table - high.astype(np.float64)).astype(ml_dtypes.bfloat16)
    return high, low


@functools.cache
def tables():
    c = np.arange(NY)
    wave = 32 * (c // 64) + c % 32
    is_sine = (c % 64) >= 32
    wave[32] = NY // 2
    is_sine[32] = False
    angle = TWO_PI / NY * ((wave[:, None] * np.arange(NY)[None, :]) % NY)
    norm = np.where((wave == 0) | (wave == NY // 2), 1.0 / NY, 2.0 / NY) ** 0.5
    basis_y = np.where(is_sine[:, None], np.sin(angle), np.cos(angle)) * norm[:, None]
    r = np.arange(HALF)
    m = r % 256
    even = 2 * m
    even[256] = NX // 2
    odd = 2 * m + 1
    wave = np.concatenate([even, odd])
    is_sine = np.concatenate([r > 256, r >= 256])
    angle = TWO_PI / NX * ((np.arange(NX)[:, None] * wave[None, :]) % NX)
    norm = np.where((wave == 0) | (wave == NX // 2), 1.0 / NX, 2.0 / NX) ** 0.5
    basis_x = np.where(is_sine[None, :], np.sin(angle), np.cos(angle)) * norm[None, :]
    n = np.arange(HALF)
    order_gz = 32 * (n % 16) + 4 * (n // 64) + n // 16 % 4
    order_gx = 32 * (n // 16 % 16) + 16 * (n // 256) + n % 16
    rows = (np.arange(NX + ROWS) - 16) % NX
    return dict(
        y=parts_of(basis_y),
        yt=parts_of(np.ascontiguousarray(basis_y.T)),
        gz=parts_of(basis_x[order_gz]),
        gx=parts_of(basis_x[order_gx]),
        own=np.concatenate(parts_of(basis_x[rows]), axis=1),
    )


def split(value):
    high = value.astype(BF16)
    return high, (value - high.astype(F32)).astype(BF16)


def dot(lhs, rhs, dims):
    return lax.dot_general(lhs, rhs, dims, preferred_element_type=F32)


def data_by_table(value, high, low, dims):
    count = value.shape[0]
    vh, vl = split(value)
    both = dot(jnp.concatenate([vh, vl], 0), high, dims)
    return both[:count] + both[count:] + dot(vh, low, dims)


def table_by_data(high, low, value):
    count = value.shape[1]
    vh, vl = split(value)
    both = dot(high, jnp.concatenate([vh, vl], 1), NN)
    return both[:, :count] + both[:, count:] + dot(low, vh, NN)


def wave_squares(ids_ref):
    share = ids_ref[1]
    c = lax.broadcasted_iota(jnp.int32, (64, NX), 0)
    r = lax.broadcasted_iota(jnp.int32, (64, NX), 1)
    ky = 32 * share + c % 32
    ky = jnp.where((share == 0) & (c == 32), NY // 2, ky)
    m = r % 256
    kx = jnp.where(r == 256, NX // 2, jnp.where(r < HALF, 2 * m, 2 * m + 1))
    kx = kx.astype(F32) * (TWO_PI / NX)
    ky = ky.astype(F32) * (TWO_PI / NY)
    return kx, ky, kx * kx + ky * ky


def to_waves(sums, gaps, high, low):
    even = data_by_table(sums, high[:, :HALF], low[:, :HALF], NN)
    odd = data_by_table(gaps, high[:, HALF:], low[:, HALF:], NN)
    return jnp.concatenate([even, odd], 1)


def low_lanes(shape):
    return lax.broadcasted_iota(jnp.int32, shape, 1) < 64


def folded_waves(got_ref, high, low):
    sums, gaps = [], []
    mask = low_lanes((64, 128))
    for j in range(4):
        first, second = got_ref[2 * j], got_ref[2 * j + 1]
        first_turned = pltpu.roll(first, 64, 1)
        second_turned = pltpu.roll(second, 64, 1)
        sums.append(jnp.where(mask, first + first_turned, second + second_turned))
        gaps.append(jnp.where(mask, first - first_turned, second_turned - second))
    return to_waves(jnp.concatenate(sums, 1), jnp.concatenate(gaps, 1), high, low)


def send_rows(waves, high, low, out_ref):
    even = data_by_table(waves[:, :HALF], high[:, :HALF], low[:, :HALF], NT)
    odd = data_by_table(waves[:, HALF:], high[:, HALF:], low[:, HALF:], NT)
    top, bottom = even + odd, even - odd
    mask = low_lanes((waves.shape[0], 128))
    for j in range(4):
        upper = top[:, 128 * j : 128 * j + 128]
        lower = bottom[:, 128 * j : 128 * j + 128]
        out_ref[2 * j] = jnp.where(mask, upper, pltpu.roll(lower, 64, 1))
        out_ref[2 * j + 1] = jnp.where(mask, pltpu.roll(upper, 64, 1), lower)


def start_kernel(ids_ref, phis_ref, eta_ref, yh_ref, yl_ref, out_ref):
    first = pl.multiple_of(64 * ids_ref[1], 64)
    high = yh_ref[pl.ds(first, 64), :]
    low = yl_ref[pl.ds(first, 64), :]
    coefs = data_by_table(phis_ref[...], high, low, NT)
    eta = eta_ref[...]
    pieces = [jnp.concatenate([coefs[:16], coefs[16:]], 1)]
    pieces += [eta[:, 128 * j : 128 * j + 128] for j in range(4)]
    block = jnp.concatenate(pieces, 0)
    out_ref[...] = jnp.broadcast_to(block[None], out_ref.shape)


def first_kernel(ids_ref, got_ref, gxh_ref, gxl_ref, gzh_ref, gzl_ref, out_ref, waves_ref):
    got = jnp.concatenate([got_ref[pl.ds(32 * a, 16), :] for a in range(32)], 0)
    turned = jnp.concatenate([got[128 * j : 128 * j + 128].T for j in range(4)], 1)
    sums = turned[:, :256] + turned[:, 256:]
    gaps = turned[:, :256] - turned[:, 256:]
    sums = jnp.concatenate([sums[:64], sums[64:]], 1)
    gaps = jnp.concatenate([gaps[:64], gaps[64:]], 1)
    waves = to_waves(sums, gaps, gxh_ref[...], gxl_ref[...])
    waves_ref[...] = waves
    kx, ky, squares = wave_squares(ids_ref)
    both = jnp.concatenate([jnp.sqrt(squares) * waves, squares * waves], 0)
    send_rows(both, gzh_ref[...], gzl_ref[...], out_ref)


def second_kernel(got_ref, eta_ref, yh_ref, yl_ref, th_ref, tl_ref, out_ref, turned_ref, curve_ref):
    turned = []
    for j in range(4):
        block = [
            eta_ref[pl.ds(512 * half + 16 + 4 * j + q, 16, stride=32), :]
            for half in range(2)
            for q in range(4)
        ]
        turned.append(jnp.concatenate(block, 0).T)
    eta = jnp.concatenate(turned, 0)
    turned_ref[...] = eta
    first = jnp.concatenate([got_ref[s, :64, :] for s in range(8)], 0)
    second = jnp.concatenate([got_ref[s, 64:, :] for s in range(8)], 0)
    fields = table_by_data(th_ref[...], tl_ref[...], jnp.concatenate([first, second], 1))
    curve_ref[...] = 0.5 * eta * fields[:, 128:]
    waves = table_by_data(yh_ref[...], yl_ref[...], -eta * fields[:, :128])
    for s in range(8):
        out_ref[s] = waves[64 * s : 64 * s + 64]


def third_kernel(ids_ref, got_ref, gzh_ref, gzl_ref, out_ref, waves_ref):
    waves = folded_waves(got_ref, gzh_ref[...], gzl_ref[...])
    waves_ref[...] = waves
    kx, ky, squares = wave_squares(ids_ref)
    send_rows(jnp.sqrt(squares) * waves, gzh_ref[...], gzl_ref[...], out_ref)


def fourth_kernel(got_ref, eta_ref, curve_ref, yh_ref, yl_ref, th_ref, tl_ref, out_ref):
    coefs = jnp.concatenate([got_ref[s] for s in range(8)], 0)
    field = table_by_data(th_ref[...], tl_ref[...], coefs)
    waves = table_by_data(yh_ref[...], yl_ref[...], -eta_ref[...] * (field + curve_ref[...]))
    for s in range(8):
        out_ref[s] = waves[64 * s : 64 * s + 64]


def fifth_kernel(ids_ref, got_ref, gzh_ref, gzl_ref, own_ref, first_ref, second_ref, out_ref):
    third = folded_waves(got_ref, gzh_ref[...], gzl_ref[...])
    first = first_ref[...]
    both = first + second_ref[...]
    kx, ky, squares = wave_squares(ids_ref)
    size = jnp.sqrt(squares)
    blocks = []
    for part in (0, HALF):
        speed = kx[:, part : part + 256]
        blocks.append(speed * first[:, part + 256 : part + HALF])
        blocks.append(-speed * first[:, part : part + 256])
    slope_x = jnp.concatenate(blocks, 1)
    speed = ky[:32]
    slope_y = jnp.concatenate([speed * first[32:], -speed * first[:32]], 0)
    fields = jnp.concatenate(
        [size * (both + third), squares * both, size * squares * first, slope_x, slope_y], 0
    )
    fh, fl = split(fields)
    oh, ol = own_ref[:, :NX], own_ref[:, NX:]
    rows = dot(oh, fh, NT) + dot(oh, fl, NT) + dot(ol, fh, NT)
    for s in range(8):
        out_ref[s] = rows


def last_kernel(
    ids_ref, pairs_ref, count_ref, got_ref, eta_ref, parts_ref, yh_ref, yl_ref,
    surface_ref, rate_ref, field_ref, target_ref, chan_ref, own_ref, sum_ref,
):
    slab = ids_ref[0]
    mask = low_lanes((ROWS, 128))
    fields = []
    for f in range(5):
        pieces = []
        lane = 128 * (f // 2)
        for j in range(4):
            first = got_ref[2 * j, :, lane : lane + 128] if f < 4 else got_ref[2 * j, :, 256:320]
            second = got_ref[2 * j + 1, :, lane : lane + 128] if f < 4 else got_ref[2 * j + 1, :, 256:320]
            if f == 4:
                pieces.append(jnp.concatenate([first, second], 1))
            elif f % 2 == 0:
                pieces.append(jnp.where(mask, first, pltpu.roll(second, 64, 1)))
            else:
                pieces.append(jnp.where(mask, pltpu.roll(first, 64, 1), second))
        fields.append(jnp.concatenate(pieces, 1))
    fields = data_by_table(jnp.concatenate(fields, 0), yh_ref[...], yl_ref[...], NN)
    eta = eta_ref[...]
    vertical = (
        fields[:ROWS]
        + eta * fields[ROWS : 2 * ROWS]
        + 0.5 * eta * eta * fields[2 * ROWS : 3 * ROWS]
    )
    surface_ref[...] = vertical[16:48]
    sampled = (fields[3 * ROWS : 4 * ROWS], fields[4 * ROWS :], vertical)
    for f in range(3):
        field_ref[2 * f] = sampled[f]
        field_ref[2 * f + 1] = pltpu.roll(sampled[f], NY - 1, 1) - sampled[f]
    row_ids = lax.broadcasted_iota(jnp.int32, (24, 128), 0).astype(F32)

    def sample(cx, carry):
        first_row = pl.multiple_of(16 * cx, 16)
        origin = (32 * slab - 16 + 16 * cx).astype(F32)
        found = [[], [], []]
        place_x = parts_ref[0, pl.ds(first_row, 16), :] * 8.0 - origin
        place_y = parts_ref[1, pl.ds(first_row, 16), :] * 64.0
        for cy in range(4):
            for cz in range(4):
                cell = 4 * cy + cz
                along = place_y[cell : cell + 1] - 128.0 * cy
                index = jnp.clip(along.astype(jnp.int32), 0, 127)
                part = along - index.astype(F32)
                index = jnp.broadcast_to(index, (24, 128))
                weight = jnp.maximum(0.0, 1.0 - jnp.abs(place_x[cell : cell + 1] - row_ids))
                weight_next = weight * part
                for f in range(3):
                    here = field_ref[2 * f, pl.ds(first_row, 24), 128 * cy : 128 * cy + 128]
                    step = field_ref[2 * f + 1, pl.ds(first_row, 24), 128 * cy : 128 * cy + 128]
                    here = jnp.take_along_axis(here, index, axis=1)
                    step = jnp.take_along_axis(step, index, axis=1)
                    found[f].append(
                        jnp.sum(weight * here + weight_next * step, axis=0, keepdims=True)
                    )
        for f in range(3):
            target_ref[f, pl.ds(first_row, 16), :] = jnp.concatenate(found[f], 0)
        return carry

    lax.fori_loop(0, 4, sample, 0)
    depth = jnp.exp((parts_ref[2] - 32.0) * (1.0 / 32.0))
    close = jnp.clip(1.0 - parts_ref[0] * (1.0 / 256.0), 0.0, 1.0)
    close = close * close
    for i in range(3):
        chan_ref[i] = parts_ref[i]
        speed = parts_ref[3 + i]
        chan_ref[3 + i] = speed + close * (target_ref[i] * depth - speed)
    chan_ref[6] = parts_ref[6]
    mass = parts_ref[7]
    chan_ref[7] = KERNEL_COEF * mass
    chan_ref[8] = (-2.0 * KERNEL_COEF) * (mass / parts_ref[6])

    def own_rows(values):
        pieces = []
        for cx in (1, 2):
            for cy in range(4):
                first = 16 * cx + 4 * cy + 1
                pieces.append(values[first : first + 2])
        return jnp.concatenate(pieces, 0)

    columns = jnp.concatenate([own_rows(chan_ref[i]) for i in range(8)], 0).T
    for i in range(7):
        for o in range(16):
            k = 16 * i + o
            own_ref[o, i] = jnp.broadcast_to(columns[:, k : k + 1], (128, 128))
    sum_ref[...] = jnp.zeros_like(sum_ref)

    def add_pair(t, carry):
        o = pairs_ref[0, t]
        cell = pairs_ref[1, t]
        other = [chan_ref[i, pl.ds(cell, 1), :] for i in range(9)]
        for piece in range(4):
            span = pl.ds(32 * piece, 32)
            gap_x = own_ref[o, 0, span, :] - other[0]
            gap_y = own_ref[o, 1, span, :] - other[1]
            gap_z = own_ref[o, 2, span, :] - other[2]
            radius = jnp.sqrt(gap_x * gap_x + gap_y * gap_y + gap_z * gap_z)
            reach = jnp.maximum(1.0 - 0.5 * radius, 0.0)
            approach = (own_ref[o, 3, span, :] - other[3]) * gap_x
            approach = approach + (own_ref[o, 4, span, :] - other[4]) * gap_y
            approach = approach + (own_ref[o, 5, span, :] - other[5]) * gap_z
            flow = other[7] * approach + (other[6] - own_ref[o, 6, span, :]) * other[8]
            sum_ref[o, span, :] += reach * reach * reach * flow
        return carry

    lax.fori_loop(0, count_ref[0], add_pair, 0)
    ones = jnp.ones((8, 384), BF16)
    rates = []
    for o in range(16):
        total = sum_ref[o]
        high, rest = split(total)
        middle, last = split(total - high.astype(F32))
        rates.append(dot(ones, jnp.concatenate([high, middle, last], 1), NT)[:1])
    rate_ref[...] = jnp.where(own_rows(mass) > 0.0, jnp.concatenate(rates, 0), 0.0)


def call(kernel, outs, in_specs, scratch=(), name=None):
    return pl.pallas_call(
        kernel,
        out_shape=[jax.ShapeDtypeStruct(s, F32) for s in outs],
        in_specs=in_specs,
        out_specs=[VM] * len(outs),
        scratch_shapes=list(scratch),
        compiler_params=pltpu.CompilerParams(vmem_limit_bytes=48 * 1024 * 1024),
        name=name,
    )


def passed(values, axis, by):
    size = lax.axis_size(axis)
    return lax.ppermute(values, axis, [(i, (i + by) % size) for i in range(size)])


def swap(block, axis):
    return lax.all_to_all(block, axis, split_axis=0, concat_axis=0, tiled=True)


def per_device(eta, phis, particles, cell_count, pair_cells, pair_count):
    slab = lax.axis_index("gx")
    layer = lax.axis_index("gz")
    ids = jnp.stack([slab, layer]).astype(jnp.int32)
    table = tables()
    yh, yl = (jnp.asarray(t) for t in table["y"])
    th, tl = (jnp.asarray(t) for t in table["yt"])
    gzh, gzl = (jnp.asarray(t) for t in table["gz"])
    gxh, gxl = (jnp.asarray(t) for t in table["gx"])
    own = lax.dynamic_slice(jnp.asarray(table["own"]), (32 * slab, 0), (ROWS, 2 * NX))

    live = jnp.arange(128, dtype=jnp.int32) < cell_count[..., None]
    mass = jnp.where(live, particles[7], 0.0)
    cells = jnp.concatenate([particles[:7], mass[None]], 0)
    eta_before = passed(eta[16:], "gx", 1)
    eta_after = passed(eta[:24], "gx", -1)
    cells_before = passed(cells[:, 1:], "gx", 1)
    cells_after = passed(cells[:, :1], "gx", -1)
    cells = jnp.concatenate([cells_before, cells, cells_after], 1)
    below = passed(cells[:, :, :, 1:], "gz", 1)
    above = passed(cells[:, :, :, :1], "gz", -1)
    cells = jnp.concatenate([below, cells, above], 3)
    at_x = 2 * slab - 1 + jnp.arange(4, dtype=jnp.int32)
    at_z = 2 * layer - 1 + jnp.arange(4, dtype=jnp.int32)
    inside_x = (at_x >= 0) & (at_x < 64)
    inside_z = (at_z >= 0) & (at_z < 16)
    inside = (inside_x[:, None] & inside_z[None, :])[:, None, :, None]
    inside = inside | (jnp.arange(8) < 7)[:, None, None, None, None]
    cells = jnp.where(inside, cells, 0.0).reshape(8, 64, 128)
    eta_rows = jnp.concatenate([eta_before, eta, eta_after], 0)

    eta_part = lax.dynamic_slice(eta, (4 * layer, 0), (4, NY))
    (block,) = call(start_kernel, [(32, 32, 128)], [SM, VM, VM, VM, VM], name="start")(
        ids, phis, eta_part, yh, yl
    )
    gathered = swap(block, "gx").reshape(1024, 128)
    block, first = call(
        first_kernel, [(8, 128, 128), (64, NX)], [SM] + [VM] * 5, name="first"
    )(ids, gathered, gxh, gxl, gzh, gzl)
    got = swap(block, "gz")
    block, eta_turned, curve = call(
        second_kernel, [(8, 64, 128), (NY, 128), (NY, 128)], [VM] * 6, name="second"
    )(got, gathered, yh, yl, th, tl)
    got = swap(block, "gz")
    block, second = call(
        third_kernel, [(8, 64, 128), (64, NX)], [SM] + [VM] * 3, name="third"
    )(ids, got, gzh, gzl)
    got = swap(block, "gz")
    (block,) = call(fourth_kernel, [(8, 64, 128)], [VM] * 7, name="fourth")(
        got, eta_turned, curve, yh, yl, th, tl
    )
    got = swap(block, "gz")
    (block,) = call(fifth_kernel, [(8, ROWS, 320)], [SM] + [VM] * 6, name="fifth")(
        ids, got, gzh, gzl, own, first, second
    )
    got = swap(block, "gz")
    surface, rate = call(
        last_kernel,
        [(32, NY), (16, 128)],
        [SM, SM, SM] + [VM] * 5,
        [
            pltpu.VMEM((6, ROWS, NY), F32),
            pltpu.VMEM((3, 64, 128), F32),
            pltpu.VMEM((9, 64, 128), F32),
            pltpu.VMEM((16, 7, 128, 128), F32),
            pltpu.VMEM((16, 128, 128), F32),
        ],
        name="last",
    )(ids, pair_cells.reshape(2, 96), pair_count.reshape(1), got, eta_rows, cells, yh, yl)
    return surface, rate.reshape(2, 4, 2, 128)


def solution(mesh):
    in_specs = (
        P("gx", None),
        P("gx", None),
        P(None, "gx", None, "gz", None),
        P("gx", None, "gz"),
        P("gx", "gz", None, None),
        P("gx", "gz", None),
    )
    out_specs = (P("gx", None), P("gx", None, "gz", None))
    return jax.shard_map(
        per_device, mesh=mesh, in_specs=in_specs, out_specs=out_specs, check_vma=False
    )
```

```python
import functools

import jax
import jax.numpy as jnp
import ml_dtypes
import numpy as np
from jax import lax
from jax.experimental import pallas as pl
from jax.experimental.pallas import tpu as pltpu
from jax.sharding import PartitionSpec as P

TWO_PI = 6.283185307179586
KERNEL_COEF = -5.0 * 21.0 / (16.0 * 3.141592653589793)
NX = 1024
NY = 512
HALF = 512
ROWS = 72
F32 = jnp.float32
BF16 = jnp.bfloat16
NN = (((1,), (0,)), ((), ()))
NT = (((1,), (1,)), ((), ()))
VM = pl.BlockSpec(memory_space=pltpu.VMEM)
SM = pl.BlockSpec(memory_space=pltpu.SMEM)
HB = pl.BlockSpec(memory_space=pltpu.HBM)
GROUP = 8


def parts_of(table):
    high = table.astype(ml_dtypes.bfloat16)
    low = (table - high.astype(np.float64)).astype(ml_dtypes.bfloat16)
    return high, low


@functools.cache
def tables():
    c = np.arange(NY)
    wave = 32 * (c // 64) + c % 32
    is_sine = (c % 64) >= 32
    wave[32] = NY // 2
    is_sine[32] = False
    angle = TWO_PI / NY * ((wave[:, None] * np.arange(NY)[None, :]) % NY)
    norm = np.where((wave == 0) | (wave == NY // 2), 1.0 / NY, 2.0 / NY) ** 0.5
    basis_y = np.where(is_sine[:, None], np.sin(angle), np.cos(angle)) * norm[:, None]
    r = np.arange(HALF)
    m = r % 256
    even = 2 * m
    even[256] = NX // 2
    odd = 2 * m + 1
    wave = np.concatenate([even, odd])
    is_sine = np.concatenate([r > 256, r >= 256])
    angle = TWO_PI / NX * ((np.arange(NX)[:, None] * wave[None, :]) % NX)
    norm = np.where((wave == 0) | (wave == NX // 2), 1.0 / NX, 2.0 / NX) ** 0.5
    basis_x = np.where(is_sine[None, :], np.sin(angle), np.cos(angle)) * norm[None, :]
    n = np.arange(HALF)
    order_gz = 32 * (n % 16) + 4 * (n // 64) + n // 16 % 4
    rows = (np.arange(NX + ROWS) - 16) % NX
    yh, yl = parts_of(basis_y)
    xh, xl = parts_of(basis_x[order_gz])
    return dict(
        y=np.stack([yh, yl]),
        x=np.stack([xh[:, :HALF], xh[:, HALF:], xl[:, :HALF], xl[:, HALF:]]),
        own=np.concatenate(parts_of(basis_x[rows]), axis=1),
    )


def split(value):
    high = value.astype(BF16)
    return high, (value - high.astype(F32)).astype(BF16)


def dot(lhs, rhs, dims):
    return lax.dot_general(lhs, rhs, dims, preferred_element_type=F32)


def data_by_table(value, high, low, dims):
    count = value.shape[0]
    vh, vl = split(value)
    both = dot(jnp.concatenate([vh, vl], 0), high, dims)
    return both[:count] + both[count:] + dot(vh, low, dims)


def table_by_data(high, low, value):
    count = value.shape[0]
    vh, vl = split(value)
    both = dot(high, jnp.concatenate([vh, vl], 0), NT)
    return both[:, :count] + both[:, count:] + dot(low, vh, NT)


def wave_squares(ids_ref):
    share = ids_ref[1]
    c = lax.broadcasted_iota(jnp.int32, (64, NX), 0)
    r = lax.broadcasted_iota(jnp.int32, (64, NX), 1)
    ky = 32 * share + c % 32
    ky = jnp.where((share == 0) & (c == 32), NY // 2, ky)
    m = r % 256
    kx = jnp.where(r == 256, NX // 2, jnp.where(r < HALF, 2 * m, 2 * m + 1))
    kx = kx.astype(F32) * (TWO_PI / NX)
    ky = ky.astype(F32) * (TWO_PI / NY)
    return kx, ky, kx * kx + ky * ky


def to_waves(sums, gaps, x_ref):
    even = data_by_table(sums, x_ref[0], x_ref[2], NN)
    odd = data_by_table(gaps, x_ref[1], x_ref[3], NN)
    return jnp.concatenate([even, odd], 1)


def low_lanes(shape):
    return lax.broadcasted_iota(jnp.int32, shape, 1) < 64


def folded_waves(got_ref, x_ref):
    sums, gaps = [], []
    mask = low_lanes((64, 128))
    for j in range(4):
        first, second = got_ref[2 * j], got_ref[2 * j + 1]
        first_turned = pltpu.roll(first, 64, 1)
        second_turned = pltpu.roll(second, 64, 1)
        sums.append(jnp.where(mask, first + first_turned, second + second_turned))
        gaps.append(jnp.where(mask, first - first_turned, second_turned - second))
    return to_waves(jnp.concatenate(sums, 1), jnp.concatenate(gaps, 1), x_ref)


def from_waves(waves, x_ref):
    even = table_by_data(x_ref[0], x_ref[2], waves[:, :HALF])
    odd = table_by_data(x_ref[1], x_ref[3], waves[:, HALF:])
    return even + odd, even - odd


def by_share(first, second):
    mask = low_lanes(first.shape)
    return (
        jnp.where(mask, first, pltpu.roll(second, 64, 1)),
        jnp.where(mask, pltpu.roll(first, 64, 1), second),
    )


def fetch(source, buffer, sems, place):
    copy = pltpu.make_async_copy(source, buffer, sems.at[place])
    copy.start()
    return copy


def wait_all(copies):
    for copy in copies:
        copy.wait()


def send_block(block_ref, out_ref, sems):
    wait_all([fetch(block_ref, out_ref.at[s], sems, s) for s in range(out_ref.shape[0])])


def start_kernel(
    ids_ref, phis_hbm, eta_hbm, y_hbm, out_ref, phis_ref, eta_ref, table_ref, block_ref, sems, out_sems
):
    first = pl.multiple_of(64 * ids_ref[1], 64)
    rows = pl.multiple_of(8 * (ids_ref[1] // 2), 8)
    copies = [
        fetch(y_hbm.at[:, pl.ds(first, 64), :], table_ref, sems, 0),
        fetch(phis_hbm, phis_ref, sems, 1),
        fetch(eta_hbm.at[pl.ds(rows, 8), :], eta_ref, sems, 2),
    ]
    wait_all(copies)
    coefs = data_by_table(phis_ref[...], table_ref[0], table_ref[1], NT)
    eta = eta_ref[...]
    eta = jnp.where(ids_ref[1] % 2 == 0, eta[:4], eta[4:])
    block_ref[:16] = jnp.concatenate([coefs[:16], coefs[16:]], 1)
    for j in range(4):
        block_ref[16 + 4 * j : 20 + 4 * j] = eta[:, 128 * j : 128 * j + 128]
    send_block(block_ref, out_ref, out_sems)


def first_kernel(ids_ref, got_ref, x_ref, *refs):
    out_hbm, waves_hbm, out_ref, waves_ref, sems = refs[4:]
    kx, ky, squares = wave_squares(ids_ref)
    size = jnp.sqrt(squares)
    got = [
        got_ref[pl.ds(512 * half + r, 16, stride=32), :] for half in range(2) for r in range(16)
    ]
    turned = [jnp.concatenate(got[8 * j : 8 * j + 8], 0).T for j in range(4)]
    first, second = jnp.concatenate(turned[:2], 1), jnp.concatenate(turned[2:], 1)
    sums, gaps = first + second, first - second
    sums = jnp.concatenate([sums[:64], sums[64:]], 1)
    gaps = jnp.concatenate([gaps[:64], gaps[64:]], 1)
    waves = to_waves(sums, gaps, x_ref)
    waves_ref[...] = waves
    copies = [fetch(waves_ref, waves_hbm, sems, 8)]
    both = jnp.concatenate([size * waves, squares * waves], 0)
    top, bottom = from_waves(both, x_ref)
    for s in range(8):
        out_ref[s, :64] = top[64 * s : 64 * s + 64]
        out_ref[s, 64:] = bottom[64 * s : 64 * s + 64]
        copies.append(fetch(out_ref.at[s], out_hbm.at[s], sems, s))
    wait_all(copies)


def second_kernel(got_ref, gathered_ref, y_ref, *refs):
    out_hbm, eta_hbm, curve_hbm, token_ref, out_ref, eta_ref, curve_ref, sems = refs[2:]
    pairs = [by_share(got_ref[2 * j], got_ref[2 * j + 1]) for j in range(4)]
    first = jnp.concatenate([p[0] for p in pairs], 1)
    second = jnp.concatenate([p[1] for p in pairs], 1)
    fields = data_by_table(jnp.concatenate([first, second], 0), y_ref[0], y_ref[1], NN)
    columns = []
    for j in range(4):
        block = [
            gathered_ref[pl.ds(512 * half + 16 + 4 * j + q, 16, stride=32), :]
            for half in range(2)
            for q in range(4)
        ]
        columns.append(jnp.concatenate(block, 0))
    eta = jnp.concatenate(columns, 1)
    eta_ref[...] = eta
    curve_ref[...] = 0.5 * eta * fields[128:]
    copies = [fetch(eta_ref, eta_hbm, sems, 8), fetch(curve_ref, curve_hbm, sems, 9)]
    waves = table_by_data(y_ref[0], y_ref[1], -eta * fields[:128])
    token_ref[...] = waves[:8, :128]
    for s in range(8):
        out_ref[s] = waves[64 * s : 64 * s + 64]
        copies.append(fetch(out_ref.at[s], out_hbm.at[s], sems, s))
    wait_all(copies)


def third_kernel(ids_ref, got_ref, x_ref, token_ref, out_hbm, waves_hbm, out_ref, waves_ref, sems):
    kx, ky, squares = wave_squares(ids_ref)
    size = jnp.sqrt(squares)
    waves = folded_waves(got_ref, x_ref)
    waves_ref[...] = waves
    copies = [fetch(waves_ref, waves_hbm, sems, 8)]
    top, bottom = from_waves(size * waves, x_ref)
    both = jnp.concatenate([top, bottom], 1)
    for s in range(8):
        out_ref[s] = both[64 * s : 64 * s + 64]
        copies.append(fetch(out_ref.at[s], out_hbm.at[s], sems, s))
    wait_all(copies)


def fourth_kernel(
    got_ref, eta_hbm, curve_hbm, y_ref, out_hbm, out_ref, eta_ref, curve_ref, sems
):
    copies = [fetch(eta_hbm, eta_ref, sems, 8), fetch(curve_hbm, curve_ref, sems, 9)]
    pairs = [by_share(got_ref[2 * j], got_ref[2 * j + 1]) for j in range(4)]
    coefs = jnp.concatenate(
        [jnp.concatenate([p[half] for p in pairs], 1) for half in range(2)], 0
    )
    field = data_by_table(coefs, y_ref[0], y_ref[1], NN)
    wait_all(copies)
    waves = table_by_data(y_ref[0], y_ref[1], -eta_ref[...] * (field + curve_ref[...]))
    copies = []
    for s in range(8):
        out_ref[s] = waves[64 * s : 64 * s + 64]
        copies.append(fetch(out_ref.at[s], out_hbm.at[s], sems, s))
    wait_all(copies)


def fifth_kernel(
    ids_ref, got_ref, x_ref, own_hbm, first_hbm, second_hbm, out_hbm,
    own_ref, out_ref, first_ref, second_ref, sems, out_sems,
):
    start = pl.multiple_of(32 * ids_ref[0], 32)
    copies = [
        fetch(first_hbm, first_ref, sems, 1),
        fetch(second_hbm, second_ref, sems, 2),
        fetch(own_hbm.at[pl.ds(start, 80), :], own_ref, sems, 0),
    ]
    kx, ky, squares = wave_squares(ids_ref)
    size = jnp.sqrt(squares)
    third = folded_waves(got_ref, x_ref)
    wait_all(copies)
    first = first_ref[...]
    both = first + second_ref[...]
    blocks = []
    for part in (0, HALF):
        speed = kx[:, part : part + 256]
        blocks.append(speed * first[:, part + 256 : part + HALF])
        blocks.append(-speed * first[:, part : part + 256])
    slope_x = jnp.concatenate(blocks, 1)
    speed = ky[:32]
    slope_y = jnp.concatenate([speed * first[32:], -speed * first[:32]], 0)
    fields = jnp.concatenate(
        [size * (both + third), squares * both, size * squares * first, slope_x, slope_y], 0
    )
    fh, fl = split(fields)
    oh, ol = own_ref[:, :NX], own_ref[:, NX:]
    rows = dot(oh, fh, NT) + dot(oh, fl, NT) + dot(ol, fh, NT)
    out_ref[...] = rows[:ROWS]
    send_block(out_ref, out_hbm, out_sems)


def own_rows(values):
    pieces = []
    for cx in (1, 2):
        for cy in range(4):
            first = 16 * cx + 4 * cy + 1
            pieces.append(values[first : first + 2])
    return jnp.concatenate(pieces, 0)


def live_mass(ids_ref, parts_ref):
    cell = lax.broadcasted_iota(jnp.int32, (64, 128), 0)
    at_x = 2 * ids_ref[0] - 1 + cell // 16
    at_z = 2 * ids_ref[1] - 1 + cell % 4
    inside = (at_x >= 0) & (at_x < 64) & (at_z >= 0) & (at_z < 16)
    return jnp.where(inside, parts_ref[7], 0.0)


def spread_own(values, out_ref):
    columns = jnp.concatenate([own_rows(v) for v in values], 0)
    missing = 128 - columns.shape[0]
    if missing:
        columns = jnp.concatenate([columns, jnp.zeros((missing, 128), F32)], 0)
    columns = columns.T
    for i in range(len(values)):
        for o in range(16):
            k = 16 * i + o
            out_ref[o, i] = jnp.broadcast_to(columns[:, k : k + 1], (128, 128))


def reach_groups(count_ref):
    return (count_ref[0] + GROUP - 1) // GROUP


def reach_copy(source, target, sems, group):
    span = pl.ds(pl.multiple_of(group * GROUP, GROUP), GROUP)
    return pltpu.make_async_copy(source.at[span], target.at[span], sems.at[group])


def reach_kernel(
    ids_ref, pairs_ref, count_ref, parts_ref, token_ref,
    reach_hbm, place_hbm, sum_hbm, done_ref,
    reach_ref, place_ref, density_ref, sum_ref, chan_ref, sems, reach_sems,
):
    mass = live_mass(ids_ref, parts_ref)
    chan_ref[0] = parts_ref[6]
    chan_ref[1] = KERNEL_COEF * mass
    chan_ref[2] = (-2.0 * KERNEL_COEF) * (mass / parts_ref[6])
    spread_own([parts_ref[i] for i in range(3)], place_ref)
    copies = [fetch(place_ref, place_hbm, sems, 0)]
    spread_own([parts_ref[6]], density_ref)
    sum_ref[...] = jnp.zeros_like(sum_ref)
    done_ref[...] = token_ref[...]
    def add_pair(t, carry):
        o = pairs_ref[0, t]
        cell = pairs_ref[1, t]
        place = [parts_ref[i, pl.ds(cell, 1), :] for i in range(3)]
        density, weight, volume = [chan_ref[i, pl.ds(cell, 1), :] for i in range(3)]
        for piece in range(4):
            span = pl.ds(32 * piece, 32)
            gap_x = place_ref[o, 0, span, :] - place[0]
            gap_y = place_ref[o, 1, span, :] - place[1]
            gap_z = place_ref[o, 2, span, :] - place[2]
            radius = jnp.sqrt(gap_x * gap_x + gap_y * gap_y + gap_z * gap_z)
            reach = jnp.maximum(1.0 - 0.5 * radius, 0.0)
            reach = reach * reach * reach
            reach_ref[t, span, :] = reach * weight
            sum_ref[o, span, :] += reach * ((density - density_ref[o, 0, span, :]) * volume)
        return carry

    def add_group(g, carry):
        last = jnp.minimum(GROUP * g + GROUP, count_ref[0])
        lax.fori_loop(GROUP * g, last, add_pair, 0)
        reach_copy(reach_ref, reach_hbm, reach_sems, g).start()
        return carry

    def wait_group(g, carry):
        reach_copy(reach_ref, reach_hbm, reach_sems, g).wait()
        return carry

    groups = reach_groups(count_ref)
    lax.fori_loop(0, groups, add_group, 0)
    copies.append(fetch(sum_ref, sum_hbm, sems, 1))
    lax.fori_loop(0, groups, wait_group, 0)
    wait_all(copies)


def last_kernel(
    ids_ref, pairs_ref, count_ref, got_ref, before_hbm, eta_hbm, after_hbm, parts_hbm, y_ref,
    reach_hbm, place_hbm, sum_hbm, surface_ref, rate_ref,
    eta_ref, parts_ref, reach_ref, place_ref, sum_ref,
    field_ref, target_ref, speed_ref, own_ref, sems, reach_sems,
):
    copies = [
        fetch(before_hbm, eta_ref.at[:16], sems, 0),
        fetch(eta_hbm, eta_ref.at[16:48], sems, 1),
        fetch(after_hbm, eta_ref.at[48:], sems, 2),
        fetch(parts_hbm, parts_ref, sems, 3),
        fetch(place_hbm, place_ref, sems, 4),
        fetch(sum_hbm, sum_ref, sems, 5),
    ]

    def start_group(g, carry):
        reach_copy(reach_hbm, reach_ref, reach_sems, g).start()
        return carry

    def wait_group(g, carry):
        reach_copy(reach_hbm, reach_ref, reach_sems, g).wait()
        return carry

    groups = reach_groups(count_ref)
    lax.fori_loop(0, groups, start_group, 0)
    slab = ids_ref[0]
    mask = low_lanes((ROWS, 128))
    fields = []
    for f in range(5):
        pieces = []
        lane = 128 * (f // 2)
        for j in range(4):
            first = got_ref[2 * j, :, lane : lane + 128] if f < 4 else got_ref[2 * j, :, 256:320]
            second = got_ref[2 * j + 1, :, lane : lane + 128] if f < 4 else got_ref[2 * j + 1, :, 256:320]
            if f == 4:
                pieces.append(jnp.concatenate([first, second], 1))
            elif f % 2 == 0:
                pieces.append(jnp.where(mask, first, pltpu.roll(second, 64, 1)))
            else:
                pieces.append(jnp.where(mask, pltpu.roll(first, 64, 1), second))
        fields.append(jnp.concatenate(pieces, 1))
    fields = data_by_table(
        jnp.concatenate(fields, 0), y_ref[0], y_ref[1], NN
    )
    wait_all(copies[:4])
    eta = eta_ref[...]
    vertical = (
        fields[:ROWS]
        + eta * fields[ROWS : 2 * ROWS]
        + 0.5 * eta * eta * fields[2 * ROWS : 3 * ROWS]
    )
    surface_ref[...] = vertical[16:48]
    sampled = (fields[3 * ROWS : 4 * ROWS], fields[4 * ROWS :], vertical)
    for f in range(3):
        field_ref[2 * f] = sampled[f]
        field_ref[2 * f + 1] = pltpu.roll(sampled[f], NY - 1, 1) - sampled[f]
    row_ids = lax.broadcasted_iota(jnp.int32, (24, 128), 0).astype(F32)

    def sample(cx, carry):
        first_row = pl.multiple_of(16 * cx, 16)
        origin = (32 * slab - 16 + 16 * cx).astype(F32)
        found = [[], [], []]
        place_x = parts_ref[0, pl.ds(first_row, 16), :] * 8.0 - origin
        place_y = parts_ref[1, pl.ds(first_row, 16), :] * 64.0
        for cy in range(4):
            for cz in range(4):
                cell = 4 * cy + cz
                along = place_y[cell : cell + 1] - 128.0 * cy
                index = jnp.clip(along.astype(jnp.int32), 0, 127)
                part = along - index.astype(F32)
                index = jnp.broadcast_to(index, (24, 128))
                weight = jnp.maximum(0.0, 1.0 - jnp.abs(place_x[cell : cell + 1] - row_ids))
                weight_next = weight * part
                for f in range(3):
                    here = field_ref[2 * f, pl.ds(first_row, 24), 128 * cy : 128 * cy + 128]
                    step = field_ref[2 * f + 1, pl.ds(first_row, 24), 128 * cy : 128 * cy + 128]
                    here = jnp.take_along_axis(here, index, axis=1)
                    step = jnp.take_along_axis(step, index, axis=1)
                    found[f].append(
                        jnp.sum(weight * here + weight_next * step, axis=0, keepdims=True)
                    )
        for f in range(3):
            target_ref[f, pl.ds(first_row, 16), :] = jnp.concatenate(found[f], 0)
        return carry

    lax.fori_loop(0, 4, sample, 0)
    depth = jnp.exp((parts_ref[2] - 32.0) * (1.0 / 32.0))
    close = jnp.clip(1.0 - parts_ref[0] * (1.0 / 256.0), 0.0, 1.0)
    close = close * close
    for i in range(3):
        speed = parts_ref[3 + i]
        speed_ref[i] = speed + close * (target_ref[i] * depth - speed)
    spread_own([speed_ref[i] for i in range(3)], own_ref)
    wait_all(copies[4:])
    lax.fori_loop(0, groups, wait_group, 0)

    def add_pair(t, carry):
        o = pairs_ref[0, t]
        cell = pairs_ref[1, t]
        place = [parts_ref[i, pl.ds(cell, 1), :] for i in range(3)]
        speed = [speed_ref[i, pl.ds(cell, 1), :] for i in range(3)]
        for piece in range(4):
            span = pl.ds(32 * piece, 32)
            approach = 0.0
            for i in range(3):
                approach = approach + (own_ref[o, i, span, :] - speed[i]) * (
                    place_ref[o, i, span, :] - place[i]
                )
            sum_ref[o, span, :] += reach_ref[t, span, :] * approach
        return carry

    lax.fori_loop(0, count_ref[0], add_pair, 0)
    ones = jnp.ones((8, 384), BF16)
    rates = []
    for o in range(16):
        total = sum_ref[o]
        high, rest = split(total)
        middle, last = split(total - high.astype(F32))
        rates.append(dot(ones, jnp.concatenate([high, middle, last], 1), NT)[:1])
    mass = own_rows(parts_ref[7])
    rate_ref[...] = jnp.where(mass > 0.0, jnp.concatenate(rates, 0), 0.0)


def call(kernel, args, kinds, outs, name, vmem, scratch):
    specs = dict(S=SM, H=HB, V=VM)
    args = [
        pltpu.with_memory_space_constraint(a, pltpu.HBM) if k == "H" else a
        for a, k in zip(args, kinds, strict=True)
    ]
    return pl.pallas_call(
        kernel,
        out_shape=[
            pltpu.HBM(s, F32) if k == "H" else jax.ShapeDtypeStruct(s, F32) for s, k in outs
        ],
        in_specs=[specs[k] for k in kinds],
        out_specs=[specs[k] for _, k in outs],
        scratch_shapes=[pltpu.VMEM(s, F32) if isinstance(s, tuple) else s for s in scratch],
        compiler_params=pltpu.CompilerParams(vmem_limit_bytes=vmem * 1024 * 1024),
        name=name,
    )(*args)


def dma_sems(count):
    return pltpu.SemaphoreType.DMA((count,))


def passed(values, axis, by):
    size = lax.axis_size(axis)
    return lax.ppermute(values, axis, [(i, (i + by) % size) for i in range(size)])


def swap(block, axis):
    return lax.all_to_all(block, axis, split_axis=0, concat_axis=0, tiled=True)


def per_device(eta, phis, particles, cell_count, pair_cells, pair_count):
    slab = lax.axis_index("gx")
    layer = lax.axis_index("gz")
    ids = jnp.stack([slab, layer]).astype(jnp.int32)
    table = tables()
    y = jnp.asarray(table["y"])
    x = jnp.asarray(table["x"])
    own = jnp.asarray(table["own"])

    live = jnp.arange(128, dtype=jnp.int32) < cell_count[..., None]
    mass = jnp.where(live, particles[7], 0.0)
    cells = jnp.concatenate([particles[:7], mass[None]], 0)
    eta_before = passed(eta[16:], "gx", 1)
    eta_after = passed(eta[:24], "gx", -1)
    cells_before = passed(cells[:, 1:], "gx", 1)
    cells_after = passed(cells[:, :1], "gx", -1)
    cells = jnp.concatenate([cells_before, cells, cells_after], 1)
    below = passed(cells[:, :, :, 1:], "gz", 1)
    above = passed(cells[:, :, :, :1], "gz", -1)
    cells = jnp.concatenate([below, cells, above], 3)
    cells = cells.reshape(8, 64, 128)
    pairs = pair_cells.reshape(2, 96)
    count = pair_count.reshape(1)

    (block,) = call(
        start_kernel, (ids, phis, eta, y), "SHHH", [((32, 32, 128), "H")], "start", 4,
        [
            (32, NY),
            (8, NY),
            pltpu.VMEM((2, 64, NY), BF16),
            (32, 128),
            dma_sems(3),
            dma_sems(32),
        ],
    )
    gathered = swap(block, "gx").reshape(1024, 128)
    block, first = call(
        first_kernel,
        (ids, gathered, x, cells_before, cells_after, eta_before, eta_after),
        "SVVHHHH",
        [((8, 128, 128), "H"), ((64, NX), "H")],
        "first",
        8,
        [(8, 128, 128), (64, NX), dma_sems(9)],
    )
    got = swap(block, "gz")
    block, eta_part, curve, token = call(
        second_kernel,
        (got, gathered, y, below, above),
        "VVVHH",
        [((8, 64, 128), "H"), ((128, NY), "H"), ((128, NY), "H"), ((8, 128), "V")],
        "second",
        8,
        [(8, 64, 128), (128, NY), (128, NY), dma_sems(10)],
    )
    got = swap(block, "gz")
    reach, place, before, token = call(
        reach_kernel,
        (ids, pairs, count, cells, token),
        "SSSVV",
        [
            ((96, 128, 128), "H"),
            ((16, 3, 128, 128), "H"),
            ((16, 128, 128), "H"),
            ((8, 128), "V"),
        ],
        "reach",
        16,
        [
            (96, 128, 128),
            (16, 3, 128, 128),
            (16, 1, 128, 128),
            (16, 128, 128),
            (3, 64, 128),
            dma_sems(2),
            dma_sems(96 // GROUP),
        ],
    )
    block, second = call(
        third_kernel,
        (ids, got, x, token),
        "SVVV",
        [((8, 64, 128), "H"), ((64, NX), "H")],
        "third",
        8,
        [(8, 64, 128), (64, NX), dma_sems(9)],
    )
    got = swap(block, "gz")
    (block,) = call(
        fourth_kernel,
        (got, eta_part, curve, y),
        "VHHV",
        [((8, 64, 128), "H")],
        "fourth",
        8,
        [(8, 64, 128), (128, NY), (128, NY), dma_sems(10)],
    )
    got = swap(block, "gz")
    (block,) = call(
        fifth_kernel,
        (ids, got, x, own, first, second),
        "SVVHHH",
        [((8, ROWS, 320), "H")],
        "fifth",
        8,
        [
            pltpu.VMEM((80, 2 * NX), BF16),
            (ROWS, 320),
            (64, NX),
            (64, NX),
            dma_sems(3),
            dma_sems(8),
        ],
    )
    got = swap(block, "gz")
    surface, rate = call(
        last_kernel,
        (
            ids, pairs, count, got, eta_before, eta, eta_after, cells, y, reach, place, before
        ),
        "SSSVHHHHVHHH",
        [((32, NY), "V"), ((16, 128), "V")],
        "last",
        24,
        [
            (ROWS, NY),
            (8, 64, 128),
            (96, 128, 128),
            (16, 3, 128, 128),
            (16, 128, 128),
            (6, ROWS, NY),
            (3, 64, 128),
            (3, 64, 128),
            (16, 3, 128, 128),
            dma_sems(6),
            dma_sems(96 // GROUP),
        ],
    )
    return surface, rate.reshape(2, 4, 2, 128)


def solution(mesh):
    in_specs = (
        P("gx", None),
        P("gx", None),
        P(None, "gx", None, "gz", None),
        P("gx", None, "gz"),
        P("gx", "gz", None, None),
        P("gx", "gz", None),
    )
    out_specs = (P("gx", None), P("gx", None, "gz", None))
    return jax.shard_map(
        per_device, mesh=mesh, in_specs=in_specs, out_specs=out_specs, check_vma=False
    )
```

```python
import functools

import jax
import jax.numpy as jnp
import ml_dtypes
import numpy as np
from jax import lax
from jax.experimental import pallas as pl
from jax.experimental.pallas import tpu as pltpu
from jax.sharding import PartitionSpec as P

TWO_PI = 6.283185307179586
KERNEL_COEF = -5.0 * 21.0 / (16.0 * 3.141592653589793)
NX = 1024
NY = 512
HALF = 512
ROWS = 72
F32 = jnp.float32
BF16 = jnp.bfloat16
NN = (((1,), (0,)), ((), ()))
NT = (((1,), (1,)), ((), ()))
VM = pl.BlockSpec(memory_space=pltpu.VMEM)
SM = pl.BlockSpec(memory_space=pltpu.SMEM)
HB = pl.BlockSpec(memory_space=pltpu.HBM)
GROUP = 8
PART = 48


def parts_of(table):
    high = table.astype(ml_dtypes.bfloat16)
    low = (table - high.astype(np.float64)).astype(ml_dtypes.bfloat16)
    return high, low


@functools.cache
def tables():
    c = np.arange(NY)
    wave = 32 * (c // 64) + c % 32
    is_sine = (c % 64) >= 32
    wave[32] = NY // 2
    is_sine[32] = False
    angle = TWO_PI / NY * ((wave[:, None] * np.arange(NY)[None, :]) % NY)
    norm = np.where((wave == 0) | (wave == NY // 2), 1.0 / NY, 2.0 / NY) ** 0.5
    basis_y = np.where(is_sine[:, None], np.sin(angle), np.cos(angle)) * norm[:, None]
    r = np.arange(HALF)
    m = r % 256
    even = 2 * m
    even[256] = NX // 2
    odd = 2 * m + 1
    wave = np.concatenate([even, odd])
    is_sine = np.concatenate([r > 256, r >= 256])
    angle = TWO_PI / NX * ((np.arange(NX)[:, None] * wave[None, :]) % NX)
    norm = np.where((wave == 0) | (wave == NX // 2), 1.0 / NX, 2.0 / NX) ** 0.5
    basis_x = np.where(is_sine[None, :], np.sin(angle), np.cos(angle)) * norm[None, :]
    n = np.arange(HALF)
    order_gz = 32 * (n % 16) + 4 * (n // 64) + n // 16 % 4
    rows = (np.arange(NX + ROWS) - 16) % NX
    yh, yl = parts_of(basis_y)
    xh, xl = parts_of(basis_x[order_gz])
    return dict(
        y=np.stack([yh, yl]),
        x=np.stack([xh[:, :HALF], xh[:, HALF:], xl[:, :HALF], xl[:, HALF:]]),
        own=np.concatenate(parts_of(basis_x[rows]), axis=1),
    )


def split(value):
    high = value.astype(BF16)
    return high, (value - high.astype(F32)).astype(BF16)


def dot(lhs, rhs, dims):
    return lax.dot_general(lhs, rhs, dims, preferred_element_type=F32)


def data_by_table(value, high, low, dims):
    count = value.shape[0]
    vh, vl = split(value)
    both = dot(jnp.concatenate([vh, vl], 0), high, dims)
    return both[:count] + both[count:] + dot(vh, low, dims)


def table_by_data(high, low, value):
    count = value.shape[0]
    vh, vl = split(value)
    both = dot(high, jnp.concatenate([vh, vl], 0), NT)
    return both[:, :count] + both[:, count:] + dot(low, vh, NT)


def wave_squares(ids_ref):
    share = ids_ref[1]
    c = lax.broadcasted_iota(jnp.int32, (64, NX), 0)
    r = lax.broadcasted_iota(jnp.int32, (64, NX), 1)
    ky = 32 * share + c % 32
    ky = jnp.where((share == 0) & (c == 32), NY // 2, ky)
    m = r % 256
    kx = jnp.where(r == 256, NX // 2, jnp.where(r < HALF, 2 * m, 2 * m + 1))
    kx = kx.astype(F32) * (TWO_PI / NX)
    ky = ky.astype(F32) * (TWO_PI / NY)
    return kx, ky, kx * kx + ky * ky


def to_waves(sums, gaps, x_ref):
    even = data_by_table(sums, x_ref[0], x_ref[2], NN)
    odd = data_by_table(gaps, x_ref[1], x_ref[3], NN)
    return jnp.concatenate([even, odd], 1)


def low_lanes(shape):
    return lax.broadcasted_iota(jnp.int32, shape, 1) < 64


def folded_waves(got_ref, x_ref):
    sums, gaps = [], []
    mask = low_lanes((64, 128))
    for j in range(4):
        first, second = got_ref[2 * j], got_ref[2 * j + 1]
        first_turned = pltpu.roll(first, 64, 1)
        second_turned = pltpu.roll(second, 64, 1)
        sums.append(jnp.where(mask, first + first_turned, second + second_turned))
        gaps.append(jnp.where(mask, first - first_turned, second_turned - second))
    return to_waves(jnp.concatenate(sums, 1), jnp.concatenate(gaps, 1), x_ref)


def from_waves(waves, x_ref):
    even = table_by_data(x_ref[0], x_ref[2], waves[:, :HALF])
    odd = table_by_data(x_ref[1], x_ref[3], waves[:, HALF:])
    return even + odd, even - odd


def by_share(first, second):
    mask = low_lanes(first.shape)
    return (
        jnp.where(mask, first, pltpu.roll(second, 64, 1)),
        jnp.where(mask, pltpu.roll(first, 64, 1), second),
    )


def fetch(source, buffer, sems, place):
    copy = pltpu.make_async_copy(source, buffer, sems.at[place])
    copy.start()
    return copy


def wait_all(copies):
    for copy in copies:
        copy.wait()


def send_block(block_ref, out_ref, sems):
    wait_all([fetch(block_ref, out_ref.at[s], sems, s) for s in range(out_ref.shape[0])])


def start_kernel(
    ids_ref, phis_hbm, eta_hbm, y_hbm, out_ref, phis_ref, eta_ref, table_ref, block_ref, sems, out_sems
):
    first = pl.multiple_of(64 * ids_ref[1], 64)
    rows = pl.multiple_of(8 * (ids_ref[1] // 2), 8)
    copies = [
        fetch(y_hbm.at[:, pl.ds(first, 64), :], table_ref, sems, 0),
        fetch(phis_hbm, phis_ref, sems, 1),
        fetch(eta_hbm.at[pl.ds(rows, 8), :], eta_ref, sems, 2),
    ]
    wait_all(copies)
    coefs = data_by_table(phis_ref[...], table_ref[0], table_ref[1], NT)
    eta = eta_ref[...]
    eta = jnp.where(ids_ref[1] % 2 == 0, eta[:4], eta[4:])
    block_ref[:16] = jnp.concatenate([coefs[:16], coefs[16:]], 1)
    for j in range(4):
        block_ref[16 + 4 * j : 20 + 4 * j] = eta[:, 128 * j : 128 * j + 128]
    send_block(block_ref, out_ref, out_sems)


def first_kernel(
    ids_ref, got_ref, x_ref, wide_hbm, out_hbm, waves_hbm, out_ref, waves_ref, sems
):
    kx, ky, squares = wave_squares(ids_ref)
    size = jnp.sqrt(squares)
    got = [
        got_ref[pl.ds(512 * half + r, 16, stride=32), :] for half in range(2) for r in range(16)
    ]
    turned = [jnp.concatenate(got[8 * j : 8 * j + 8], 0).T for j in range(4)]
    first, second = jnp.concatenate(turned[:2], 1), jnp.concatenate(turned[2:], 1)
    sums, gaps = first + second, first - second
    sums = jnp.concatenate([sums[:64], sums[64:]], 1)
    gaps = jnp.concatenate([gaps[:64], gaps[64:]], 1)
    waves = to_waves(sums, gaps, x_ref)
    waves_ref[...] = waves
    copies = [fetch(waves_ref, waves_hbm, sems, 8)]
    both = jnp.concatenate([size * waves, squares * waves], 0)
    top, bottom = from_waves(both, x_ref)
    for s in range(8):
        out_ref[s, :64] = top[64 * s : 64 * s + 64]
        out_ref[s, 64:] = bottom[64 * s : 64 * s + 64]
        copies.append(fetch(out_ref.at[s], out_hbm.at[s], sems, s))
    wait_all(copies)


def second_kernel(
    got_ref, gathered_ref, y_ref, below_hbm, above_hbm, out_hbm, eta_hbm, curve_hbm, token_ref,
    out_ref, eta_ref, curve_ref, sems,
):
    pairs = [by_share(got_ref[2 * j], got_ref[2 * j + 1]) for j in range(4)]
    first = jnp.concatenate([p[0] for p in pairs], 1)
    second = jnp.concatenate([p[1] for p in pairs], 1)
    fields = data_by_table(jnp.concatenate([first, second], 0), y_ref[0], y_ref[1], NN)
    columns = []
    for j in range(4):
        block = [
            gathered_ref[pl.ds(512 * half + 16 + 4 * j + q, 16, stride=32), :]
            for half in range(2)
            for q in range(4)
        ]
        columns.append(jnp.concatenate(block, 0))
    eta = jnp.concatenate(columns, 1)
    eta_ref[...] = eta
    curve_ref[...] = 0.5 * eta * fields[128:]
    copies = [fetch(eta_ref, eta_hbm, sems, 8), fetch(curve_ref, curve_hbm, sems, 9)]
    waves = table_by_data(y_ref[0], y_ref[1], -eta * fields[:128])
    token_ref[...] = waves[:8, :128]
    for s in range(8):
        out_ref[s] = waves[64 * s : 64 * s + 64]
        copies.append(fetch(out_ref.at[s], out_hbm.at[s], sems, s))
    wait_all(copies)


def third_kernel(
    ids_ref, got_ref, x_ref, token_ref, out_hbm, waves_hbm, next_ref, out_ref, waves_ref, sems
):
    next_ref[...] = token_ref[...]
    kx, ky, squares = wave_squares(ids_ref)
    size = jnp.sqrt(squares)
    waves = folded_waves(got_ref, x_ref)
    waves_ref[...] = waves
    copies = [fetch(waves_ref, waves_hbm, sems, 8)]
    top, bottom = from_waves(size * waves, x_ref)
    both = jnp.concatenate([top, bottom], 1)
    for s in range(8):
        out_ref[s] = both[64 * s : 64 * s + 64]
        copies.append(fetch(out_ref.at[s], out_hbm.at[s], sems, s))
    wait_all(copies)


def fourth_kernel(
    got_ref, eta_hbm, curve_hbm, y_ref, token_ref, out_hbm, out_ref, eta_ref, curve_ref, sems
):
    copies = [fetch(eta_hbm, eta_ref, sems, 8), fetch(curve_hbm, curve_ref, sems, 9)]
    pairs = [by_share(got_ref[2 * j], got_ref[2 * j + 1]) for j in range(4)]
    coefs = jnp.concatenate(
        [jnp.concatenate([p[half] for p in pairs], 1) for half in range(2)], 0
    )
    field = data_by_table(coefs, y_ref[0], y_ref[1], NN)
    wait_all(copies)
    waves = table_by_data(y_ref[0], y_ref[1], -eta_ref[...] * (field + curve_ref[...]))
    copies = []
    for s in range(8):
        out_ref[s] = waves[64 * s : 64 * s + 64]
        copies.append(fetch(out_ref.at[s], out_hbm.at[s], sems, s))
    wait_all(copies)


def fifth_kernel(
    ids_ref, got_ref, x_ref, own_hbm, first_hbm, second_hbm, out_hbm,
    own_ref, out_ref, first_ref, second_ref, sems,
):
    start = pl.multiple_of(32 * ids_ref[0], 32)
    copies = [
        fetch(first_hbm, first_ref, sems, 1),
        fetch(second_hbm, second_ref, sems, 2),
        fetch(own_hbm.at[pl.ds(start, 80), :], own_ref, sems, 0),
    ]
    kx, ky, squares = wave_squares(ids_ref)
    size = jnp.sqrt(squares)
    third = folded_waves(got_ref, x_ref)
    wait_all(copies)
    first = first_ref[...]
    both = first + second_ref[...]
    blocks = []
    for part in (0, HALF):
        speed = kx[:, part : part + 256]
        blocks.append(speed * first[:, part + 256 : part + HALF])
        blocks.append(-speed * first[:, part : part + 256])
    slope_x = jnp.concatenate(blocks, 1)
    speed = ky[:32]
    slope_y = jnp.concatenate([speed * first[32:], -speed * first[:32]], 0)
    fields = jnp.concatenate(
        [size * (both + third), squares * both, size * squares * first, slope_x, slope_y], 0
    )
    fh, fl = split(fields)
    oh, ol = own_ref[:, :NX], own_ref[:, NX:]
    rows = dot(oh, fh, NT) + dot(oh, fl, NT) + dot(ol, fh, NT)
    out_ref[...] = rows[:ROWS]
    fetch(out_ref, out_hbm, sems, 3).wait()


def own_rows(values):
    pieces = []
    for cx in (1, 2):
        for cy in range(4):
            first = 16 * cx + 4 * cy + 1
            pieces.append(values[first : first + 2])
    return jnp.concatenate(pieces, 0)


def live_mass(ids_ref, mass):
    cell = lax.broadcasted_iota(jnp.int32, (64, 128), 0)
    at_x = 2 * ids_ref[0] - 1 + cell // 16
    at_z = 2 * ids_ref[1] - 1 + cell % 4
    inside = (at_x >= 0) & (at_x < 64) & (at_z >= 0) & (at_z < 16)
    return jnp.where(inside, mass, 0.0)


def pack_kernel(
    count_ref, parts_hbm, eta_hbm, own_hbm, up_hbm, down_hbm,
    parts_ref, eta_ref, own_ref, up_ref, down_ref, sems,
):
    wait_all([fetch(parts_hbm, parts_ref, sems, 3), fetch(eta_hbm, eta_ref, sems, 4)])
    lane = lax.broadcasted_iota(jnp.int32, (2, 128), 1)
    row = lax.broadcasted_iota(jnp.int32, (2, 128), 0)
    for i in range(8):
        for cx in range(2):
            for cy in range(4):
                value = parts_ref[i, cx, cy]
                if i == 7:
                    live = jnp.where(row == 0, count_ref[cx, cy, 0], count_ref[cx, cy, 1])
                    value = jnp.where(lane < live, value, 0.0)
                at = 16 * i + 8 * cx + 2 * cy
                own_ref[at : at + 2] = value
                at = 8 * i + 2 * cy
                side_ref = up_ref if cx == 1 else down_ref
                side_ref[at : at + 2] = value
    for j in range(4):
        up_ref[64 + 16 * j : 80 + 16 * j] = eta_ref[16:, 128 * j : 128 * j + 128]
        down_ref[64 + 24 * j : 88 + 24 * j] = eta_ref[:24, 128 * j : 128 * j + 128]
    wait_all([
        fetch(up_ref, up_hbm, sems, 0),
        fetch(down_ref, down_hbm, sems, 1),
        fetch(own_ref, own_hbm, sems, 2),
    ])


def extend_kernel(
    before_hbm, own_hbm, after_hbm, eta_hbm, wide_hbm, low_hbm, high_hbm, rows_hbm,
    before_ref, own_ref, after_ref, wide_ref, low_ref, high_ref, rows_ref, sems,
):
    wait_all([
        fetch(before_hbm, before_ref, sems, 4),
        fetch(own_hbm, own_ref, sems, 5),
        fetch(after_hbm, after_ref, sems, 6),
        fetch(eta_hbm, rows_ref.at[16:48], sems, 7),
    ])
    for i in range(8):
        wide_ref[32 * i : 32 * i + 8] = before_ref[8 * i : 8 * i + 8]
        wide_ref[32 * i + 8 : 32 * i + 24] = own_ref[16 * i : 16 * i + 16]
        wide_ref[32 * i + 24 : 32 * i + 32] = after_ref[8 * i : 8 * i + 8]
    for i in range(8):
        low_ref[16 * i : 16 * i + 16] = wide_ref[pl.ds(32 * i, 16, stride=2), :]
        high_ref[16 * i : 16 * i + 16] = wide_ref[pl.ds(32 * i + 1, 16, stride=2), :]
    for j in range(4):
        rows_ref[:16, 128 * j : 128 * j + 128] = before_ref[64 + 16 * j : 80 + 16 * j]
        rows_ref[48:, 128 * j : 128 * j + 128] = after_ref[64 + 24 * j : 88 + 24 * j]
    wait_all([
        fetch(low_ref, low_hbm, sems, 0),
        fetch(high_ref, high_hbm, sems, 1),
        fetch(wide_ref, wide_hbm, sems, 2),
        fetch(rows_ref, rows_hbm, sems, 3),
    ])


def spread_own(values, out_ref):
    columns = jnp.concatenate([own_rows(v) for v in values], 0)
    missing = 128 - columns.shape[0]
    if missing:
        columns = jnp.concatenate([columns, jnp.zeros((missing, 128), F32)], 0)
    columns = columns.T
    for i in range(len(values)):
        for o in range(16):
            k = 16 * i + o
            out_ref[o, i] = jnp.broadcast_to(columns[:, k : k + 1], (128, 128))


def reach_groups(count_ref, part):
    used = jnp.clip(count_ref[0] - part * PART, 0, PART)
    return (used + GROUP - 1) // GROUP


def reach_copy(source, target, sems, group):
    return pltpu.make_async_copy(source, target, sems.at[group])


def span_of(ref, group):
    return ref.at[pl.ds(pl.multiple_of(group * GROUP, GROUP), GROUP)]


def reach_channels(ids_ref, cells_ref, chan_ref):
    parts = [cells_ref[64 * i : 64 * i + 64] for i in (0, 1, 2, 6, 7)]
    mass = live_mass(ids_ref, parts[4])
    for i in range(3):
        chan_ref[i] = 0.5 * parts[i]
    chan_ref[3] = parts[3]
    chan_ref[4] = (2.0 * KERNEL_COEF) * mass
    chan_ref[5] = (-2.0 * KERNEL_COEF) * (mass / parts[3])


def reach_pairs(
    part, pairs_ref, count_ref, chan_ref, place_ref, density_ref,
    reach_ref, reach_hbm, sum_ref, reach_sems,
):
    def add_pair(t, carry):
        o = pairs_ref[0, t]
        cell = pairs_ref[1, t]
        place = [chan_ref[i, pl.ds(cell, 1), :] for i in range(3)]
        density, weight, volume = [chan_ref[i, pl.ds(cell, 1), :] for i in range(3, 6)]
        for piece in range(4):
            span = pl.ds(32 * piece, 32)
            gap_x = place_ref[o, 0, span, :] - place[0]
            gap_y = place_ref[o, 1, span, :] - place[1]
            gap_z = place_ref[o, 2, span, :] - place[2]
            square = gap_x * gap_x + gap_y * gap_y + gap_z * gap_z
            reach = jnp.maximum(1.0 - square * lax.rsqrt(jnp.maximum(square, 1e-30)), 0.0)
            reach = reach * reach * reach
            reach_ref[t - part * PART, span, :] = reach * weight
            sum_ref[o, span, :] += reach * ((density - density_ref[o, 0, span, :]) * volume)
        return carry

    def add_group(g, carry):
        start = part * PART + GROUP * g
        stop = jnp.minimum(start + GROUP, count_ref[0])
        lax.fori_loop(start, stop, add_pair, 0)
        reach_copy(span_of(reach_ref, g), span_of(reach_hbm, g), reach_sems, g).start()
        return carry

    lax.fori_loop(0, reach_groups(count_ref, part), add_group, 0)


def reach_end(part, count_ref, reach_ref, reach_hbm, reach_sems):
    def wait_group(g, carry):
        reach_copy(span_of(reach_ref, g), span_of(reach_hbm, g), reach_sems, g).wait()
        return carry

    lax.fori_loop(0, reach_groups(count_ref, part), wait_group, 0)


def reach_kernel(
    ids_ref, pairs_ref, count_ref, wide_hbm, below_hbm, above_hbm, token_ref,
    reach_hbm, place_hbm, density_hbm, sum_hbm, cells_hbm, done_ref,
    wide_ref, below_ref, above_ref, reach_ref, place_ref, density_ref, sum_ref, cells_ref,
    chan_ref, sems, reach_sems,
):
    copies = [
        fetch(wide_hbm, wide_ref, sems, 3),
        fetch(below_hbm, below_ref, sems, 4),
        fetch(above_hbm, above_ref, sems, 5),
    ]
    sum_ref[...] = jnp.zeros_like(sum_ref)
    done_ref[...] = token_ref[...]
    wait_all(copies)
    for i in range(8):
        low = wide_ref[pl.ds(32 * i, 16, stride=2), :]
        high = wide_ref[pl.ds(32 * i + 1, 16, stride=2), :]
        cells_ref[pl.ds(64 * i, 16, stride=4), :] = below_ref[16 * i : 16 * i + 16]
        cells_ref[pl.ds(64 * i + 1, 16, stride=4), :] = low
        cells_ref[pl.ds(64 * i + 2, 16, stride=4), :] = high
        cells_ref[pl.ds(64 * i + 3, 16, stride=4), :] = above_ref[16 * i : 16 * i + 16]
    copies = [fetch(cells_ref, cells_hbm, sems, 2)]
    reach_channels(ids_ref, cells_ref, chan_ref)
    spread_own([chan_ref[i] for i in range(3)], place_ref)
    copies.append(fetch(place_ref, place_hbm, sems, 0))
    spread_own([chan_ref[3]], density_ref)
    copies.append(fetch(density_ref, density_hbm, sems, 6))
    reach_pairs(
        0, pairs_ref, count_ref, chan_ref, place_ref, density_ref,
        reach_ref, reach_hbm, sum_ref, reach_sems,
    )
    copies.append(fetch(sum_ref, sum_hbm, sems, 1))
    reach_end(0, count_ref, reach_ref, reach_hbm, reach_sems)
    wait_all(copies)


def reach_rest_kernel(
    ids_ref, pairs_ref, count_ref, place_hbm, density_hbm, before_hbm, cells_hbm, token_ref,
    reach_hbm, sum_hbm, done_ref,
    reach_ref, place_ref, density_ref, sum_ref, cells_ref, chan_ref, sems, reach_sems,
):
    copies = [
        fetch(cells_hbm, cells_ref, sems, 0),
        fetch(place_hbm, place_ref, sems, 1),
        fetch(density_hbm, density_ref, sems, 2),
        fetch(before_hbm, sum_ref, sems, 3),
    ]
    done_ref[...] = token_ref[...]
    wait_all(copies[:1])
    reach_channels(ids_ref, cells_ref, chan_ref)
    wait_all(copies[1:])
    reach_pairs(
        1, pairs_ref, count_ref, chan_ref, place_ref, density_ref,
        reach_ref, reach_hbm, sum_ref, reach_sems,
    )
    last_copy = fetch(sum_ref, sum_hbm, sems, 4)
    reach_end(1, count_ref, reach_ref, reach_hbm, reach_sems)
    last_copy.wait()


def last_kernel(ids_ref, pairs_ref, count_ref, *refs):
    blocks_hbm, refs = refs[:8], refs[8:]
    (
        eta_hbm, cells_hbm, y_ref, reach_hbm, rest_hbm, place_hbm, sum_hbm, surface_ref, rate_ref,
        blocks, eta_ref, cells_ref, reach_ref, place_ref, sum_ref,
        coef_ref, field_ref, target_ref, speed_ref, half_ref, own_ref, sems, reach_sems,
    ) = refs
    block_copies = [fetch(blocks_hbm[i], blocks.at[i], sems, 4 + i) for i in range(8)]
    copies = [
        fetch(eta_hbm, eta_ref, sems, 0),
        fetch(cells_hbm, cells_ref, sems, 1),
        fetch(place_hbm, place_ref, sems, 2),
        fetch(sum_hbm, sum_ref, sems, 3),
    ]

    def start_group(g, carry):
        reach_copy(span_of(reach_hbm, g), span_of(reach_ref, g), reach_sems, g).start()
        return carry

    def start_rest(g, carry):
        at = g + PART // GROUP
        reach_copy(span_of(rest_hbm, g), span_of(reach_ref, at), reach_sems, at).start()
        return carry

    def wait_group(g, carry):
        reach_copy(span_of(reach_hbm, g), span_of(reach_ref, g), reach_sems, g).wait()
        return carry

    def wait_rest(g, carry):
        at = g + PART // GROUP
        reach_copy(span_of(rest_hbm, g), span_of(reach_ref, at), reach_sems, at).wait()
        return carry

    groups, rest_groups = reach_groups(count_ref, 0), reach_groups(count_ref, 1)
    lax.fori_loop(0, groups, start_group, 0)
    lax.fori_loop(0, rest_groups, start_rest, 0)
    slab = ids_ref[0]
    layer = ids_ref[1]
    wait_all(block_copies)
    for step in range(4):
        share = (layer // 2 + 4 - step) % 4
        lanes = pl.ds(pl.multiple_of(128 * share, 128), 128)
        mine, theirs = blocks[step], blocks[4 + step]
        for f in range(0, 4, 2):
            here = mine[:, 64 * f : 64 * f + 128]
            there = theirs[:, 64 * f : 64 * f + 128]
            first = jnp.where(layer % 2 == 0, here, there)
            second = jnp.where(layer % 2 == 0, there, here)
            first, second = by_share(first, second)
            coef_ref[ROWS * f : ROWS * f + ROWS, lanes] = first
            coef_ref[ROWS * f + ROWS : ROWS * f + 2 * ROWS, lanes] = second
        here, there = mine[:, 256:320], theirs[:, 256:320]
        first = jnp.where(layer % 2 == 0, here, there)
        second = jnp.where(layer % 2 == 0, there, here)
        coef_ref[4 * ROWS :, lanes] = jnp.concatenate([first, second], 1)
    fields = data_by_table(coef_ref[...], y_ref[0], y_ref[1], NN)
    wait_all(copies[:2])
    parts = [cells_ref[64 * i : 64 * i + 64] for i in range(8)]
    eta = eta_ref[...]
    vertical = (
        fields[:ROWS]
        + eta * fields[ROWS : 2 * ROWS]
        + 0.5 * eta * eta * fields[2 * ROWS : 3 * ROWS]
    )
    surface_ref[...] = vertical[16:48]
    sampled = (fields[3 * ROWS : 4 * ROWS], fields[4 * ROWS :], vertical)
    for f in range(3):
        field_ref[2 * f] = sampled[f]
        field_ref[2 * f + 1] = pltpu.roll(sampled[f], NY - 1, 1) - sampled[f]
    row_ids = lax.broadcasted_iota(jnp.int32, (24, 128), 0).astype(F32)

    def sample(cx, carry):
        first_row = pl.multiple_of(16 * cx, 16)
        origin = (32 * slab - 16 + 16 * cx).astype(F32)
        found = [[], [], []]
        place_x = cells_ref[pl.ds(first_row, 16), :] * 8.0 - origin
        place_y = cells_ref[pl.ds(pl.multiple_of(first_row + 64, 16), 16), :] * 64.0
        for cy in range(4):
            for cz in range(4):
                cell = 4 * cy + cz
                along = place_y[cell : cell + 1] - 128.0 * cy
                index = jnp.clip(along.astype(jnp.int32), 0, 127)
                part = along - index.astype(F32)
                index = jnp.broadcast_to(index, (24, 128))
                weight = jnp.maximum(0.0, 1.0 - jnp.abs(place_x[cell : cell + 1] - row_ids))
                weight_next = weight * part
                for f in range(3):
                    here = field_ref[2 * f, pl.ds(first_row, 24), 128 * cy : 128 * cy + 128]
                    step = field_ref[2 * f + 1, pl.ds(first_row, 24), 128 * cy : 128 * cy + 128]
                    here = jnp.take_along_axis(here, index, axis=1)
                    step = jnp.take_along_axis(step, index, axis=1)
                    found[f].append(
                        jnp.sum(weight * here + weight_next * step, axis=0, keepdims=True)
                    )
        for f in range(3):
            target_ref[f, pl.ds(first_row, 16), :] = jnp.concatenate(found[f], 0)
        return carry

    lax.fori_loop(0, 4, sample, 0)
    depth = jnp.exp((parts[2] - 32.0) * (1.0 / 32.0))
    close = jnp.clip(1.0 - parts[0] * (1.0 / 256.0), 0.0, 1.0)
    close = close * close
    for i in range(3):
        half_ref[i] = 0.5 * parts[i]
        speed = parts[3 + i]
        speed_ref[i] = speed + close * (target_ref[i] * depth - speed)
    spread_own([speed_ref[i] for i in range(3)], own_ref)
    wait_all(copies[2:])
    lax.fori_loop(0, groups, wait_group, 0)
    lax.fori_loop(0, rest_groups, wait_rest, 0)

    def add_pair(t, carry):
        o = pairs_ref[0, t]
        cell = pairs_ref[1, t]
        place = [half_ref[i, pl.ds(cell, 1), :] for i in range(3)]
        speed = [speed_ref[i, pl.ds(cell, 1), :] for i in range(3)]
        for piece in range(4):
            span = pl.ds(32 * piece, 32)
            approach = 0.0
            for i in range(3):
                approach = approach + (own_ref[o, i, span, :] - speed[i]) * (
                    place_ref[o, i, span, :] - place[i]
                )
            sum_ref[o, span, :] += reach_ref[t, span, :] * approach
        return carry

    lax.fori_loop(0, count_ref[0], add_pair, 0)
    ones = jnp.ones((8, 384), BF16)
    rates = []
    for o in range(16):
        total = sum_ref[o]
        high, rest = split(total)
        middle, last = split(total - high.astype(F32))
        rates.append(dot(ones, jnp.concatenate([high, middle, last], 1), NT)[:1])
    mass = own_rows(parts[7])
    rate_ref[...] = jnp.where(mass > 0.0, jnp.concatenate(rates, 0), 0.0)


def call(kernel, args, kinds, outs, name, vmem, scratch):
    specs = dict(S=SM, H=HB, V=VM)
    args = [
        pltpu.with_memory_space_constraint(a, pltpu.HBM) if k == "H" else a
        for a, k in zip(args, kinds, strict=True)
    ]
    return pl.pallas_call(
        kernel,
        out_shape=[
            pltpu.HBM(s, F32) if k == "H" else jax.ShapeDtypeStruct(s, F32) for s, k in outs
        ],
        in_specs=[specs[k] for k in kinds],
        out_specs=[specs[k] for _, k in outs],
        scratch_shapes=[pltpu.VMEM(s, F32) if isinstance(s, tuple) else s for s in scratch],
        compiler_params=pltpu.CompilerParams(vmem_limit_bytes=vmem * 1024 * 1024),
        name=name,
    )(*args)


def dma_sems(count):
    return pltpu.SemaphoreType.DMA((count,))


def passed(values, axis, by):
    size = lax.axis_size(axis)
    return lax.ppermute(values, axis, [(i, (i + by) % size) for i in range(size)])


def swap(block, axis):
    return lax.all_to_all(block, axis, split_axis=0, concat_axis=0, tiled=True)


def per_device(eta, phis, particles, cell_count, pair_cells, pair_count):
    slab = lax.axis_index("gx")
    layer = lax.axis_index("gz")
    ids = jnp.stack([slab, layer]).astype(jnp.int32)
    table = tables()
    y = jnp.asarray(table["y"])
    x = jnp.asarray(table["x"])
    own = jnp.asarray(table["own"])

    half_layers = lax.axis_size("gz") // 2

    own_cells, up, down = call(
        pack_kernel, (cell_count, particles, eta), "SHH",
        [((128, 128), "H"), ((128, 128), "H"), ((160, 128), "H")], "pack", 4,
        [(8, 2, 4, 2, 128), (32, NY), (128, 128), (128, 128), (160, 128), dma_sems(5)],
    )
    cells_before = passed(up, "gx", 1)
    cells_after = passed(down, "gx", -1)
    wide, low, high, eta_rows = call(
        extend_kernel, (cells_before, own_cells, cells_after, eta), "HHHH",
        [((256, 128), "H"), ((128, 128), "H"), ((128, 128), "H"), ((ROWS, NY), "H")], "extend", 4,
        [
            (128, 128),
            (128, 128),
            (160, 128),
            (256, 128),
            (128, 128),
            (128, 128),
            (ROWS, NY),
            dma_sems(8),
        ],
    )
    below = passed(high, "gz", 1)
    above = passed(low, "gz", -1)
    pairs = pair_cells.reshape(2, 96)
    count = pair_count.reshape(1)

    (block,) = call(
        start_kernel, (ids, phis, eta, y), "SHHH", [((32, 32, 128), "H")], "start", 4,
        [
            (32, NY),
            (8, NY),
            pltpu.VMEM((2, 64, NY), BF16),
            (32, 128),
            dma_sems(3),
            dma_sems(32),
        ],
    )
    gathered = swap(block, "gx").reshape(1024, 128)
    block, first = call(
        first_kernel,
        (ids, gathered, x, wide),
        "SVVH",
        [((8, 128, 128), "H"), ((64, NX), "H")],
        "first",
        8,
        [(8, 128, 128), (64, NX), dma_sems(9)],
    )
    got = swap(block, "gz")
    block, eta_part, curve, token = call(
        second_kernel,
        (got, gathered, y, below, above),
        "VVVHH",
        [((8, 64, 128), "H"), ((128, NY), "H"), ((128, NY), "H"), ((8, 128), "V")],
        "second",
        8,
        [(8, 64, 128), (128, NY), (128, NY), dma_sems(10)],
    )
    got = swap(block, "gz")
    reach, place, density, before, cells, token = call(
        reach_kernel,
        (ids, pairs, count, wide, below, above, token),
        "SSSHHHV",
        [
            ((PART, 128, 128), "H"),
            ((16, 3, 128, 128), "H"),
            ((16, 1, 128, 128), "H"),
            ((16, 128, 128), "H"),
            ((512, 128), "H"),
            ((8, 128), "V"),
        ],
        "reach",
        16,
        [
            (256, 128),
            (128, 128),
            (128, 128),
            (PART, 128, 128),
            (16, 3, 128, 128),
            (16, 1, 128, 128),
            (16, 128, 128),
            (512, 128),
            (6, 64, 128),
            dma_sems(7),
            dma_sems(PART // GROUP),
        ],
    )
    block, second, token = call(
        third_kernel,
        (ids, got, x, token),
        "SVVV",
        [((8, 64, 128), "H"), ((64, NX), "H"), ((8, 128), "V")],
        "third",
        8,
        [(8, 64, 128), (64, NX), dma_sems(9)],
    )
    got = swap(block, "gz")
    rest, before, token = call(
        reach_rest_kernel,
        (ids, pairs, count, place, density, before, cells, token),
        "SSSHHHHV",
        [((PART, 128, 128), "H"), ((16, 128, 128), "H"), ((8, 128), "V")],
        "rest",
        16,
        [
            (PART, 128, 128),
            (16, 3, 128, 128),
            (16, 1, 128, 128),
            (16, 128, 128),
            (512, 128),
            (6, 64, 128),
            dma_sems(5),
            dma_sems(PART // GROUP),
        ],
    )
    (block,) = call(
        fourth_kernel,
        (got, eta_part, curve, y, token),
        "VHHVV",
        [((8, 64, 128), "H")],
        "fourth",
        8,
        [(8, 64, 128), (128, NY), (128, NY), dma_sems(10)],
    )
    got = swap(block, "gz")
    (block,) = call(
        fifth_kernel,
        (ids, got, x, own, first, second),
        "SVVHHH",
        [((ROWS, 320), "H")],
        "fifth",
        8,
        [
            pltpu.VMEM((80, 2 * NX), BF16),
            (ROWS, 320),
            (64, NX),
            (64, NX),
            dma_sems(4),
        ],
    )
    along = [block] + [
        lax.ppermute(
            block,
            "gz",
            [
                (2 * i + core, 2 * ((i + step) % half_layers) + core)
                for i in range(half_layers)
                for core in range(2)
            ],
        )
        for step in range(1, half_layers)
    ]
    across = [
        lax.ppermute(b, "gz", [(i, i ^ 1) for i in range(2 * half_layers)]) for b in along
    ]
    surface, rate = call(
        last_kernel,
        (ids, pairs, count, *along, *across, eta_rows, cells, y, reach, rest, place, before),
        "SSS" + "H" * 10 + "VHHHH",
        [((32, NY), "V"), ((16, 128), "V")],
        "last",
        24,
        [
            (8, ROWS, 320),
            (ROWS, NY),
            (512, 128),
            (96, 128, 128),
            (16, 3, 128, 128),
            (16, 128, 128),
            (5 * ROWS, NY),
            (6, ROWS, NY),
            (3, 64, 128),
            (3, 64, 128),
            (3, 64, 128),
            (16, 3, 128, 128),
            dma_sems(12),
            dma_sems(96 // GROUP),
        ],
    )
    return surface, rate.reshape(2, 4, 2, 128)


def solution(mesh):
    in_specs = (
        P("gx", None),
        P("gx", None),
        P(None, "gx", None, "gz", None),
        P("gx", None, "gz"),
        P("gx", "gz", None, None),
        P("gx", "gz", None),
    )
    out_specs = (P("gx", None), P("gx", None, "gz", None))
    return jax.shard_map(
        per_device, mesh=mesh, in_specs=in_specs, out_specs=out_specs, check_vma=False
    )
```

```python
import functools

import jax
import jax.numpy as jnp
import ml_dtypes
import numpy as np
from jax import lax
from jax.experimental import pallas as pl
from jax.experimental.pallas import tpu as pltpu
from jax.sharding import PartitionSpec as P

TWO_PI = 6.283185307179586
KERNEL_COEF = -5.0 * 21.0 / (16.0 * 3.141592653589793)
NX = 1024
NY = 512
HALF = 512
ROWS = 72
F32 = jnp.float32
BF16 = jnp.bfloat16
NN = (((1,), (0,)), ((), ()))
NT = (((1,), (1,)), ((), ()))
VM = pl.BlockSpec(memory_space=pltpu.VMEM)
SM = pl.BlockSpec(memory_space=pltpu.SMEM)
HB = pl.BlockSpec(memory_space=pltpu.HBM)
GROUP = 8
PART = 48
TALL = 80
EARLY = 2 * ROWS


def parts_of(table):
    high = table.astype(ml_dtypes.bfloat16)
    low = (table - high.astype(np.float64)).astype(ml_dtypes.bfloat16)
    return high, low


@functools.cache
def tables():
    c = np.arange(NY)
    wave = 32 * (c // 64) + c % 32
    is_sine = (c % 64) >= 32
    wave[32] = NY // 2
    is_sine[32] = False
    angle = TWO_PI / NY * ((wave[:, None] * np.arange(NY)[None, :]) % NY)
    norm = np.where((wave == 0) | (wave == NY // 2), 1.0 / NY, 2.0 / NY) ** 0.5
    basis_y = np.where(is_sine[:, None], np.sin(angle), np.cos(angle)) * norm[:, None]
    r = np.arange(HALF)
    m = r % 256
    even = 2 * m
    even[256] = NX // 2
    odd = 2 * m + 1
    wave = np.concatenate([even, odd])
    is_sine = np.concatenate([r > 256, r >= 256])
    angle = TWO_PI / NX * ((np.arange(NX)[:, None] * wave[None, :]) % NX)
    norm = np.where((wave == 0) | (wave == NX // 2), 1.0 / NX, 2.0 / NX) ** 0.5
    basis_x = np.where(is_sine[None, :], np.sin(angle), np.cos(angle)) * norm[None, :]
    n = np.arange(HALF)
    order_gz = 32 * (n % 16) + 4 * (n // 64) + n // 16 % 4
    rows = (np.arange(NX + ROWS) - 16) % NX
    yh, yl = parts_of(basis_y)
    xh, xl = parts_of(basis_x[order_gz])
    return dict(
        y=np.stack([yh, yl]),
        x=np.stack([xh[:, :HALF], xh[:, HALF:], xl[:, :HALF], xl[:, HALF:]]),
        own=np.concatenate(parts_of(basis_x[rows]), axis=1),
    )


def split(value):
    high = value.astype(BF16)
    return high, (value - high.astype(F32)).astype(BF16)


def dot(lhs, rhs, dims):
    return lax.dot_general(lhs, rhs, dims, preferred_element_type=F32)


def data_by_table(value, high, low, dims):
    count = value.shape[0]
    vh, vl = split(value)
    both = dot(jnp.concatenate([vh, vl], 0), high, dims)
    return both[:count] + both[count:] + dot(vh, low, dims)


def table_by_data(high, low, value):
    count = value.shape[0]
    vh, vl = split(value)
    both = dot(high, jnp.concatenate([vh, vl], 0), NT)
    return both[:, :count] + both[:, count:] + dot(low, vh, NT)


def wave_squares(ids_ref):
    share = ids_ref[1]
    c = lax.broadcasted_iota(jnp.int32, (64, NX), 0)
    r = lax.broadcasted_iota(jnp.int32, (64, NX), 1)
    ky = 32 * share + c % 32
    ky = jnp.where((share == 0) & (c == 32), NY // 2, ky)
    m = r % 256
    kx = jnp.where(r == 256, NX // 2, jnp.where(r < HALF, 2 * m, 2 * m + 1))
    kx = kx.astype(F32) * (TWO_PI / NX)
    ky = ky.astype(F32) * (TWO_PI / NY)
    return kx, ky, kx * kx + ky * ky


def to_waves(sums, gaps, x_ref):
    even = data_by_table(sums, x_ref[0], x_ref[2], NN)
    odd = data_by_table(gaps, x_ref[1], x_ref[3], NN)
    return jnp.concatenate([even, odd], 1)


def low_lanes(shape):
    return lax.broadcasted_iota(jnp.int32, shape, 1) < 64


def folded_waves(got_ref, x_ref):
    sums, gaps = [], []
    mask = low_lanes((64, 128))
    for j in range(4):
        first, second = got_ref[2 * j], got_ref[2 * j + 1]
        first_turned = pltpu.roll(first, 64, 1)
        second_turned = pltpu.roll(second, 64, 1)
        sums.append(jnp.where(mask, first + first_turned, second + second_turned))
        gaps.append(jnp.where(mask, first - first_turned, second_turned - second))
    return to_waves(jnp.concatenate(sums, 1), jnp.concatenate(gaps, 1), x_ref)


def from_waves(waves, x_ref):
    even = table_by_data(x_ref[0], x_ref[2], waves[:, :HALF])
    odd = table_by_data(x_ref[1], x_ref[3], waves[:, HALF:])
    return even + odd, even - odd


def by_share(first, second):
    mask = low_lanes(first.shape)
    return (
        jnp.where(mask, first, pltpu.roll(second, 64, 1)),
        jnp.where(mask, pltpu.roll(first, 64, 1), second),
    )


def fetch(source, buffer, sems, place):
    copy = pltpu.make_async_copy(source, buffer, sems.at[place])
    copy.start()
    return copy


def wait_all(copies):
    for copy in copies:
        copy.wait()


def send_block(block_ref, out_ref, sems):
    wait_all([fetch(block_ref, out_ref.at[s], sems, s) for s in range(out_ref.shape[0])])


def start_kernel(
    ids_ref, phis_hbm, eta_hbm, y_hbm, out_ref, phis_ref, eta_ref, table_ref, block_ref, sems, out_sems
):
    first = pl.multiple_of(64 * ids_ref[1], 64)
    rows = pl.multiple_of(8 * (ids_ref[1] // 2), 8)
    copies = [
        fetch(y_hbm.at[:, pl.ds(first, 64), :], table_ref, sems, 0),
        fetch(phis_hbm, phis_ref, sems, 1),
        fetch(eta_hbm.at[pl.ds(rows, 8), :], eta_ref, sems, 2),
    ]
    wait_all(copies)
    coefs = data_by_table(phis_ref[...], table_ref[0], table_ref[1], NT)
    eta = eta_ref[...]
    eta = jnp.where(ids_ref[1] % 2 == 0, eta[:4], eta[4:])
    block_ref[:16] = jnp.concatenate([coefs[:16], coefs[16:]], 1)
    for j in range(4):
        block_ref[16 + 4 * j : 20 + 4 * j] = eta[:, 128 * j : 128 * j + 128]
    send_block(block_ref, out_ref, out_sems)


def first_kernel(
    ids_ref, got_ref, x_ref, wide_hbm, out_hbm, waves_hbm, out_ref, waves_ref, sems
):
    kx, ky, squares = wave_squares(ids_ref)
    size = jnp.sqrt(squares)
    got = [
        got_ref[pl.ds(512 * half + r, 16, stride=32), :] for half in range(2) for r in range(16)
    ]
    turned = [jnp.concatenate(got[8 * j : 8 * j + 8], 0).T for j in range(4)]
    first, second = jnp.concatenate(turned[:2], 1), jnp.concatenate(turned[2:], 1)
    sums, gaps = first + second, first - second
    sums = jnp.concatenate([sums[:64], sums[64:]], 1)
    gaps = jnp.concatenate([gaps[:64], gaps[64:]], 1)
    waves = to_waves(sums, gaps, x_ref)
    waves_ref[...] = waves
    copies = [fetch(waves_ref, waves_hbm, sems, 8)]
    both = jnp.concatenate([size * waves, squares * waves], 0)
    top, bottom = from_waves(both, x_ref)
    for s in range(8):
        out_ref[s, :64] = top[64 * s : 64 * s + 64]
        out_ref[s, 64:] = bottom[64 * s : 64 * s + 64]
        copies.append(fetch(out_ref.at[s], out_hbm.at[s], sems, s))
    wait_all(copies)


def second_kernel(
    got_ref, gathered_ref, y_ref, below_hbm, above_hbm, out_hbm, eta_hbm, curve_hbm, token_ref,
    out_ref, eta_ref, curve_ref, sems,
):
    pairs = [by_share(got_ref[2 * j], got_ref[2 * j + 1]) for j in range(4)]
    first = jnp.concatenate([p[0] for p in pairs], 1)
    second = jnp.concatenate([p[1] for p in pairs], 1)
    fields = data_by_table(jnp.concatenate([first, second], 0), y_ref[0], y_ref[1], NN)
    columns = []
    for j in range(4):
        block = [
            gathered_ref[pl.ds(512 * half + 16 + 4 * j + q, 16, stride=32), :]
            for half in range(2)
            for q in range(4)
        ]
        columns.append(jnp.concatenate(block, 0))
    eta = jnp.concatenate(columns, 1)
    eta_ref[...] = eta
    curve_ref[...] = 0.5 * eta * fields[128:]
    copies = [fetch(eta_ref, eta_hbm, sems, 8), fetch(curve_ref, curve_hbm, sems, 9)]
    waves = table_by_data(y_ref[0], y_ref[1], -eta * fields[:128])
    token_ref[...] = waves[:8, :128]
    for s in range(8):
        out_ref[s] = waves[64 * s : 64 * s + 64]
        copies.append(fetch(out_ref.at[s], out_hbm.at[s], sems, s))
    wait_all(copies)


def third_kernel(
    ids_ref, got_ref, x_ref, token_ref, out_hbm, waves_hbm, next_ref, out_ref, waves_ref, sems
):
    next_ref[...] = token_ref[...]
    kx, ky, squares = wave_squares(ids_ref)
    size = jnp.sqrt(squares)
    waves = folded_waves(got_ref, x_ref)
    waves_ref[...] = waves
    copies = [fetch(waves_ref, waves_hbm, sems, 8)]
    top, bottom = from_waves(size * waves, x_ref)
    both = jnp.concatenate([top, bottom], 1)
    for s in range(8):
        out_ref[s] = both[64 * s : 64 * s + 64]
        copies.append(fetch(out_ref.at[s], out_hbm.at[s], sems, s))
    wait_all(copies)


def fourth_kernel(
    got_ref, eta_hbm, curve_hbm, y_ref, token_ref, out_hbm, next_ref, out_ref, eta_ref, curve_ref, sems
):
    next_ref[...] = token_ref[...]
    copies = [fetch(eta_hbm, eta_ref, sems, 8), fetch(curve_hbm, curve_ref, sems, 9)]
    pairs = [by_share(got_ref[2 * j], got_ref[2 * j + 1]) for j in range(4)]
    coefs = jnp.concatenate(
        [jnp.concatenate([p[half] for p in pairs], 1) for half in range(2)], 0
    )
    field = data_by_table(coefs, y_ref[0], y_ref[1], NN)
    wait_all(copies)
    waves = table_by_data(y_ref[0], y_ref[1], -eta_ref[...] * (field + curve_ref[...]))
    copies = []
    for s in range(8):
        out_ref[s] = waves[64 * s : 64 * s + 64]
        copies.append(fetch(out_ref.at[s], out_hbm.at[s], sems, s))
    wait_all(copies)


def own_fields(own_ref, fields):
    fh, fl = split(fields)
    oh, ol = own_ref[:, :NX], own_ref[:, NX:]
    return dot(oh, fh, NT) + dot(oh, fl, NT) + dot(ol, fh, NT)


def early_kernel(
    ids_ref, own_hbm, first_hbm, second_hbm, token_ref, out_hbm,
    own_ref, first_ref, second_ref, out_ref, sems,
):
    start = pl.multiple_of(32 * ids_ref[0], 32)
    copies = [
        fetch(first_hbm, first_ref, sems, 1),
        fetch(second_hbm, second_ref, sems, 2),
        fetch(own_hbm.at[pl.ds(start, TALL), :], own_ref, sems, 0),
    ]
    kx, ky, squares = wave_squares(ids_ref)
    size = jnp.sqrt(squares)
    wait_all(copies)
    first = first_ref[...]
    both = first + second_ref[...]
    blocks = []
    for part in (0, HALF):
        speed = kx[:, part : part + 256]
        blocks.append(speed * first[:, part + 256 : part + HALF])
        blocks.append(-speed * first[:, part : part + 256])
    slope_x = jnp.concatenate(blocks, 1)
    speed = ky[:32]
    slope_y = jnp.concatenate([speed * first[32:], -speed * first[:32]], 0)
    rows = own_fields(
        own_ref,
        jnp.concatenate([squares * both, size * squares * first, slope_x, slope_y], 0),
    )
    out_ref[:ROWS] = rows[:ROWS, :128]
    out_ref[ROWS:] = rows[:ROWS, 128:]
    fetch(out_ref, out_hbm, sems, 3).wait()


def fifth_kernel(
    ids_ref, got_ref, x_ref, own_hbm, first_hbm, second_hbm, early_hbm, out_hbm,
    own_ref, out_ref, first_ref, second_ref, sems,
):
    start = pl.multiple_of(32 * ids_ref[0], 32)
    copies = [
        fetch(first_hbm, first_ref, sems, 1),
        fetch(second_hbm, second_ref, sems, 2),
        fetch(own_hbm.at[pl.ds(start, TALL), :], own_ref, sems, 0),
        fetch(early_hbm, out_ref.at[:EARLY], sems, 4),
    ]
    kx, ky, squares = wave_squares(ids_ref)
    size = jnp.sqrt(squares)
    third = folded_waves(got_ref, x_ref)
    wait_all(copies[:3])
    rows = own_fields(own_ref, size * (first_ref[...] + second_ref[...] + third))
    out_ref[EARLY:] = jnp.concatenate([rows[: TALL // 2], rows[TALL // 2 :]], 1)
    wait_all(copies[3:])
    fetch(out_ref, out_hbm, sems, 3).wait()


def own_rows(values):
    pieces = []
    for cx in (1, 2):
        for cy in range(4):
            first = 16 * cx + 4 * cy + 1
            pieces.append(values[first : first + 2])
    return jnp.concatenate(pieces, 0)


def live_mass(ids_ref, mass):
    cell = lax.broadcasted_iota(jnp.int32, (64, 128), 0)
    at_x = 2 * ids_ref[0] - 1 + cell // 16
    at_z = 2 * ids_ref[1] - 1 + cell % 4
    inside = (at_x >= 0) & (at_x < 64) & (at_z >= 0) & (at_z < 16)
    return jnp.where(inside, mass, 0.0)


def pack_kernel(
    count_ref, parts_hbm, eta_hbm, own_hbm, up_hbm, down_hbm,
    parts_ref, eta_ref, own_ref, up_ref, down_ref, sems,
):
    wait_all([fetch(parts_hbm, parts_ref, sems, 3), fetch(eta_hbm, eta_ref, sems, 4)])
    lane = lax.broadcasted_iota(jnp.int32, (2, 128), 1)
    row = lax.broadcasted_iota(jnp.int32, (2, 128), 0)
    for i in range(8):
        for cx in range(2):
            for cy in range(4):
                value = parts_ref[i, cx, cy]
                if i == 7:
                    live = jnp.where(row == 0, count_ref[cx, cy, 0], count_ref[cx, cy, 1])
                    value = jnp.where(lane < live, value, 0.0)
                at = 16 * i + 8 * cx + 2 * cy
                own_ref[at : at + 2] = value
                at = 8 * i + 2 * cy
                side_ref = up_ref if cx == 1 else down_ref
                side_ref[at : at + 2] = value
    for j in range(4):
        up_ref[64 + 16 * j : 80 + 16 * j] = eta_ref[16:, 128 * j : 128 * j + 128]
        down_ref[64 + 24 * j : 88 + 24 * j] = eta_ref[:24, 128 * j : 128 * j + 128]
    wait_all([
        fetch(up_ref, up_hbm, sems, 0),
        fetch(down_ref, down_hbm, sems, 1),
        fetch(own_ref, own_hbm, sems, 2),
    ])


def extend_kernel(
    before_hbm, own_hbm, after_hbm, eta_hbm, wide_hbm, low_hbm, high_hbm, rows_hbm,
    before_ref, own_ref, after_ref, wide_ref, low_ref, high_ref, rows_ref, sems,
):
    wait_all([
        fetch(before_hbm, before_ref, sems, 4),
        fetch(own_hbm, own_ref, sems, 5),
        fetch(after_hbm, after_ref, sems, 6),
        fetch(eta_hbm, rows_ref.at[16:48], sems, 7),
    ])
    for i in range(8):
        wide_ref[32 * i : 32 * i + 8] = before_ref[8 * i : 8 * i + 8]
        wide_ref[32 * i + 8 : 32 * i + 24] = own_ref[16 * i : 16 * i + 16]
        wide_ref[32 * i + 24 : 32 * i + 32] = after_ref[8 * i : 8 * i + 8]
    for i in range(8):
        low_ref[16 * i : 16 * i + 16] = wide_ref[pl.ds(32 * i, 16, stride=2), :]
        high_ref[16 * i : 16 * i + 16] = wide_ref[pl.ds(32 * i + 1, 16, stride=2), :]
    for j in range(4):
        rows_ref[:16, 128 * j : 128 * j + 128] = before_ref[64 + 16 * j : 80 + 16 * j]
        rows_ref[48:, 128 * j : 128 * j + 128] = after_ref[64 + 24 * j : 88 + 24 * j]
    wait_all([
        fetch(low_ref, low_hbm, sems, 0),
        fetch(high_ref, high_hbm, sems, 1),
        fetch(wide_ref, wide_hbm, sems, 2),
        fetch(rows_ref, rows_hbm, sems, 3),
    ])


def spread_own(values, out_ref):
    columns = jnp.concatenate([own_rows(v) for v in values], 0)
    missing = 128 - columns.shape[0]
    if missing:
        columns = jnp.concatenate([columns, jnp.zeros((missing, 128), F32)], 0)
    columns = columns.T
    for i in range(len(values)):
        for o in range(16):
            k = 16 * i + o
            out_ref[o, i] = jnp.broadcast_to(columns[:, k : k + 1], (128, 128))


def reach_groups(count_ref, part):
    used = jnp.clip(count_ref[0] - part * PART, 0, PART)
    return (used + GROUP - 1) // GROUP


def reach_copy(source, target, sems, group):
    return pltpu.make_async_copy(source, target, sems.at[group])


def span_of(ref, group):
    return ref.at[pl.ds(pl.multiple_of(group * GROUP, GROUP), GROUP)]


def reach_channels(ids_ref, cells_ref, chan_ref):
    parts = [cells_ref[64 * i : 64 * i + 64] for i in (0, 1, 2, 6, 7)]
    mass = live_mass(ids_ref, parts[4])
    for i in range(3):
        chan_ref[i] = 0.5 * parts[i]
    chan_ref[3] = parts[3]
    chan_ref[4] = (2.0 * KERNEL_COEF) * mass
    chan_ref[5] = (-2.0 * KERNEL_COEF) * (mass / parts[3])


def reach_pairs(
    part, pairs_ref, count_ref, chan_ref, place_ref, density_ref,
    reach_ref, reach_hbm, sum_ref, reach_sems,
):
    def add_pair(t, carry):
        o = pairs_ref[0, t]
        cell = pairs_ref[1, t]
        place = [chan_ref[i, pl.ds(cell, 1), :] for i in range(3)]
        density, weight, volume = [chan_ref[i, pl.ds(cell, 1), :] for i in range(3, 6)]
        for piece in range(4):
            span = pl.ds(32 * piece, 32)
            gap_x = place_ref[o, 0, span, :] - place[0]
            gap_y = place_ref[o, 1, span, :] - place[1]
            gap_z = place_ref[o, 2, span, :] - place[2]
            square = gap_x * gap_x + gap_y * gap_y + gap_z * gap_z
            reach = jnp.maximum(1.0 - square * lax.rsqrt(jnp.maximum(square, 1e-30)), 0.0)
            reach = reach * reach * reach
            reach_ref[t - part * PART, span, :] = reach * weight
            sum_ref[o, span, :] += reach * ((density - density_ref[o, 0, span, :]) * volume)
        return carry

    def add_group(g, carry):
        start = part * PART + GROUP * g
        stop = jnp.minimum(start + GROUP, count_ref[0])
        lax.fori_loop(start, stop, add_pair, 0)
        reach_copy(span_of(reach_ref, g), span_of(reach_hbm, g), reach_sems, g).start()
        return carry

    lax.fori_loop(0, reach_groups(count_ref, part), add_group, 0)


def reach_end(part, count_ref, reach_ref, reach_hbm, reach_sems):
    def wait_group(g, carry):
        reach_copy(span_of(reach_ref, g), span_of(reach_hbm, g), reach_sems, g).wait()
        return carry

    lax.fori_loop(0, reach_groups(count_ref, part), wait_group, 0)


def reach_kernel(
    ids_ref, pairs_ref, count_ref, wide_hbm, below_hbm, above_hbm, token_ref,
    reach_hbm, place_hbm, density_hbm, sum_hbm, cells_hbm, done_ref,
    wide_ref, below_ref, above_ref, reach_ref, place_ref, density_ref, sum_ref, cells_ref,
    chan_ref, sems, reach_sems,
):
    copies = [
        fetch(wide_hbm, wide_ref, sems, 3),
        fetch(below_hbm, below_ref, sems, 4),
        fetch(above_hbm, above_ref, sems, 5),
    ]
    sum_ref[...] = jnp.zeros_like(sum_ref)
    done_ref[...] = token_ref[...]
    wait_all(copies)
    for i in range(8):
        low = wide_ref[pl.ds(32 * i, 16, stride=2), :]
        high = wide_ref[pl.ds(32 * i + 1, 16, stride=2), :]
        cells_ref[pl.ds(64 * i, 16, stride=4), :] = below_ref[16 * i : 16 * i + 16]
        cells_ref[pl.ds(64 * i + 1, 16, stride=4), :] = low
        cells_ref[pl.ds(64 * i + 2, 16, stride=4), :] = high
        cells_ref[pl.ds(64 * i + 3, 16, stride=4), :] = above_ref[16 * i : 16 * i + 16]
    copies = [fetch(cells_ref, cells_hbm, sems, 2)]
    reach_channels(ids_ref, cells_ref, chan_ref)
    spread_own([chan_ref[i] for i in range(3)], place_ref)
    copies.append(fetch(place_ref, place_hbm, sems, 0))
    spread_own([chan_ref[3]], density_ref)
    copies.append(fetch(density_ref, density_hbm, sems, 6))
    reach_pairs(
        0, pairs_ref, count_ref, chan_ref, place_ref, density_ref,
        reach_ref, reach_hbm, sum_ref, reach_sems,
    )
    copies.append(fetch(sum_ref, sum_hbm, sems, 1))
    reach_end(0, count_ref, reach_ref, reach_hbm, reach_sems)
    wait_all(copies)


def reach_rest_kernel(
    ids_ref, pairs_ref, count_ref, place_hbm, density_hbm, before_hbm, cells_hbm, token_ref,
    reach_hbm, sum_hbm, done_ref,
    reach_ref, place_ref, density_ref, sum_ref, cells_ref, chan_ref, sems, reach_sems,
):
    copies = [
        fetch(cells_hbm, cells_ref, sems, 0),
        fetch(place_hbm, place_ref, sems, 1),
        fetch(density_hbm, density_ref, sems, 2),
        fetch(before_hbm, sum_ref, sems, 3),
    ]
    done_ref[...] = token_ref[...]
    wait_all(copies[:1])
    reach_channels(ids_ref, cells_ref, chan_ref)
    wait_all(copies[1:])
    reach_pairs(
        1, pairs_ref, count_ref, chan_ref, place_ref, density_ref,
        reach_ref, reach_hbm, sum_ref, reach_sems,
    )
    last_copy = fetch(sum_ref, sum_hbm, sems, 4)
    reach_end(1, count_ref, reach_ref, reach_hbm, reach_sems)
    last_copy.wait()


def last_kernel(ids_ref, pairs_ref, count_ref, *refs):
    blocks_hbm, refs = refs[:8], refs[8:]
    (
        eta_hbm, cells_hbm, y_ref, reach_hbm, rest_hbm, place_hbm, sum_hbm, surface_ref, rate_ref,
        blocks, eta_ref, cells_ref, reach_ref, place_ref, sum_ref,
        coef_ref, field_ref, target_ref, speed_ref, half_ref, own_ref, sems, reach_sems,
    ) = refs
    block_copies = [fetch(blocks_hbm[i], blocks.at[i], sems, 4 + i) for i in range(8)]
    copies = [
        fetch(eta_hbm, eta_ref, sems, 0),
        fetch(cells_hbm, cells_ref, sems, 1),
        fetch(place_hbm, place_ref, sems, 2),
        fetch(sum_hbm, sum_ref, sems, 3),
    ]

    def start_group(g, carry):
        reach_copy(span_of(reach_hbm, g), span_of(reach_ref, g), reach_sems, g).start()
        return carry

    def start_rest(g, carry):
        at = g + PART // GROUP
        reach_copy(span_of(rest_hbm, g), span_of(reach_ref, at), reach_sems, at).start()
        return carry

    def wait_group(g, carry):
        reach_copy(span_of(reach_hbm, g), span_of(reach_ref, g), reach_sems, g).wait()
        return carry

    def wait_rest(g, carry):
        at = g + PART // GROUP
        reach_copy(span_of(rest_hbm, g), span_of(reach_ref, at), reach_sems, at).wait()
        return carry

    groups, rest_groups = reach_groups(count_ref, 0), reach_groups(count_ref, 1)
    lax.fori_loop(0, groups, start_group, 0)
    lax.fori_loop(0, rest_groups, start_rest, 0)
    slab = ids_ref[0]
    layer = ids_ref[1]
    wait_all(block_copies)
    for step in range(4):
        share = (layer // 2 + 4 - step) % 4
        lanes = pl.ds(pl.multiple_of(128 * share, 128), 128)
        mine, theirs = blocks.at[step], blocks.at[4 + step]
        for at, size in ((0, ROWS), (ROWS, ROWS), (EARLY, TALL // 2)):
            here = mine[at : at + size, :]
            there = theirs[at : at + size, :]
            first = jnp.where(layer % 2 == 0, here, there)
            second = jnp.where(layer % 2 == 0, there, here)
            first, second = by_share(first, second)
            coef_ref[2 * at : 2 * at + size, lanes] = first
            coef_ref[2 * at + size : 2 * at + 2 * size, lanes] = second
    fields = data_by_table(coef_ref[...], y_ref[0], y_ref[1], NN)
    wait_all(copies[:2])
    parts = [cells_ref[64 * i : 64 * i + 64] for i in range(8)]
    eta = eta_ref[...]
    vertical = (
        fields[4 * ROWS : 5 * ROWS]
        + eta * fields[:ROWS]
        + 0.5 * eta * eta * fields[ROWS : 2 * ROWS]
    )
    surface_ref[...] = vertical[16:48]
    sampled = (fields[2 * ROWS : 3 * ROWS], fields[3 * ROWS : 4 * ROWS], vertical)
    for f in range(3):
        field_ref[2 * f] = sampled[f]
        field_ref[2 * f + 1] = pltpu.roll(sampled[f], NY - 1, 1) - sampled[f]
    row_ids = lax.broadcasted_iota(jnp.int32, (24, 128), 0).astype(F32)

    def sample(cx, carry):
        first_row = pl.multiple_of(16 * cx, 16)
        origin = (32 * slab - 16 + 16 * cx).astype(F32)
        found = [[], [], []]
        place_x = cells_ref[pl.ds(first_row, 16), :] * 8.0 - origin
        place_y = cells_ref[pl.ds(pl.multiple_of(first_row + 64, 16), 16), :] * 64.0
        for cy in range(4):
            for cz in range(4):
                cell = 4 * cy + cz
                along = place_y[cell : cell + 1] - 128.0 * cy
                index = jnp.clip(along.astype(jnp.int32), 0, 127)
                part = along - index.astype(F32)
                index = jnp.broadcast_to(index, (24, 128))
                weight = jnp.maximum(0.0, 1.0 - jnp.abs(place_x[cell : cell + 1] - row_ids))
                weight_next = weight * part
                for f in range(3):
                    here = field_ref[2 * f, pl.ds(first_row, 24), 128 * cy : 128 * cy + 128]
                    step = field_ref[2 * f + 1, pl.ds(first_row, 24), 128 * cy : 128 * cy + 128]
                    here = jnp.take_along_axis(here, index, axis=1)
                    step = jnp.take_along_axis(step, index, axis=1)
                    found[f].append(
                        jnp.sum(weight * here + weight_next * step, axis=0, keepdims=True)
                    )
        for f in range(3):
            target_ref[f, pl.ds(first_row, 16), :] = jnp.concatenate(found[f], 0)
        return carry

    lax.fori_loop(0, 4, sample, 0)
    depth = jnp.exp((parts[2] - 32.0) * (1.0 / 32.0))
    close = jnp.clip(1.0 - parts[0] * (1.0 / 256.0), 0.0, 1.0)
    close = close * close
    for i in range(3):
        half_ref[i] = 0.5 * parts[i]
        speed = parts[3 + i]
        speed_ref[i] = speed + close * (target_ref[i] * depth - speed)
    spread_own([speed_ref[i] for i in range(3)], own_ref)
    wait_all(copies[2:])

    def add_pair(t, carry):
        o = pairs_ref[0, t]
        cell = pairs_ref[1, t]
        place = [half_ref[i, pl.ds(cell, 1), :] for i in range(3)]
        speed = [speed_ref[i, pl.ds(cell, 1), :] for i in range(3)]
        for piece in range(4):
            span = pl.ds(32 * piece, 32)
            approach = 0.0
            for i in range(3):
                approach = approach + (own_ref[o, i, span, :] - speed[i]) * (
                    place_ref[o, i, span, :] - place[i]
                )
            sum_ref[o, span, :] += reach_ref[t, span, :] * approach
        return carry

    def add_group(g, carry):
        wait_group(g, 0)
        stop = jnp.minimum(GROUP * g + GROUP, count_ref[0])
        return lax.fori_loop(GROUP * g, stop, add_pair, carry)

    def add_rest(g, carry):
        wait_rest(g, 0)
        start = PART + GROUP * g
        stop = jnp.minimum(start + GROUP, count_ref[0])
        return lax.fori_loop(start, stop, add_pair, carry)

    lax.fori_loop(0, groups, add_group, 0)
    lax.fori_loop(0, rest_groups, add_rest, 0)
    ones = jnp.ones((8, 384), BF16)
    rates = []
    for o in range(16):
        total = sum_ref[o]
        high, rest = split(total)
        middle, last = split(total - high.astype(F32))
        rates.append(dot(ones, jnp.concatenate([high, middle, last], 1), NT)[:1])
    mass = own_rows(parts[7])
    rate_ref[...] = jnp.where(mass > 0.0, jnp.concatenate(rates, 0), 0.0)


def call(kernel, args, kinds, outs, name, vmem, scratch):
    specs = dict(S=SM, H=HB, V=VM)
    args = [
        pltpu.with_memory_space_constraint(a, pltpu.HBM) if k == "H" else a
        for a, k in zip(args, kinds, strict=True)
    ]
    return pl.pallas_call(
        kernel,
        out_shape=[
            pltpu.HBM(s, F32) if k == "H" else jax.ShapeDtypeStruct(s, F32) for s, k in outs
        ],
        in_specs=[specs[k] for k in kinds],
        out_specs=[specs[k] for _, k in outs],
        scratch_shapes=[pltpu.VMEM(s, F32) if isinstance(s, tuple) else s for s in scratch],
        compiler_params=pltpu.CompilerParams(vmem_limit_bytes=vmem * 1024 * 1024),
        name=name,
    )(*args)


def dma_sems(count):
    return pltpu.SemaphoreType.DMA((count,))


def passed(values, axis, by):
    size = lax.axis_size(axis)
    return lax.ppermute(values, axis, [(i, (i + by) % size) for i in range(size)])


def swap(block, axis):
    return lax.all_to_all(block, axis, split_axis=0, concat_axis=0, tiled=True)


def per_device(eta, phis, particles, cell_count, pair_cells, pair_count):
    slab = lax.axis_index("gx")
    layer = lax.axis_index("gz")
    ids = jnp.stack([slab, layer]).astype(jnp.int32)
    table = tables()
    y = jnp.asarray(table["y"])
    x = jnp.asarray(table["x"])
    own = jnp.asarray(table["own"])

    half_layers = lax.axis_size("gz") // 2

    own_cells, up, down = call(
        pack_kernel, (cell_count, particles, eta), "SHH",
        [((128, 128), "H"), ((128, 128), "H"), ((160, 128), "H")], "pack", 4,
        [(8, 2, 4, 2, 128), (32, NY), (128, 128), (128, 128), (160, 128), dma_sems(5)],
    )
    cells_before = passed(up, "gx", 1)
    cells_after = passed(down, "gx", -1)
    wide, low, high, eta_rows = call(
        extend_kernel, (cells_before, own_cells, cells_after, eta), "HHHH",
        [((256, 128), "H"), ((128, 128), "H"), ((128, 128), "H"), ((ROWS, NY), "H")], "extend", 4,
        [
            (128, 128),
            (128, 128),
            (160, 128),
            (256, 128),
            (128, 128),
            (128, 128),
            (ROWS, NY),
            dma_sems(8),
        ],
    )
    below = passed(high, "gz", 1)
    above = passed(low, "gz", -1)
    pairs = pair_cells.reshape(2, 96)
    count = pair_count.reshape(1)

    (block,) = call(
        start_kernel, (ids, phis, eta, y), "SHHH", [((32, 32, 128), "H")], "start", 4,
        [
            (32, NY),
            (8, NY),
            pltpu.VMEM((2, 64, NY), BF16),
            (32, 128),
            dma_sems(3),
            dma_sems(32),
        ],
    )
    gathered = swap(block, "gx").reshape(1024, 128)
    block, first = call(
        first_kernel,
        (ids, gathered, x, wide),
        "SVVH",
        [((8, 128, 128), "H"), ((64, NX), "H")],
        "first",
        8,
        [(8, 128, 128), (64, NX), dma_sems(9)],
    )
    got = swap(block, "gz")
    block, eta_part, curve, token = call(
        second_kernel,
        (got, gathered, y, below, above),
        "VVVHH",
        [((8, 64, 128), "H"), ((128, NY), "H"), ((128, NY), "H"), ((8, 128), "V")],
        "second",
        8,
        [(8, 64, 128), (128, NY), (128, NY), dma_sems(10)],
    )
    got = swap(block, "gz")
    reach, place, density, before, cells, token = call(
        reach_kernel,
        (ids, pairs, count, wide, below, above, token),
        "SSSHHHV",
        [
            ((PART, 128, 128), "H"),
            ((16, 3, 128, 128), "H"),
            ((16, 1, 128, 128), "H"),
            ((16, 128, 128), "H"),
            ((512, 128), "H"),
            ((8, 128), "V"),
        ],
        "reach",
        16,
        [
            (256, 128),
            (128, 128),
            (128, 128),
            (PART, 128, 128),
            (16, 3, 128, 128),
            (16, 1, 128, 128),
            (16, 128, 128),
            (512, 128),
            (6, 64, 128),
            dma_sems(7),
            dma_sems(PART // GROUP),
        ],
    )
    block, second, token = call(
        third_kernel,
        (ids, got, x, token),
        "SVVV",
        [((8, 64, 128), "H"), ((64, NX), "H"), ((8, 128), "V")],
        "third",
        8,
        [(8, 64, 128), (64, NX), dma_sems(9)],
    )
    got = swap(block, "gz")
    rest, before, token = call(
        reach_rest_kernel,
        (ids, pairs, count, place, density, before, cells, token),
        "SSSHHHHV",
        [((PART, 128, 128), "H"), ((16, 128, 128), "H"), ((8, 128), "V")],
        "rest",
        16,
        [
            (PART, 128, 128),
            (16, 3, 128, 128),
            (16, 1, 128, 128),
            (16, 128, 128),
            (512, 128),
            (6, 64, 128),
            dma_sems(5),
            dma_sems(PART // GROUP),
        ],
    )
    block, token = call(
        fourth_kernel,
        (got, eta_part, curve, y, token),
        "VHHVV",
        [((8, 64, 128), "H"), ((8, 128), "V")],
        "fourth",
        8,
        [(8, 64, 128), (128, NY), (128, NY), dma_sems(10)],
    )
    got = swap(block, "gz")
    (early,) = call(
        early_kernel,
        (ids, own, first, second, token),
        "SHHHV",
        [((EARLY, 128), "H")],
        "early",
        8,
        [pltpu.VMEM((TALL, 2 * NX), BF16), (64, NX), (64, NX), (EARLY, 128), dma_sems(4)],
    )
    (block,) = call(
        fifth_kernel,
        (ids, got, x, own, first, second, early),
        "SVVHHHH",
        [((EARLY + TALL // 2, 128), "H")],
        "fifth",
        8,
        [
            pltpu.VMEM((TALL, 2 * NX), BF16),
            (EARLY + TALL // 2, 128),
            (64, NX),
            (64, NX),
            dma_sems(5),
        ],
    )
    along = [block] + [
        lax.ppermute(
            block,
            "gz",
            [
                (2 * i + core, 2 * ((i + step) % half_layers) + core)
                for i in range(half_layers)
                for core in range(2)
            ],
        )
        for step in range(1, half_layers)
    ]
    across = [
        lax.ppermute(b, "gz", [(i, i ^ 1) for i in range(2 * half_layers)]) for b in along
    ]
    surface, rate = call(
        last_kernel,
        (ids, pairs, count, *along, *across, eta_rows, cells, y, reach, rest, place, before),
        "SSS" + "H" * 10 + "VHHHH",
        [((32, NY), "V"), ((16, 128), "V")],
        "last",
        24,
        [
            (8, EARLY + TALL // 2, 128),
            (ROWS, NY),
            (512, 128),
            (96, 128, 128),
            (16, 3, 128, 128),
            (16, 128, 128),
            (2 * EARLY + TALL, NY),
            (6, ROWS, NY),
            (3, 64, 128),
            (3, 64, 128),
            (3, 64, 128),
            (16, 3, 128, 128),
            dma_sems(12),
            dma_sems(96 // GROUP),
        ],
    )
    return surface, rate.reshape(2, 4, 2, 128)


def solution(mesh):
    in_specs = (
        P("gx", None),
        P("gx", None),
        P(None, "gx", None, "gz", None),
        P("gx", None, "gz"),
        P("gx", "gz", None, None),
        P("gx", "gz", None),
    )
    out_specs = (P("gx", None), P("gx", None, "gz", None))
    return jax.shard_map(
        per_device, mesh=mesh, in_specs=in_specs, out_specs=out_specs, check_vma=False
    )
```

```python
import functools

import jax
import jax.numpy as jnp
import ml_dtypes
import numpy as np
from jax import lax
from jax.experimental import pallas as pl
from jax.experimental.pallas import tpu as pltpu
from jax.sharding import PartitionSpec as P

TWO_PI = 6.283185307179586
KERNEL_COEF = -5.0 * 21.0 / (16.0 * 3.141592653589793)
NX = 1024
NY = 512
HALF = 512
ROWS = 72
F32 = jnp.float32
BF16 = jnp.bfloat16
NN = (((1,), (0,)), ((), ()))
NT = (((1,), (1,)), ((), ()))
VM = pl.BlockSpec(memory_space=pltpu.VMEM)
SM = pl.BlockSpec(memory_space=pltpu.SMEM)
HB = pl.BlockSpec(memory_space=pltpu.HBM)
GROUP = 8
PART = 48
TALL = 80
EARLY = 2 * ROWS


def parts_of(table):
    high = table.astype(ml_dtypes.bfloat16)
    low = (table - high.astype(np.float64)).astype(ml_dtypes.bfloat16)
    return high, low


@functools.cache
def tables():
    c = np.arange(NY)
    wave = 32 * (c // 64) + c % 32
    is_sine = (c % 64) >= 32
    wave[32] = NY // 2
    is_sine[32] = False
    angle = TWO_PI / NY * ((wave[:, None] * np.arange(NY)[None, :]) % NY)
    norm = np.where((wave == 0) | (wave == NY // 2), 1.0 / NY, 2.0 / NY) ** 0.5
    basis_y = np.where(is_sine[:, None], np.sin(angle), np.cos(angle)) * norm[:, None]
    r = np.arange(HALF)
    m = r % 256
    even = 2 * m
    even[256] = NX // 2
    odd = 2 * m + 1
    wave = np.concatenate([even, odd])
    is_sine = np.concatenate([r > 256, r >= 256])
    angle = TWO_PI / NX * ((np.arange(NX)[:, None] * wave[None, :]) % NX)
    norm = np.where((wave == 0) | (wave == NX // 2), 1.0 / NX, 2.0 / NX) ** 0.5
    basis_x = np.where(is_sine[None, :], np.sin(angle), np.cos(angle)) * norm[None, :]
    n = np.arange(HALF)
    order_gz = 32 * (n % 16) + 4 * (n // 64) + n // 16 % 4
    rows = (np.arange(NX + ROWS) - 16) % NX
    yh, yl = parts_of(basis_y)
    xh, xl = parts_of(basis_x[order_gz])
    return dict(
        y=np.stack([yh, yl]),
        x=np.stack([xh[:, :HALF], xh[:, HALF:], xl[:, :HALF], xl[:, HALF:]]),
        own=np.concatenate(parts_of(basis_x[rows]), axis=1),
    )


def split(value):
    high = value.astype(BF16)
    return high, (value - high.astype(F32)).astype(BF16)


def dot(lhs, rhs, dims):
    return lax.dot_general(lhs, rhs, dims, preferred_element_type=F32)


def data_by_table(value, high, low, dims):
    count = value.shape[0]
    vh, vl = split(value)
    both = dot(jnp.concatenate([vh, vl], 0), high, dims)
    return both[:count] + both[count:] + dot(vh, low, dims)


def table_by_data(high, low, value):
    count = value.shape[0]
    vh, vl = split(value)
    both = dot(high, jnp.concatenate([vh, vl], 0), NT)
    return both[:, :count] + both[:, count:] + dot(low, vh, NT)


def wave_squares(ids_ref):
    share = ids_ref[1]
    c = lax.broadcasted_iota(jnp.int32, (64, NX), 0)
    r = lax.broadcasted_iota(jnp.int32, (64, NX), 1)
    ky = 32 * share + c % 32
    ky = jnp.where((share == 0) & (c == 32), NY // 2, ky)
    m = r % 256
    kx = jnp.where(r == 256, NX // 2, jnp.where(r < HALF, 2 * m, 2 * m + 1))
    kx = kx.astype(F32) * (TWO_PI / NX)
    ky = ky.astype(F32) * (TWO_PI / NY)
    return kx, ky, kx * kx + ky * ky


def to_waves(sums, gaps, x_ref):
    even = data_by_table(sums, x_ref[0], x_ref[2], NN)
    odd = data_by_table(gaps, x_ref[1], x_ref[3], NN)
    return jnp.concatenate([even, odd], 1)


def low_lanes(shape):
    return lax.broadcasted_iota(jnp.int32, shape, 1) < 64


def folded_waves(got_ref, x_ref):
    sums, gaps = [], []
    mask = low_lanes((64, 128))
    for j in range(4):
        first, second = got_ref[2 * j], got_ref[2 * j + 1]
        first_turned = pltpu.roll(first, 64, 1)
        second_turned = pltpu.roll(second, 64, 1)
        sums.append(jnp.where(mask, first + first_turned, second + second_turned))
        gaps.append(jnp.where(mask, first - first_turned, second_turned - second))
    return to_waves(jnp.concatenate(sums, 1), jnp.concatenate(gaps, 1), x_ref)


def from_waves(waves, x_ref):
    even = table_by_data(x_ref[0], x_ref[2], waves[:, :HALF])
    odd = table_by_data(x_ref[1], x_ref[3], waves[:, HALF:])
    return even + odd, even - odd


def by_share(first, second):
    mask = low_lanes(first.shape)
    return (
        jnp.where(mask, first, pltpu.roll(second, 64, 1)),
        jnp.where(mask, pltpu.roll(first, 64, 1), second),
    )


def fetch(source, buffer, sems, place):
    copy = pltpu.make_async_copy(source, buffer, sems.at[place])
    copy.start()
    return copy


def wait_all(copies):
    for copy in copies:
        copy.wait()


def send_block(block_ref, out_ref, sems):
    wait_all([fetch(block_ref, out_ref.at[s], sems, s) for s in range(out_ref.shape[0])])


def start_kernel(
    ids_ref, phis_hbm, eta_hbm, y_hbm, out_ref, phis_ref, eta_ref, table_ref, block_ref, sems, out_sems
):
    first = pl.multiple_of(64 * ids_ref[1], 64)
    rows = pl.multiple_of(8 * (ids_ref[1] // 2), 8)
    copies = [
        fetch(y_hbm.at[:, pl.ds(first, 64), :], table_ref, sems, 0),
        fetch(phis_hbm, phis_ref, sems, 1),
        fetch(eta_hbm.at[pl.ds(rows, 8), :], eta_ref, sems, 2),
    ]
    wait_all(copies)
    coefs = data_by_table(phis_ref[...], table_ref[0], table_ref[1], NT)
    eta = eta_ref[...]
    eta = jnp.where(ids_ref[1] % 2 == 0, eta[:4], eta[4:])
    block_ref[:16] = jnp.concatenate([coefs[:16], coefs[16:]], 1)
    for j in range(4):
        block_ref[16 + 4 * j : 20 + 4 * j] = eta[:, 128 * j : 128 * j + 128]
    send_block(block_ref, out_ref, out_sems)


def first_kernel(
    ids_ref, got_ref, x_ref, wide_hbm, out_hbm, waves_hbm, out_ref, waves_ref, sems
):
    kx, ky, squares = wave_squares(ids_ref)
    size = jnp.sqrt(squares)
    got = [
        got_ref[pl.ds(512 * half + r, 16, stride=32), :] for half in range(2) for r in range(16)
    ]
    turned = [jnp.concatenate(got[8 * j : 8 * j + 8], 0).T for j in range(4)]
    first, second = jnp.concatenate(turned[:2], 1), jnp.concatenate(turned[2:], 1)
    sums, gaps = first + second, first - second
    sums = jnp.concatenate([sums[:64], sums[64:]], 1)
    gaps = jnp.concatenate([gaps[:64], gaps[64:]], 1)
    waves = to_waves(sums, gaps, x_ref)
    waves_ref[...] = waves
    copies = [fetch(waves_ref, waves_hbm, sems, 8)]
    both = jnp.concatenate([size * waves, squares * waves], 0)
    top, bottom = from_waves(both, x_ref)
    for s in range(8):
        out_ref[s, :64] = top[64 * s : 64 * s + 64]
        out_ref[s, 64:] = bottom[64 * s : 64 * s + 64]
        copies.append(fetch(out_ref.at[s], out_hbm.at[s], sems, s))
    wait_all(copies)


def second_kernel(
    got_ref, gathered_ref, y_ref, below_hbm, above_hbm, out_hbm, eta_hbm, curve_hbm, token_ref,
    out_ref, eta_ref, curve_ref, sems,
):
    pairs = [by_share(got_ref[2 * j], got_ref[2 * j + 1]) for j in range(4)]
    first = jnp.concatenate([p[0] for p in pairs], 1)
    second = jnp.concatenate([p[1] for p in pairs], 1)
    fields = data_by_table(jnp.concatenate([first, second], 0), y_ref[0], y_ref[1], NN)
    columns = []
    for j in range(4):
        block = [
            gathered_ref[pl.ds(512 * half + 16 + 4 * j + q, 16, stride=32), :]
            for half in range(2)
            for q in range(4)
        ]
        columns.append(jnp.concatenate(block, 0))
    eta = jnp.concatenate(columns, 1)
    eta_ref[...] = eta
    curve_ref[...] = 0.5 * eta * fields[128:]
    copies = [fetch(eta_ref, eta_hbm, sems, 8), fetch(curve_ref, curve_hbm, sems, 9)]
    waves = table_by_data(y_ref[0], y_ref[1], -eta * fields[:128])
    token_ref[...] = waves[:8, :128]
    for s in range(8):
        out_ref[s] = waves[64 * s : 64 * s + 64]
        copies.append(fetch(out_ref.at[s], out_hbm.at[s], sems, s))
    wait_all(copies)


def third_kernel(
    ids_ref, got_ref, x_ref, token_ref, out_hbm, waves_hbm, next_ref, out_ref, waves_ref, sems
):
    next_ref[...] = token_ref[...]
    kx, ky, squares = wave_squares(ids_ref)
    size = jnp.sqrt(squares)
    waves = folded_waves(got_ref, x_ref)
    waves_ref[...] = waves
    copies = [fetch(waves_ref, waves_hbm, sems, 8)]
    top, bottom = from_waves(size * waves, x_ref)
    both = jnp.concatenate([top, bottom], 1)
    for s in range(8):
        out_ref[s] = both[64 * s : 64 * s + 64]
        copies.append(fetch(out_ref.at[s], out_hbm.at[s], sems, s))
    wait_all(copies)


def fourth_kernel(
    got_ref, eta_hbm, curve_hbm, y_ref, token_ref, out_hbm, next_ref, out_ref, eta_ref, curve_ref, sems
):
    next_ref[...] = token_ref[...]
    copies = [fetch(eta_hbm, eta_ref, sems, 8), fetch(curve_hbm, curve_ref, sems, 9)]
    pairs = [by_share(got_ref[2 * j], got_ref[2 * j + 1]) for j in range(4)]
    coefs = jnp.concatenate(
        [jnp.concatenate([p[half] for p in pairs], 1) for half in range(2)], 0
    )
    field = data_by_table(coefs, y_ref[0], y_ref[1], NN)
    wait_all(copies)
    waves = table_by_data(y_ref[0], y_ref[1], -eta_ref[...] * (field + curve_ref[...]))
    copies = []
    for s in range(8):
        out_ref[s] = waves[64 * s : 64 * s + 64]
        copies.append(fetch(out_ref.at[s], out_hbm.at[s], sems, s))
    wait_all(copies)


def own_fields(own_ref, fields):
    fh, fl = split(fields)
    oh, ol = own_ref[:, :NX], own_ref[:, NX:]
    return dot(oh, fh, NT) + dot(oh, fl, NT) + dot(ol, fh, NT)


def early_kernel(
    ids_ref, own_hbm, first_hbm, second_hbm, token_ref, out_hbm,
    own_ref, first_ref, second_ref, out_ref, sems,
):
    start = pl.multiple_of(32 * ids_ref[0], 32)
    copies = [
        fetch(first_hbm, first_ref, sems, 1),
        fetch(second_hbm, second_ref, sems, 2),
        fetch(own_hbm.at[pl.ds(start, TALL), :], own_ref, sems, 0),
    ]
    kx, ky, squares = wave_squares(ids_ref)
    size = jnp.sqrt(squares)
    wait_all(copies)
    first = first_ref[...]
    both = first + second_ref[...]
    blocks = []
    for part in (0, HALF):
        speed = kx[:, part : part + 256]
        blocks.append(speed * first[:, part + 256 : part + HALF])
        blocks.append(-speed * first[:, part : part + 256])
    slope_x = jnp.concatenate(blocks, 1)
    speed = ky[:32]
    slope_y = jnp.concatenate([speed * first[32:], -speed * first[:32]], 0)
    rows = own_fields(
        own_ref,
        jnp.concatenate([squares * both, size * squares * first, slope_x, slope_y], 0),
    )
    out_ref[:ROWS] = rows[:ROWS, :128]
    out_ref[ROWS:] = rows[:ROWS, 128:]
    fetch(out_ref, out_hbm, sems, 3).wait()


def fifth_kernel(
    ids_ref, got_ref, x_ref, own_hbm, first_hbm, second_hbm, early_hbm, out_hbm,
    own_ref, out_ref, first_ref, second_ref, sems,
):
    start = pl.multiple_of(32 * ids_ref[0], 32)
    copies = [
        fetch(first_hbm, first_ref, sems, 1),
        fetch(second_hbm, second_ref, sems, 2),
        fetch(own_hbm.at[pl.ds(start, TALL), :], own_ref, sems, 0),
        fetch(early_hbm, out_ref.at[:EARLY], sems, 4),
    ]
    kx, ky, squares = wave_squares(ids_ref)
    size = jnp.sqrt(squares)
    third = folded_waves(got_ref, x_ref)
    wait_all(copies[:3])
    rows = own_fields(own_ref, size * (first_ref[...] + second_ref[...] + third))
    out_ref[EARLY:] = jnp.concatenate([rows[: TALL // 2], rows[TALL // 2 :]], 1)
    wait_all(copies[3:])
    fetch(out_ref, out_hbm, sems, 3).wait()


def own_rows(values):
    pieces = []
    for cx in (1, 2):
        for cy in range(4):
            first = 16 * cx + 4 * cy + 1
            pieces.append(values[first : first + 2])
    return jnp.concatenate(pieces, 0)


def live_mass(ids_ref, mass):
    cell = lax.broadcasted_iota(jnp.int32, (64, 128), 0)
    at_x = 2 * ids_ref[0] - 1 + cell // 16
    at_z = 2 * ids_ref[1] - 1 + cell % 4
    inside = (at_x >= 0) & (at_x < 64) & (at_z >= 0) & (at_z < 16)
    return jnp.where(inside, mass, 0.0)


def pack_kernel(
    count_ref, parts_hbm, own_hbm, low_hbm, high_hbm, parts_ref, own_ref, low_ref, high_ref, sems
):
    fetch(parts_hbm, parts_ref, sems, 3).wait()
    lane = lax.broadcasted_iota(jnp.int32, (2, 128), 1)
    row = lax.broadcasted_iota(jnp.int32, (2, 128), 0)
    for i in range(8):
        for cx in range(2):
            for cy in range(4):
                value = parts_ref[i, cx, cy]
                if i == 7:
                    live = jnp.where(row == 0, count_ref[cx, cy, 0], count_ref[cx, cy, 1])
                    value = jnp.where(lane < live, value, 0.0)
                at = 8 * i + 4 * cx + cy
                own_ref[2 * at : 2 * at + 2] = value
                low_ref[at : at + 1] = value[:1]
                high_ref[at : at + 1] = value[1:]
    wait_all([
        fetch(low_ref, low_hbm, sems, 0),
        fetch(high_ref, high_hbm, sems, 1),
        fetch(own_ref, own_hbm, sems, 2),
    ])


def extend_kernel(
    below_hbm, own_hbm, above_hbm, eta_hbm, wide_hbm, up_hbm, down_hbm,
    below_ref, own_ref, above_ref, eta_ref, wide_ref, up_ref, down_ref, sems,
):
    wait_all([
        fetch(below_hbm, below_ref, sems, 3),
        fetch(own_hbm, own_ref, sems, 4),
        fetch(above_hbm, above_ref, sems, 5),
        fetch(eta_hbm, eta_ref, sems, 6),
    ])
    for i in range(8):
        wide_ref[pl.ds(32 * i, 8, stride=4), :] = below_ref[8 * i : 8 * i + 8]
        wide_ref[pl.ds(32 * i + 1, 8, stride=4), :] = own_ref[pl.ds(16 * i, 8, stride=2), :]
        wide_ref[pl.ds(32 * i + 2, 8, stride=4), :] = own_ref[pl.ds(16 * i + 1, 8, stride=2), :]
        wide_ref[pl.ds(32 * i + 3, 8, stride=4), :] = above_ref[8 * i : 8 * i + 8]
    for i in range(8):
        down_ref[16 * i : 16 * i + 16] = wide_ref[32 * i : 32 * i + 16]
        up_ref[16 * i : 16 * i + 16] = wide_ref[32 * i + 16 : 32 * i + 32]
    for j in range(4):
        up_ref[128 + 16 * j : 144 + 16 * j] = eta_ref[16:, 128 * j : 128 * j + 128]
        down_ref[128 + 24 * j : 152 + 24 * j] = eta_ref[:24, 128 * j : 128 * j + 128]
    wait_all([
        fetch(up_ref, up_hbm, sems, 0),
        fetch(down_ref, down_hbm, sems, 1),
        fetch(wide_ref, wide_hbm, sems, 2),
    ])


def spread_own(values, out_ref):
    columns = jnp.concatenate([own_rows(v) for v in values], 0)
    missing = 128 - columns.shape[0]
    if missing:
        columns = jnp.concatenate([columns, jnp.zeros((missing, 128), F32)], 0)
    columns = columns.T
    for i in range(len(values)):
        for o in range(16):
            k = 16 * i + o
            out_ref[o, i] = jnp.broadcast_to(columns[:, k : k + 1], (128, 128))


def reach_groups(count_ref, part):
    used = jnp.clip(count_ref[0] - part * PART, 0, PART)
    return (used + GROUP - 1) // GROUP


def reach_copy(source, target, sems, group):
    return pltpu.make_async_copy(source, target, sems.at[group])


def span_of(ref, group):
    return ref.at[pl.ds(pl.multiple_of(group * GROUP, GROUP), GROUP)]


def reach_channels(ids_ref, cells_ref, chan_ref):
    parts = [cells_ref[64 * i : 64 * i + 64] for i in (0, 1, 2, 6, 7)]
    mass = live_mass(ids_ref, parts[4])
    for i in range(3):
        chan_ref[i] = 0.5 * parts[i]
    chan_ref[3] = parts[3]
    chan_ref[4] = (2.0 * KERNEL_COEF) * mass
    chan_ref[5] = (-2.0 * KERNEL_COEF) * (mass / parts[3])


def reach_pairs(
    part, pairs_ref, count_ref, chan_ref, place_ref, density_ref,
    reach_ref, reach_hbm, sum_ref, reach_sems,
):
    def add_pair(t, carry):
        o = pairs_ref[0, t]
        cell = pairs_ref[1, t]
        place = [chan_ref[i, pl.ds(cell, 1), :] for i in range(3)]
        density, weight, volume = [chan_ref[i, pl.ds(cell, 1), :] for i in range(3, 6)]
        for piece in range(4):
            span = pl.ds(32 * piece, 32)
            gap_x = place_ref[o, 0, span, :] - place[0]
            gap_y = place_ref[o, 1, span, :] - place[1]
            gap_z = place_ref[o, 2, span, :] - place[2]
            square = gap_x * gap_x + gap_y * gap_y + gap_z * gap_z
            reach = jnp.maximum(1.0 - square * lax.rsqrt(jnp.maximum(square, 1e-30)), 0.0)
            reach = reach * reach * reach
            reach_ref[t - part * PART, span, :] = reach * weight
            sum_ref[o, span, :] += reach * ((density - density_ref[o, 0, span, :]) * volume)
        return carry

    def add_group(g, carry):
        start = part * PART + GROUP * g
        stop = jnp.minimum(start + GROUP, count_ref[0])
        lax.fori_loop(start, stop, add_pair, 0)
        reach_copy(span_of(reach_ref, g), span_of(reach_hbm, g), reach_sems, g).start()
        return carry

    lax.fori_loop(0, reach_groups(count_ref, part), add_group, 0)


def reach_end(part, count_ref, reach_ref, reach_hbm, reach_sems):
    def wait_group(g, carry):
        reach_copy(span_of(reach_ref, g), span_of(reach_hbm, g), reach_sems, g).wait()
        return carry

    lax.fori_loop(0, reach_groups(count_ref, part), wait_group, 0)


def reach_kernel(
    ids_ref, pairs_ref, count_ref, wide_hbm, before_hbm, after_hbm, token_ref,
    reach_hbm, place_hbm, density_hbm, sum_hbm, cells_hbm, done_ref,
    wide_ref, before_ref, after_ref, reach_ref, place_ref, density_ref, sum_ref, cells_ref,
    chan_ref, sems, reach_sems,
):
    copies = [
        fetch(wide_hbm, wide_ref, sems, 3),
        fetch(before_hbm.at[pl.ds(0, 128), :], before_ref, sems, 4),
        fetch(after_hbm.at[pl.ds(0, 128), :], after_ref, sems, 5),
    ]
    sum_ref[...] = jnp.zeros_like(sum_ref)
    done_ref[...] = token_ref[...]
    wait_all(copies)
    for i in range(8):
        cells_ref[64 * i : 64 * i + 16] = before_ref[16 * i : 16 * i + 16]
        cells_ref[64 * i + 16 : 64 * i + 48] = wide_ref[32 * i : 32 * i + 32]
        cells_ref[64 * i + 48 : 64 * i + 64] = after_ref[16 * i : 16 * i + 16]
    copies = [fetch(cells_ref, cells_hbm, sems, 2)]
    reach_channels(ids_ref, cells_ref, chan_ref)
    spread_own([chan_ref[i] for i in range(3)], place_ref)
    copies.append(fetch(place_ref, place_hbm, sems, 0))
    spread_own([chan_ref[3]], density_ref)
    copies.append(fetch(density_ref, density_hbm, sems, 6))
    reach_pairs(
        0, pairs_ref, count_ref, chan_ref, place_ref, density_ref,
        reach_ref, reach_hbm, sum_ref, reach_sems,
    )
    copies.append(fetch(sum_ref, sum_hbm, sems, 1))
    reach_end(0, count_ref, reach_ref, reach_hbm, reach_sems)
    wait_all(copies)


def reach_rest_kernel(
    ids_ref, pairs_ref, count_ref, place_hbm, density_hbm, before_hbm, cells_hbm, token_ref,
    reach_hbm, sum_hbm, done_ref,
    reach_ref, place_ref, density_ref, sum_ref, cells_ref, chan_ref, sems, reach_sems,
):
    copies = [
        fetch(cells_hbm, cells_ref, sems, 0),
        fetch(place_hbm, place_ref, sems, 1),
        fetch(density_hbm, density_ref, sems, 2),
        fetch(before_hbm, sum_ref, sems, 3),
    ]
    done_ref[...] = token_ref[...]
    wait_all(copies[:1])
    reach_channels(ids_ref, cells_ref, chan_ref)
    wait_all(copies[1:])
    reach_pairs(
        1, pairs_ref, count_ref, chan_ref, place_ref, density_ref,
        reach_ref, reach_hbm, sum_ref, reach_sems,
    )
    last_copy = fetch(sum_ref, sum_hbm, sems, 4)
    reach_end(1, count_ref, reach_ref, reach_hbm, reach_sems)
    last_copy.wait()


def last_kernel(ids_ref, pairs_ref, count_ref, *refs):
    blocks_hbm, refs = refs[:8], refs[8:]
    (
        before_hbm, eta_hbm, after_hbm, cells_hbm, y_ref, reach_hbm, rest_hbm, place_hbm, sum_hbm, surface_ref, rate_ref,
        blocks, eta_ref, cells_ref, reach_ref, place_ref, sum_ref,
        coef_ref, field_ref, target_ref, speed_ref, half_ref, own_ref, sems, reach_sems,
    ) = refs
    block_copies = [fetch(blocks_hbm[i], blocks.at[i], sems, 4 + i) for i in range(8)]
    copies = [
        fetch(eta_hbm, eta_ref.at[pl.ds(16, 32), :], sems, 0),
        fetch(cells_hbm, cells_ref, sems, 1),
        fetch(place_hbm, place_ref, sems, 2),
        fetch(sum_hbm, sum_ref, sems, 3),
    ]

    for j in range(4):
        lanes = pl.ds(128 * j, 128)
        from_before = before_hbm.at[pl.ds(128 + 16 * j, 16), :]
        from_after = after_hbm.at[pl.ds(128 + 24 * j, 24), :]
        block_copies.append(fetch(from_before, eta_ref.at[pl.ds(0, 16), lanes], sems, 12 + j))
        block_copies.append(fetch(from_after, eta_ref.at[pl.ds(48, 24), lanes], sems, 16 + j))

    def start_group(g, carry):
        reach_copy(span_of(reach_hbm, g), span_of(reach_ref, g), reach_sems, g).start()
        return carry

    def start_rest(g, carry):
        at = g + PART // GROUP
        reach_copy(span_of(rest_hbm, g), span_of(reach_ref, at), reach_sems, at).start()
        return carry

    def wait_group(g, carry):
        reach_copy(span_of(reach_hbm, g), span_of(reach_ref, g), reach_sems, g).wait()
        return carry

    def wait_rest(g, carry):
        at = g + PART // GROUP
        reach_copy(span_of(rest_hbm, g), span_of(reach_ref, at), reach_sems, at).wait()
        return carry

    groups, rest_groups = reach_groups(count_ref, 0), reach_groups(count_ref, 1)
    lax.fori_loop(0, groups, start_group, 0)
    lax.fori_loop(0, rest_groups, start_rest, 0)
    slab = ids_ref[0]
    layer = ids_ref[1]
    wait_all(block_copies)
    for step in range(4):
        share = (layer // 2 + 4 - step) % 4
        lanes = pl.ds(pl.multiple_of(128 * share, 128), 128)
        mine, theirs = blocks.at[step], blocks.at[4 + step]
        for at, size in ((0, ROWS), (ROWS, ROWS), (EARLY, TALL // 2)):
            here = mine[at : at + size, :]
            there = theirs[at : at + size, :]
            first = jnp.where(layer % 2 == 0, here, there)
            second = jnp.where(layer % 2 == 0, there, here)
            first, second = by_share(first, second)
            coef_ref[2 * at : 2 * at + size, lanes] = first
            coef_ref[2 * at + size : 2 * at + 2 * size, lanes] = second
    fields = data_by_table(coef_ref[...], y_ref[0], y_ref[1], NN)
    wait_all(copies[:2])
    parts = [cells_ref[64 * i : 64 * i + 64] for i in range(8)]
    eta = eta_ref[...]
    vertical = (
        fields[4 * ROWS : 5 * ROWS]
        + eta * fields[:ROWS]
        + 0.5 * eta * eta * fields[ROWS : 2 * ROWS]
    )
    surface_ref[...] = vertical[16:48]
    sampled = (fields[2 * ROWS : 3 * ROWS], fields[3 * ROWS : 4 * ROWS], vertical)
    for f in range(3):
        field_ref[2 * f] = sampled[f]
        field_ref[2 * f + 1] = pltpu.roll(sampled[f], NY - 1, 1) - sampled[f]
    row_ids = lax.broadcasted_iota(jnp.int32, (24, 128), 0).astype(F32)

    def sample(cx, carry):
        first_row = pl.multiple_of(16 * cx, 16)
        origin = (32 * slab - 16 + 16 * cx).astype(F32)
        found = [[], [], []]
        place_x = cells_ref[pl.ds(first_row, 16), :] * 8.0 - origin
        place_y = cells_ref[pl.ds(pl.multiple_of(first_row + 64, 16), 16), :] * 64.0
        for cy in range(4):
            for cz in range(4):
                cell = 4 * cy + cz
                along = place_y[cell : cell + 1] - 128.0 * cy
                index = jnp.clip(along.astype(jnp.int32), 0, 127)
                part = along - index.astype(F32)
                index = jnp.broadcast_to(index, (24, 128))
                weight = jnp.maximum(0.0, 1.0 - jnp.abs(place_x[cell : cell + 1] - row_ids))
                weight_next = weight * part
                for f in range(3):
                    here = field_ref[2 * f, pl.ds(first_row, 24), 128 * cy : 128 * cy + 128]
                    step = field_ref[2 * f + 1, pl.ds(first_row, 24), 128 * cy : 128 * cy + 128]
                    here = jnp.take_along_axis(here, index, axis=1)
                    step = jnp.take_along_axis(step, index, axis=1)
                    found[f].append(
                        jnp.sum(weight * here + weight_next * step, axis=0, keepdims=True)
                    )
        for f in range(3):
            target_ref[f, pl.ds(first_row, 16), :] = jnp.concatenate(found[f], 0)
        return carry

    lax.fori_loop(0, 4, sample, 0)
    depth = jnp.exp((parts[2] - 32.0) * (1.0 / 32.0))
    close = jnp.clip(1.0 - parts[0] * (1.0 / 256.0), 0.0, 1.0)
    close = close * close
    for i in range(3):
        half_ref[i] = 0.5 * parts[i]
        speed = parts[3 + i]
        speed_ref[i] = speed + close * (target_ref[i] * depth - speed)
    spread_own([speed_ref[i] for i in range(3)], own_ref)
    wait_all(copies[2:])

    def add_pair(t, carry):
        o = pairs_ref[0, t]
        cell = pairs_ref[1, t]
        place = [half_ref[i, pl.ds(cell, 1), :] for i in range(3)]
        speed = [speed_ref[i, pl.ds(cell, 1), :] for i in range(3)]
        for piece in range(4):
            span = pl.ds(32 * piece, 32)
            approach = 0.0
            for i in range(3):
                approach = approach + (own_ref[o, i, span, :] - speed[i]) * (
                    place_ref[o, i, span, :] - place[i]
                )
            sum_ref[o, span, :] += reach_ref[t, span, :] * approach
        return carry

    def add_group(g, carry):
        wait_group(g, 0)
        stop = jnp.minimum(GROUP * g + GROUP, count_ref[0])
        return lax.fori_loop(GROUP * g, stop, add_pair, carry)

    def add_rest(g, carry):
        wait_rest(g, 0)
        start = PART + GROUP * g
        stop = jnp.minimum(start + GROUP, count_ref[0])
        return lax.fori_loop(start, stop, add_pair, carry)

    lax.fori_loop(0, groups, add_group, 0)
    lax.fori_loop(0, rest_groups, add_rest, 0)
    ones = jnp.ones((8, 384), BF16)
    rates = []
    for o in range(16):
        total = sum_ref[o]
        high, rest = split(total)
        middle, last = split(total - high.astype(F32))
        rates.append(dot(ones, jnp.concatenate([high, middle, last], 1), NT)[:1])
    mass = own_rows(parts[7])
    rate_ref[...] = jnp.where(mass > 0.0, jnp.concatenate(rates, 0), 0.0)


def call(kernel, args, kinds, outs, name, vmem, scratch):
    specs = dict(S=SM, H=HB, V=VM)
    args = [
        pltpu.with_memory_space_constraint(a, pltpu.HBM) if k == "H" else a
        for a, k in zip(args, kinds, strict=True)
    ]
    return pl.pallas_call(
        kernel,
        out_shape=[
            pltpu.HBM(s, F32) if k == "H" else jax.ShapeDtypeStruct(s, F32) for s, k in outs
        ],
        in_specs=[specs[k] for k in kinds],
        out_specs=[specs[k] for _, k in outs],
        scratch_shapes=[pltpu.VMEM(s, F32) if isinstance(s, tuple) else s for s in scratch],
        compiler_params=pltpu.CompilerParams(vmem_limit_bytes=vmem * 1024 * 1024),
        name=name,
    )(*args)


def dma_sems(count):
    return pltpu.SemaphoreType.DMA((count,))


def passed(values, axis, by):
    size = lax.axis_size(axis)
    return lax.ppermute(values, axis, [(i, (i + by) % size) for i in range(size)])


def swap(block, axis):
    return lax.all_to_all(block, axis, split_axis=0, concat_axis=0, tiled=True)


def per_device(eta, phis, particles, cell_count, pair_cells, pair_count):
    slab = lax.axis_index("gx")
    layer = lax.axis_index("gz")
    ids = jnp.stack([slab, layer]).astype(jnp.int32)
    table = tables()
    y = jnp.asarray(table["y"])
    x = jnp.asarray(table["x"])
    own = jnp.asarray(table["own"])

    half_layers = lax.axis_size("gz") // 2

    own_cells, low, high = call(
        pack_kernel, (cell_count, particles), "SH",
        [((128, 128), "H"), ((64, 128), "H"), ((64, 128), "H")], "pack", 4,
        [(8, 2, 4, 2, 128), (128, 128), (64, 128), (64, 128), dma_sems(4)],
    )
    below = passed(high, "gz", 1)
    above = passed(low, "gz", -1)
    wide, up, down = call(
        extend_kernel, (below, own_cells, above, eta), "HHHH",
        [((256, 128), "H"), ((192, 128), "H"), ((224, 128), "H")], "extend", 4,
        [
            (64, 128),
            (128, 128),
            (64, 128),
            (32, NY),
            (256, 128),
            (192, 128),
            (224, 128),
            dma_sems(7),
        ],
    )
    cells_before = passed(up, "gx", 1)
    cells_after = passed(down, "gx", -1)
    pairs = pair_cells.reshape(2, 96)
    count = pair_count.reshape(1)

    (block,) = call(
        start_kernel, (ids, phis, eta, y), "SHHH", [((32, 32, 128), "H")], "start", 4,
        [
            (32, NY),
            (8, NY),
            pltpu.VMEM((2, 64, NY), BF16),
            (32, 128),
            dma_sems(3),
            dma_sems(32),
        ],
    )
    gathered = swap(block, "gx").reshape(1024, 128)
    block, first = call(
        first_kernel,
        (ids, gathered, x, wide),
        "SVVH",
        [((8, 128, 128), "H"), ((64, NX), "H")],
        "first",
        8,
        [(8, 128, 128), (64, NX), dma_sems(9)],
    )
    got = swap(block, "gz")
    block, eta_part, curve, token = call(
        second_kernel,
        (got, gathered, y, cells_before, cells_after),
        "VVVHH",
        [((8, 64, 128), "H"), ((128, NY), "H"), ((128, NY), "H"), ((8, 128), "V")],
        "second",
        8,
        [(8, 64, 128), (128, NY), (128, NY), dma_sems(10)],
    )
    got = swap(block, "gz")
    reach, place, density, before, cells, token = call(
        reach_kernel,
        (ids, pairs, count, wide, cells_before, cells_after, token),
        "SSSHHHV",
        [
            ((PART, 128, 128), "H"),
            ((16, 3, 128, 128), "H"),
            ((16, 1, 128, 128), "H"),
            ((16, 128, 128), "H"),
            ((512, 128), "H"),
            ((8, 128), "V"),
        ],
        "reach",
        16,
        [
            (256, 128),
            (128, 128),
            (128, 128),
            (PART, 128, 128),
            (16, 3, 128, 128),
            (16, 1, 128, 128),
            (16, 128, 128),
            (512, 128),
            (6, 64, 128),
            dma_sems(7),
            dma_sems(PART // GROUP),
        ],
    )
    block, second, token = call(
        third_kernel,
        (ids, got, x, token),
        "SVVV",
        [((8, 64, 128), "H"), ((64, NX), "H"), ((8, 128), "V")],
        "third",
        8,
        [(8, 64, 128), (64, NX), dma_sems(9)],
    )
    got = swap(block, "gz")
    rest, before, token = call(
        reach_rest_kernel,
        (ids, pairs, count, place, density, before, cells, token),
        "SSSHHHHV",
        [((PART, 128, 128), "H"), ((16, 128, 128), "H"), ((8, 128), "V")],
        "rest",
        16,
        [
            (PART, 128, 128),
            (16, 3, 128, 128),
            (16, 1, 128, 128),
            (16, 128, 128),
            (512, 128),
            (6, 64, 128),
            dma_sems(5),
            dma_sems(PART // GROUP),
        ],
    )
    block, token = call(
        fourth_kernel,
        (got, eta_part, curve, y, token),
        "VHHVV",
        [((8, 64, 128), "H"), ((8, 128), "V")],
        "fourth",
        8,
        [(8, 64, 128), (128, NY), (128, NY), dma_sems(10)],
    )
    got = swap(block, "gz")
    (early,) = call(
        early_kernel,
        (ids, own, first, second, token),
        "SHHHV",
        [((EARLY, 128), "H")],
        "early",
        8,
        [pltpu.VMEM((TALL, 2 * NX), BF16), (64, NX), (64, NX), (EARLY, 128), dma_sems(4)],
    )
    (block,) = call(
        fifth_kernel,
        (ids, got, x, own, first, second, early),
        "SVVHHHH",
        [((EARLY + TALL // 2, 128), "H")],
        "fifth",
        8,
        [
            pltpu.VMEM((TALL, 2 * NX), BF16),
            (EARLY + TALL // 2, 128),
            (64, NX),
            (64, NX),
            dma_sems(5),
        ],
    )
    along = [block] + [
        lax.ppermute(
            block,
            "gz",
            [
                (2 * i + core, 2 * ((i + step) % half_layers) + core)
                for i in range(half_layers)
                for core in range(2)
            ],
        )
        for step in range(1, half_layers)
    ]
    across = [
        lax.ppermute(b, "gz", [(i, i ^ 1) for i in range(2 * half_layers)]) for b in along
    ]
    surface, rate = call(
        last_kernel,
        (ids, pairs, count, *along, *across, cells_before, eta, cells_after, cells, y, reach, rest, place, before),
        "SSS" + "H" * 12 + "VHHHH",
        [((32, NY), "V"), ((16, 128), "V")],
        "last",
        24,
        [
            (8, EARLY + TALL // 2, 128),
            (ROWS, NY),
            (512, 128),
            (96, 128, 128),
            (16, 3, 128, 128),
            (16, 128, 128),
            (2 * EARLY + TALL, NY),
            (6, ROWS, NY),
            (3, 64, 128),
            (3, 64, 128),
            (3, 64, 128),
            (16, 3, 128, 128),
            dma_sems(20),
            dma_sems(96 // GROUP),
        ],
    )
    return surface, rate.reshape(2, 4, 2, 128)


def solution(mesh):
    in_specs = (
        P("gx", None),
        P("gx", None),
        P(None, "gx", None, "gz", None),
        P("gx", None, "gz"),
        P("gx", "gz", None, None),
        P("gx", "gz", None),
    )
    out_specs = (P("gx", None), P("gx", None, "gz", None))
    return jax.shard_map(
        per_device, mesh=mesh, in_specs=in_specs, out_specs=out_specs, check_vma=False
    )
```

```python
import functools

import jax
import jax.numpy as jnp
import ml_dtypes
import numpy as np
from jax import lax
from jax.experimental import pallas as pl
from jax.experimental.pallas import tpu as pltpu
from jax.sharding import PartitionSpec as P

TWO_PI = 6.283185307179586
KERNEL_COEF = -5.0 * 21.0 / (16.0 * 3.141592653589793)
NX = 1024
NY = 512
HALF = 512
ROWS = 72
F32 = jnp.float32
BF16 = jnp.bfloat16
NN = (((1,), (0,)), ((), ()))
NT = (((1,), (1,)), ((), ()))
VM = pl.BlockSpec(memory_space=pltpu.VMEM)
SM = pl.BlockSpec(memory_space=pltpu.SMEM)
HB = pl.BlockSpec(memory_space=pltpu.HBM)
GROUP = 8
PAIRS = 96
PART = 32
REST = PAIRS - PART
TALL = 80
EARLY = 2 * ROWS


def parts_of(table):
    high = table.astype(ml_dtypes.bfloat16)
    low = (table - high.astype(np.float64)).astype(ml_dtypes.bfloat16)
    return high, low


@functools.cache
def tables():
    c = np.arange(NY)
    wave = 32 * (c // 64) + c % 32
    is_sine = (c % 64) >= 32
    wave[32] = NY // 2
    is_sine[32] = False
    angle = TWO_PI / NY * ((wave[:, None] * np.arange(NY)[None, :]) % NY)
    norm = np.where((wave == 0) | (wave == NY // 2), 1.0 / NY, 2.0 / NY) ** 0.5
    basis_y = np.where(is_sine[:, None], np.sin(angle), np.cos(angle)) * norm[:, None]
    r = np.arange(HALF)
    m = r % 256
    even = 2 * m
    even[256] = NX // 2
    odd = 2 * m + 1
    wave = np.concatenate([even, odd])
    is_sine = np.concatenate([r > 256, r >= 256])
    angle = TWO_PI / NX * ((np.arange(NX)[:, None] * wave[None, :]) % NX)
    norm = np.where((wave == 0) | (wave == NX // 2), 1.0 / NX, 2.0 / NX) ** 0.5
    basis_x = np.where(is_sine[None, :], np.sin(angle), np.cos(angle)) * norm[None, :]
    n = np.arange(HALF)
    order_gz = 32 * (n % 16) + 4 * (n // 64) + n // 16 % 4
    rows = (np.arange(NX + ROWS) - 16) % NX
    yh, yl = parts_of(basis_y)
    xh, xl = parts_of(basis_x[order_gz])
    return dict(
        y=np.stack([yh, yl]),
        x=np.stack([xh[:, :HALF], xh[:, HALF:], xl[:, :HALF], xl[:, HALF:]]),
        own=np.concatenate(parts_of(basis_x[rows]), axis=1),
    )


def split(value):
    high = value.astype(BF16)
    return high, (value - high.astype(F32)).astype(BF16)


def dot(lhs, rhs, dims):
    return lax.dot_general(lhs, rhs, dims, preferred_element_type=F32)


def data_by_table(value, high, low, dims):
    count = value.shape[0]
    vh, vl = split(value)
    both = dot(jnp.concatenate([vh, vl], 0), high, dims)
    return both[:count] + both[count:] + dot(vh, low, dims)


def table_by_data(high, low, value):
    count = value.shape[0]
    vh, vl = split(value)
    both = dot(high, jnp.concatenate([vh, vl], 0), NT)
    return both[:, :count] + both[:, count:] + dot(low, vh, NT)


def wave_squares(ids_ref):
    share = ids_ref[1]
    c = lax.broadcasted_iota(jnp.int32, (64, NX), 0)
    r = lax.broadcasted_iota(jnp.int32, (64, NX), 1)
    ky = 32 * share + c % 32
    ky = jnp.where((share == 0) & (c == 32), NY // 2, ky)
    m = r % 256
    kx = jnp.where(r == 256, NX // 2, jnp.where(r < HALF, 2 * m, 2 * m + 1))
    kx = kx.astype(F32) * (TWO_PI / NX)
    ky = ky.astype(F32) * (TWO_PI / NY)
    return kx, ky, kx * kx + ky * ky


def to_waves(sums, gaps, x_ref):
    even = data_by_table(sums, x_ref[0], x_ref[2], NN)
    odd = data_by_table(gaps, x_ref[1], x_ref[3], NN)
    return jnp.concatenate([even, odd], 1)


def low_lanes(shape):
    return lax.broadcasted_iota(jnp.int32, shape, 1) < 64


def folded_waves(got_ref, x_ref):
    sums, gaps = [], []
    mask = low_lanes((64, 128))
    for j in range(4):
        first, second = got_ref[2 * j], got_ref[2 * j + 1]
        first_turned = pltpu.roll(first, 64, 1)
        second_turned = pltpu.roll(second, 64, 1)
        sums.append(jnp.where(mask, first + first_turned, second + second_turned))
        gaps.append(jnp.where(mask, first - first_turned, second_turned - second))
    return to_waves(jnp.concatenate(sums, 1), jnp.concatenate(gaps, 1), x_ref)


def from_waves(waves, x_ref):
    even = table_by_data(x_ref[0], x_ref[2], waves[:, :HALF])
    odd = table_by_data(x_ref[1], x_ref[3], waves[:, HALF:])
    return even + odd, even - odd


def by_share(first, second):
    mask = low_lanes(first.shape)
    return (
        jnp.where(mask, first, pltpu.roll(second, 64, 1)),
        jnp.where(mask, pltpu.roll(first, 64, 1), second),
    )


def fetch(source, buffer, sems, place):
    copy = pltpu.make_async_copy(source, buffer, sems.at[place])
    copy.start()
    return copy


def wait_all(copies):
    for copy in copies:
        copy.wait()


def start_kernel(
    ids_ref, phis_hbm, eta_hbm, y_hbm, out_ref, phis_ref, eta_ref, table_ref, block_ref, all_ref,
    sems, out_sems,
):
    first = pl.multiple_of(64 * ids_ref[1], 64)
    rows = pl.multiple_of(8 * (ids_ref[1] // 2), 8)
    copies = [
        fetch(y_hbm.at[:, pl.ds(first, 64), :], table_ref, sems, 0),
        fetch(phis_hbm, phis_ref, sems, 1),
        fetch(eta_hbm.at[pl.ds(rows, 8), :], eta_ref, sems, 2),
    ]
    wait_all(copies)
    coefs = data_by_table(phis_ref[...], table_ref[0], table_ref[1], NT)
    eta = eta_ref[...]
    eta = jnp.where(ids_ref[1] % 2 == 0, eta[:4], eta[4:])
    block_ref[:16] = jnp.concatenate([coefs[:16], coefs[16:]], 1)
    for j in range(4):
        block_ref[16 + 4 * j : 20 + 4 * j] = eta[:, 128 * j : 128 * j + 128]
    all_ref[...] = jnp.broadcast_to(block_ref[...][None], all_ref.shape)
    wait_all([
        fetch(all_ref.at[pl.ds(8 * k, 8)], out_ref.at[pl.ds(8 * k, 8)], out_sems, k)
        for k in range(4)
    ])


def first_kernel(
    ids_ref, got_ref, x_ref, wide_hbm, out_hbm, waves_hbm, out_ref, waves_ref, sems
):
    kx, ky, squares = wave_squares(ids_ref)
    size = jnp.sqrt(squares)
    got = [
        got_ref[pl.ds(512 * half + r, 16, stride=32), :] for half in range(2) for r in range(16)
    ]
    turned = [jnp.concatenate(got[8 * j : 8 * j + 8], 0).T for j in range(4)]
    first, second = jnp.concatenate(turned[:2], 1), jnp.concatenate(turned[2:], 1)
    sums, gaps = first + second, first - second
    sums = jnp.concatenate([sums[:64], sums[64:]], 1)
    gaps = jnp.concatenate([gaps[:64], gaps[64:]], 1)
    waves = to_waves(sums, gaps, x_ref)
    waves_ref[...] = waves
    copies = [fetch(waves_ref, waves_hbm, sems, 8)]
    both = jnp.concatenate([size * waves, squares * waves], 0)
    top, bottom = from_waves(both, x_ref)
    for s in range(8):
        out_ref[s, :64] = top[64 * s : 64 * s + 64]
        out_ref[s, 64:] = bottom[64 * s : 64 * s + 64]
        copies.append(fetch(out_ref.at[s], out_hbm.at[s], sems, s))
    wait_all(copies)


def second_kernel(
    got_ref, gathered_ref, y_ref, below_hbm, above_hbm, out_hbm, eta_hbm, curve_hbm, token_ref,
    out_ref, eta_ref, curve_ref, sems,
):
    pairs = [by_share(got_ref[2 * j], got_ref[2 * j + 1]) for j in range(4)]
    first = jnp.concatenate([p[0] for p in pairs], 1)
    second = jnp.concatenate([p[1] for p in pairs], 1)
    fields = data_by_table(jnp.concatenate([first, second], 0), y_ref[0], y_ref[1], NN)
    columns = []
    for j in range(4):
        block = [
            gathered_ref[pl.ds(512 * half + 16 + 4 * j + q, 16, stride=32), :]
            for half in range(2)
            for q in range(4)
        ]
        columns.append(jnp.concatenate(block, 0))
    eta = jnp.concatenate(columns, 1)
    eta_ref[...] = eta
    curve_ref[...] = 0.5 * eta * fields[128:]
    copies = [fetch(eta_ref, eta_hbm, sems, 8), fetch(curve_ref, curve_hbm, sems, 9)]
    waves = table_by_data(y_ref[0], y_ref[1], -eta * fields[:128])
    token_ref[...] = waves[:8, :128]
    for s in range(8):
        out_ref[s] = waves[64 * s : 64 * s + 64]
        copies.append(fetch(out_ref.at[s], out_hbm.at[s], sems, s))
    wait_all(copies)


def third_kernel(
    ids_ref, got_ref, x_ref, token_ref, out_hbm, waves_hbm, next_ref, out_ref, waves_ref, sems
):
    next_ref[...] = token_ref[...]
    kx, ky, squares = wave_squares(ids_ref)
    size = jnp.sqrt(squares)
    waves = folded_waves(got_ref, x_ref)
    waves_ref[...] = waves
    copies = [fetch(waves_ref, waves_hbm, sems, 8)]
    top, bottom = from_waves(size * waves, x_ref)
    both = jnp.concatenate([top, bottom], 1)
    for s in range(8):
        out_ref[s] = both[64 * s : 64 * s + 64]
        copies.append(fetch(out_ref.at[s], out_hbm.at[s], sems, s))
    wait_all(copies)


def fourth_kernel(
    got_ref, eta_hbm, curve_hbm, y_ref, token_ref, out_hbm, next_ref, out_ref, eta_ref, curve_ref, sems
):
    next_ref[...] = token_ref[...]
    copies = [fetch(eta_hbm, eta_ref, sems, 8), fetch(curve_hbm, curve_ref, sems, 9)]
    pairs = [by_share(got_ref[2 * j], got_ref[2 * j + 1]) for j in range(4)]
    coefs = jnp.concatenate(
        [jnp.concatenate([p[half] for p in pairs], 1) for half in range(2)], 0
    )
    field = data_by_table(coefs, y_ref[0], y_ref[1], NN)
    wait_all(copies)
    waves = table_by_data(y_ref[0], y_ref[1], -eta_ref[...] * (field + curve_ref[...]))
    copies = []
    for s in range(8):
        out_ref[s] = waves[64 * s : 64 * s + 64]
        copies.append(fetch(out_ref.at[s], out_hbm.at[s], sems, s))
    wait_all(copies)


def own_fields(own_ref, fields):
    fh, fl = split(fields)
    oh, ol = own_ref[:, :NX], own_ref[:, NX:]
    return dot(oh, fh, NT) + dot(oh, fl, NT) + dot(ol, fh, NT)


def early_kernel(
    ids_ref, own_hbm, first_hbm, second_hbm, token_ref, out_hbm,
    own_ref, first_ref, second_ref, out_ref, sems,
):
    start = pl.multiple_of(32 * ids_ref[0], 32)
    copies = [
        fetch(first_hbm, first_ref, sems, 1),
        fetch(second_hbm, second_ref, sems, 2),
        fetch(own_hbm.at[pl.ds(start, TALL), :], own_ref, sems, 0),
    ]
    kx, ky, squares = wave_squares(ids_ref)
    size = jnp.sqrt(squares)
    wait_all(copies)
    first = first_ref[...]
    both = first + second_ref[...]
    blocks = []
    for part in (0, HALF):
        speed = kx[:, part : part + 256]
        blocks.append(speed * first[:, part + 256 : part + HALF])
        blocks.append(-speed * first[:, part : part + 256])
    slope_x = jnp.concatenate(blocks, 1)
    speed = ky[:32]
    slope_y = jnp.concatenate([speed * first[32:], -speed * first[:32]], 0)
    rows = own_fields(
        own_ref,
        jnp.concatenate([squares * both, size * squares * first, slope_x, slope_y], 0),
    )
    out_ref[:ROWS] = rows[:ROWS, :128]
    out_ref[ROWS:] = rows[:ROWS, 128:]
    fetch(out_ref, out_hbm, sems, 3).wait()


def fifth_kernel(
    ids_ref, got_ref, x_ref, own_hbm, first_hbm, second_hbm, early_hbm, out_hbm,
    own_ref, out_ref, first_ref, second_ref, sems,
):
    start = pl.multiple_of(32 * ids_ref[0], 32)
    copies = [
        fetch(first_hbm, first_ref, sems, 1),
        fetch(second_hbm, second_ref, sems, 2),
        fetch(own_hbm.at[pl.ds(start, TALL), :], own_ref, sems, 0),
        fetch(early_hbm, out_ref.at[:EARLY], sems, 4),
    ]
    kx, ky, squares = wave_squares(ids_ref)
    size = jnp.sqrt(squares)
    third = folded_waves(got_ref, x_ref)
    wait_all(copies[:3])
    rows = own_fields(own_ref, size * (first_ref[...] + second_ref[...] + third))
    out_ref[EARLY:] = jnp.concatenate([rows[: TALL // 2], rows[TALL // 2 :]], 1)
    wait_all(copies[3:])
    fetch(out_ref, out_hbm, sems, 3).wait()


def own_rows(values):
    pieces = []
    for cx in (1, 2):
        for cy in range(4):
            first = 16 * cx + 4 * cy + 1
            pieces.append(values[first : first + 2])
    return jnp.concatenate(pieces, 0)


def live_mass(ids_ref, mass):
    cell = lax.broadcasted_iota(jnp.int32, (64, 128), 0)
    at_x = 2 * ids_ref[0] - 1 + cell // 16
    at_z = 2 * ids_ref[1] - 1 + cell % 4
    inside = (at_x >= 0) & (at_x < 64) & (at_z >= 0) & (at_z < 16)
    return jnp.where(inside, mass, 0.0)


def pack_kernel(
    count_ref, parts_hbm, own_hbm, low_hbm, high_hbm, parts_ref, own_ref, low_ref, high_ref, sems
):
    fetch(parts_hbm, parts_ref, sems, 3).wait()
    lane = lax.broadcasted_iota(jnp.int32, (2, 128), 1)
    row = lax.broadcasted_iota(jnp.int32, (2, 128), 0)
    for i in range(8):
        for cx in range(2):
            for cy in range(4):
                value = parts_ref[i, cx, cy]
                if i == 7:
                    live = jnp.where(row == 0, count_ref[cx, cy, 0], count_ref[cx, cy, 1])
                    value = jnp.where(lane < live, value, 0.0)
                at = 8 * i + 4 * cx + cy
                own_ref[2 * at : 2 * at + 2] = value
                low_ref[at : at + 1] = value[:1]
                high_ref[at : at + 1] = value[1:]
    wait_all([
        fetch(low_ref, low_hbm, sems, 0),
        fetch(high_ref, high_hbm, sems, 1),
        fetch(own_ref, own_hbm, sems, 2),
    ])


def extend_kernel(
    below_hbm, own_hbm, above_hbm, eta_hbm, wide_hbm, up_hbm, down_hbm,
    below_ref, own_ref, above_ref, eta_ref, wide_ref, up_ref, down_ref, sems,
):
    wait_all([
        fetch(below_hbm, below_ref, sems, 3),
        fetch(own_hbm, own_ref, sems, 4),
        fetch(above_hbm, above_ref, sems, 5),
        fetch(eta_hbm, eta_ref, sems, 6),
    ])
    for i in range(8):
        wide_ref[pl.ds(32 * i, 8, stride=4), :] = below_ref[8 * i : 8 * i + 8]
        wide_ref[pl.ds(32 * i + 1, 8, stride=4), :] = own_ref[pl.ds(16 * i, 8, stride=2), :]
        wide_ref[pl.ds(32 * i + 2, 8, stride=4), :] = own_ref[pl.ds(16 * i + 1, 8, stride=2), :]
        wide_ref[pl.ds(32 * i + 3, 8, stride=4), :] = above_ref[8 * i : 8 * i + 8]
    for i in range(8):
        down_ref[16 * i : 16 * i + 16] = wide_ref[32 * i : 32 * i + 16]
        up_ref[16 * i : 16 * i + 16] = wide_ref[32 * i + 16 : 32 * i + 32]
    for j in range(4):
        up_ref[128 + 16 * j : 144 + 16 * j] = eta_ref[16:, 128 * j : 128 * j + 128]
        down_ref[128 + 24 * j : 152 + 24 * j] = eta_ref[:24, 128 * j : 128 * j + 128]
    wait_all([
        fetch(up_ref, up_hbm, sems, 0),
        fetch(down_ref, down_hbm, sems, 1),
        fetch(wide_ref, wide_hbm, sems, 2),
    ])


def spread_own(values, out_ref):
    columns = jnp.concatenate([own_rows(v) for v in values], 0)
    missing = 128 - columns.shape[0]
    if missing:
        columns = jnp.concatenate([columns, jnp.zeros((missing, 128), F32)], 0)
    columns = columns.T
    for i in range(len(values)):
        for o in range(16):
            k = 16 * i + o
            out_ref[o, i] = jnp.broadcast_to(columns[:, k : k + 1], (128, 128))


def reach_groups(count_ref, part):
    used = jnp.clip(count_ref[0] - part * PART, 0, REST if part else PART)
    return (used + GROUP - 1) // GROUP


def reach_copy(source, target, sems, group):
    return pltpu.make_async_copy(source, target, sems.at[group])


def span_of(ref, group):
    return ref.at[pl.ds(pl.multiple_of(group * GROUP, GROUP), GROUP)]


def reach_channels(ids_ref, cells_ref, chan_ref):
    parts = [cells_ref[64 * i : 64 * i + 64] for i in (0, 1, 2, 6, 7)]
    mass = live_mass(ids_ref, parts[4])
    for i in range(3):
        chan_ref[i] = 0.5 * parts[i]
    chan_ref[3] = parts[3]
    chan_ref[4] = (2.0 * KERNEL_COEF) * mass
    chan_ref[5] = (-2.0 * KERNEL_COEF) * (mass / parts[3])


def reach_pairs(
    part, pairs_ref, count_ref, chan_ref, place_ref, density_ref,
    reach_ref, reach_hbm, sum_ref, reach_sems,
):
    def add_pair(t, carry):
        o = pairs_ref[0, t]
        cell = pairs_ref[1, t]
        place = [chan_ref[i, pl.ds(cell, 1), :] for i in range(3)]
        density, weight, volume = [chan_ref[i, pl.ds(cell, 1), :] for i in range(3, 6)]
        for piece in range(4):
            span = pl.ds(32 * piece, 32)
            gap_x = place_ref[o, 0, span, :] - place[0]
            gap_y = place_ref[o, 1, span, :] - place[1]
            gap_z = place_ref[o, 2, span, :] - place[2]
            square = gap_x * gap_x + gap_y * gap_y + gap_z * gap_z
            reach = jnp.maximum(1.0 - square * lax.rsqrt(jnp.maximum(square, 1e-30)), 0.0)
            reach = reach * reach * reach
            reach_ref[t - part * PART, span, :] = reach * weight
            sum_ref[o, span, :] += reach * ((density - density_ref[o, 0, span, :]) * volume)
        return carry

    def add_group(g, carry):
        start = part * PART + GROUP * g
        stop = jnp.minimum(start + GROUP, count_ref[0])
        lax.fori_loop(start, stop, add_pair, 0)
        reach_copy(span_of(reach_ref, g), span_of(reach_hbm, g), reach_sems, g).start()
        return carry

    lax.fori_loop(0, reach_groups(count_ref, part), add_group, 0)


def reach_end(part, count_ref, reach_ref, reach_hbm, reach_sems):
    def wait_group(g, carry):
        reach_copy(span_of(reach_ref, g), span_of(reach_hbm, g), reach_sems, g).wait()
        return carry

    lax.fori_loop(0, reach_groups(count_ref, part), wait_group, 0)


def reach_kernel(
    ids_ref, pairs_ref, count_ref, wide_hbm, before_hbm, after_hbm, token_ref,
    reach_hbm, place_hbm, density_hbm, sum_hbm, cells_hbm, done_ref,
    wide_ref, before_ref, after_ref, reach_ref, place_ref, density_ref, sum_ref, cells_ref,
    chan_ref, sems, reach_sems,
):
    copies = [
        fetch(wide_hbm, wide_ref, sems, 3),
        fetch(before_hbm.at[pl.ds(0, 128), :], before_ref, sems, 4),
        fetch(after_hbm.at[pl.ds(0, 128), :], after_ref, sems, 5),
    ]
    sum_ref[...] = jnp.zeros_like(sum_ref)
    done_ref[...] = token_ref[...]
    wait_all(copies)
    for i in range(8):
        cells_ref[64 * i : 64 * i + 16] = before_ref[16 * i : 16 * i + 16]
        cells_ref[64 * i + 16 : 64 * i + 48] = wide_ref[32 * i : 32 * i + 32]
        cells_ref[64 * i + 48 : 64 * i + 64] = after_ref[16 * i : 16 * i + 16]
    copies = [fetch(cells_ref, cells_hbm, sems, 2)]
    reach_channels(ids_ref, cells_ref, chan_ref)
    spread_own([chan_ref[i] for i in range(3)], place_ref)
    copies.append(fetch(place_ref, place_hbm, sems, 0))
    spread_own([chan_ref[3]], density_ref)
    copies.append(fetch(density_ref, density_hbm, sems, 6))
    reach_pairs(
        0, pairs_ref, count_ref, chan_ref, place_ref, density_ref,
        reach_ref, reach_hbm, sum_ref, reach_sems,
    )
    copies.append(fetch(sum_ref, sum_hbm, sems, 1))
    reach_end(0, count_ref, reach_ref, reach_hbm, reach_sems)
    wait_all(copies)


def reach_rest_kernel(
    ids_ref, pairs_ref, count_ref, place_hbm, density_hbm, before_hbm, cells_hbm, token_ref,
    reach_hbm, sum_hbm, done_ref,
    reach_ref, place_ref, density_ref, sum_ref, cells_ref, chan_ref, sems, reach_sems,
):
    copies = [
        fetch(cells_hbm, cells_ref, sems, 0),
        fetch(place_hbm, place_ref, sems, 1),
        fetch(density_hbm, density_ref, sems, 2),
        fetch(before_hbm, sum_ref, sems, 3),
    ]
    done_ref[...] = token_ref[...]
    wait_all(copies[:1])
    reach_channels(ids_ref, cells_ref, chan_ref)
    wait_all(copies[1:])
    reach_pairs(
        1, pairs_ref, count_ref, chan_ref, place_ref, density_ref,
        reach_ref, reach_hbm, sum_ref, reach_sems,
    )
    last_copy = fetch(sum_ref, sum_hbm, sems, 4)
    reach_end(1, count_ref, reach_ref, reach_hbm, reach_sems)
    last_copy.wait()


def last_kernel(ids_ref, pairs_ref, count_ref, *refs):
    blocks_hbm, refs = refs[:8], refs[8:]
    (
        before_hbm, eta_hbm, after_hbm, cells_hbm, y_ref, reach_hbm, rest_hbm, place_hbm, sum_hbm, surface_ref, rate_ref,
        blocks, eta_ref, cells_ref, reach_ref, place_ref, sum_ref,
        coef_ref, field_ref, target_ref, speed_ref, half_ref, own_ref, sems, reach_sems,
    ) = refs
    block_copies = [fetch(blocks_hbm[i], blocks.at[i], sems, 4 + i) for i in range(8)]
    copies = [
        fetch(eta_hbm, eta_ref.at[pl.ds(16, 32), :], sems, 0),
        fetch(cells_hbm, cells_ref, sems, 1),
    ]

    for j in range(4):
        lanes = pl.ds(128 * j, 128)
        from_before = before_hbm.at[pl.ds(128 + 16 * j, 16), :]
        from_after = after_hbm.at[pl.ds(128 + 24 * j, 24), :]
        block_copies.append(fetch(from_before, eta_ref.at[pl.ds(0, 16), lanes], sems, 12 + j))
        block_copies.append(fetch(from_after, eta_ref.at[pl.ds(48, 24), lanes], sems, 16 + j))

    def start_group(g, carry):
        reach_copy(span_of(reach_hbm, g), span_of(reach_ref, g), reach_sems, g).start()
        return carry

    def start_rest(g, carry):
        at = g + PART // GROUP
        reach_copy(span_of(rest_hbm, g), span_of(reach_ref, at), reach_sems, at).start()
        return carry

    def wait_group(g, carry):
        reach_copy(span_of(reach_hbm, g), span_of(reach_ref, g), reach_sems, g).wait()
        return carry

    def wait_rest(g, carry):
        at = g + PART // GROUP
        reach_copy(span_of(rest_hbm, g), span_of(reach_ref, at), reach_sems, at).wait()
        return carry

    groups, rest_groups = reach_groups(count_ref, 0), reach_groups(count_ref, 1)
    slab = ids_ref[0]
    layer = ids_ref[1]
    wait_all(block_copies)
    copies += [fetch(place_hbm, place_ref, sems, 2), fetch(sum_hbm, sum_ref, sems, 3)]
    lax.fori_loop(0, groups, start_group, 0)
    lax.fori_loop(0, rest_groups, start_rest, 0)
    for step in range(4):
        share = (layer // 2 + 4 - step) % 4
        lanes = pl.ds(pl.multiple_of(128 * share, 128), 128)
        mine, theirs = blocks.at[step], blocks.at[4 + step]
        for at, size in ((0, ROWS), (ROWS, ROWS), (EARLY, TALL // 2)):
            here = mine[at : at + size, :]
            there = theirs[at : at + size, :]
            first = jnp.where(layer % 2 == 0, here, there)
            second = jnp.where(layer % 2 == 0, there, here)
            first, second = by_share(first, second)
            coef_ref[2 * at : 2 * at + size, lanes] = first
            coef_ref[2 * at + size : 2 * at + 2 * size, lanes] = second
    fields = data_by_table(coef_ref[...], y_ref[0], y_ref[1], NN)
    wait_all(copies[:2])
    parts = [cells_ref[64 * i : 64 * i + 64] for i in range(8)]
    eta = eta_ref[...]
    vertical = (
        fields[4 * ROWS : 5 * ROWS]
        + eta * fields[:ROWS]
        + 0.5 * eta * eta * fields[ROWS : 2 * ROWS]
    )
    surface_ref[...] = vertical[16:48]
    sampled = (fields[2 * ROWS : 3 * ROWS], fields[3 * ROWS : 4 * ROWS], vertical)
    for f in range(3):
        field_ref[2 * f] = sampled[f]
        field_ref[2 * f + 1] = pltpu.roll(sampled[f], NY - 1, 1) - sampled[f]
    row_ids = lax.broadcasted_iota(jnp.int32, (24, 128), 0).astype(F32)

    def sample(cx, carry):
        first_row = pl.multiple_of(16 * cx, 16)
        origin = (32 * slab - 16 + 16 * cx).astype(F32)
        found = [[], [], []]
        place_x = cells_ref[pl.ds(first_row, 16), :] * 8.0 - origin
        place_y = cells_ref[pl.ds(pl.multiple_of(first_row + 64, 16), 16), :] * 64.0
        for cy in range(4):
            for cz in range(4):
                cell = 4 * cy + cz
                along = place_y[cell : cell + 1] - 128.0 * cy
                index = jnp.clip(along.astype(jnp.int32), 0, 127)
                part = along - index.astype(F32)
                index = jnp.broadcast_to(index, (24, 128))
                weight = jnp.maximum(0.0, 1.0 - jnp.abs(place_x[cell : cell + 1] - row_ids))
                weight_next = weight * part
                for f in range(3):
                    here = field_ref[2 * f, pl.ds(first_row, 24), 128 * cy : 128 * cy + 128]
                    step = field_ref[2 * f + 1, pl.ds(first_row, 24), 128 * cy : 128 * cy + 128]
                    here = jnp.take_along_axis(here, index, axis=1)
                    step = jnp.take_along_axis(step, index, axis=1)
                    found[f].append(
                        jnp.sum(weight * here + weight_next * step, axis=0, keepdims=True)
                    )
        for f in range(3):
            target_ref[f, pl.ds(first_row, 16), :] = jnp.concatenate(found[f], 0)
        return carry

    lax.fori_loop(0, 4, sample, 0)
    depth = jnp.exp((parts[2] - 32.0) * (1.0 / 32.0))
    close = jnp.clip(1.0 - parts[0] * (1.0 / 256.0), 0.0, 1.0)
    close = close * close
    for i in range(3):
        half_ref[i] = 0.5 * parts[i]
        speed = parts[3 + i]
        speed_ref[i] = speed + close * (target_ref[i] * depth - speed)
    spread_own([speed_ref[i] for i in range(3)], own_ref)
    wait_all(copies[2:])

    def add_pair(t, carry):
        o = pairs_ref[0, t]
        cell = pairs_ref[1, t]
        place = [half_ref[i, pl.ds(cell, 1), :] for i in range(3)]
        speed = [speed_ref[i, pl.ds(cell, 1), :] for i in range(3)]
        for piece in range(4):
            span = pl.ds(32 * piece, 32)
            approach = 0.0
            for i in range(3):
                approach = approach + (own_ref[o, i, span, :] - speed[i]) * (
                    place_ref[o, i, span, :] - place[i]
                )
            sum_ref[o, span, :] += reach_ref[t, span, :] * approach
        return carry

    def add_group(g, carry):
        wait_group(g, 0)
        stop = jnp.minimum(GROUP * g + GROUP, count_ref[0])
        return lax.fori_loop(GROUP * g, stop, add_pair, carry)

    def add_rest(g, carry):
        wait_rest(g, 0)
        start = PART + GROUP * g
        stop = jnp.minimum(start + GROUP, count_ref[0])
        return lax.fori_loop(start, stop, add_pair, carry)

    lax.fori_loop(0, groups, add_group, 0)
    lax.fori_loop(0, rest_groups, add_rest, 0)
    ones = jnp.ones((8, 384), BF16)
    rates = []
    for o in range(16):
        total = sum_ref[o]
        high, rest = split(total)
        middle, last = split(total - high.astype(F32))
        rates.append(dot(ones, jnp.concatenate([high, middle, last], 1), NT)[:1])
    mass = own_rows(parts[7])
    rate_ref[...] = jnp.where(mass > 0.0, jnp.concatenate(rates, 0), 0.0)


def call(kernel, args, kinds, outs, name, vmem, scratch):
    specs = dict(S=SM, H=HB, V=VM)
    args = [
        pltpu.with_memory_space_constraint(a, pltpu.HBM) if k == "H" else a
        for a, k in zip(args, kinds, strict=True)
    ]
    return pl.pallas_call(
        kernel,
        out_shape=[
            pltpu.HBM(s, F32) if k == "H" else jax.ShapeDtypeStruct(s, F32) for s, k in outs
        ],
        in_specs=[specs[k] for k in kinds],
        out_specs=[specs[k] for _, k in outs],
        scratch_shapes=[pltpu.VMEM(s, F32) if isinstance(s, tuple) else s for s in scratch],
        compiler_params=pltpu.CompilerParams(vmem_limit_bytes=vmem * 1024 * 1024),
        name=name,
    )(*args)


def dma_sems(count):
    return pltpu.SemaphoreType.DMA((count,))


def passed(values, axis, by):
    size = lax.axis_size(axis)
    return lax.ppermute(values, axis, [(i, (i + by) % size) for i in range(size)])


def swap(block, axis):
    return lax.all_to_all(block, axis, split_axis=0, concat_axis=0, tiled=True)


def per_device(eta, phis, particles, cell_count, pair_cells, pair_count):
    slab = lax.axis_index("gx")
    layer = lax.axis_index("gz")
    ids = jnp.stack([slab, layer]).astype(jnp.int32)
    table = tables()
    y = jnp.asarray(table["y"])
    x = jnp.asarray(table["x"])
    own = jnp.asarray(table["own"])

    half_layers = lax.axis_size("gz") // 2

    own_cells, low, high = call(
        pack_kernel, (cell_count, particles), "SH",
        [((128, 128), "H"), ((64, 128), "H"), ((64, 128), "H")], "pack", 4,
        [(8, 2, 4, 2, 128), (128, 128), (64, 128), (64, 128), dma_sems(4)],
    )
    below = passed(high, "gz", 1)
    above = passed(low, "gz", -1)
    wide, up, down = call(
        extend_kernel, (below, own_cells, above, eta), "HHHH",
        [((256, 128), "H"), ((192, 128), "H"), ((224, 128), "H")], "extend", 4,
        [
            (64, 128),
            (128, 128),
            (64, 128),
            (32, NY),
            (256, 128),
            (192, 128),
            (224, 128),
            dma_sems(7),
        ],
    )
    cells_before = passed(up, "gx", 1)
    cells_after = passed(down, "gx", -1)
    pairs = pair_cells.reshape(2, 96)
    count = pair_count.reshape(1)

    (block,) = call(
        start_kernel, (ids, phis, eta, y), "SHHH", [((32, 32, 128), "H")], "start", 4,
        [
            (32, NY),
            (8, NY),
            pltpu.VMEM((2, 64, NY), BF16),
            (32, 128),
            (32, 32, 128),
            dma_sems(3),
            dma_sems(4),
        ],
    )
    gathered = swap(block, "gx").reshape(1024, 128)
    block, first = call(
        first_kernel,
        (ids, gathered, x, wide),
        "SVVH",
        [((8, 128, 128), "H"), ((64, NX), "H")],
        "first",
        8,
        [(8, 128, 128), (64, NX), dma_sems(9)],
    )
    got = swap(block, "gz")
    block, eta_part, curve, token = call(
        second_kernel,
        (got, gathered, y, cells_before, cells_after),
        "VVVHH",
        [((8, 64, 128), "H"), ((128, NY), "H"), ((128, NY), "H"), ((8, 128), "V")],
        "second",
        8,
        [(8, 64, 128), (128, NY), (128, NY), dma_sems(10)],
    )
    got = swap(block, "gz")
    reach, place, density, before, cells, token = call(
        reach_kernel,
        (ids, pairs, count, wide, cells_before, cells_after, token),
        "SSSHHHV",
        [
            ((PART, 128, 128), "H"),
            ((16, 3, 128, 128), "H"),
            ((16, 1, 128, 128), "H"),
            ((16, 128, 128), "H"),
            ((512, 128), "H"),
            ((8, 128), "V"),
        ],
        "reach",
        16,
        [
            (256, 128),
            (128, 128),
            (128, 128),
            (PART, 128, 128),
            (16, 3, 128, 128),
            (16, 1, 128, 128),
            (16, 128, 128),
            (512, 128),
            (6, 64, 128),
            dma_sems(7),
            dma_sems(PART // GROUP),
        ],
    )
    block, second, token = call(
        third_kernel,
        (ids, got, x, token),
        "SVVV",
        [((8, 64, 128), "H"), ((64, NX), "H"), ((8, 128), "V")],
        "third",
        8,
        [(8, 64, 128), (64, NX), dma_sems(9)],
    )
    got = swap(block, "gz")
    rest, before, token = call(
        reach_rest_kernel,
        (ids, pairs, count, place, density, before, cells, token),
        "SSSHHHHV",
        [((REST, 128, 128), "H"), ((16, 128, 128), "H"), ((8, 128), "V")],
        "rest",
        16,
        [
            (REST, 128, 128),
            (16, 3, 128, 128),
            (16, 1, 128, 128),
            (16, 128, 128),
            (512, 128),
            (6, 64, 128),
            dma_sems(5),
            dma_sems(REST // GROUP),
        ],
    )
    block, token = call(
        fourth_kernel,
        (got, eta_part, curve, y, token),
        "VHHVV",
        [((8, 64, 128), "H"), ((8, 128), "V")],
        "fourth",
        8,
        [(8, 64, 128), (128, NY), (128, NY), dma_sems(10)],
    )
    got = swap(block, "gz")
    (early,) = call(
        early_kernel,
        (ids, own, first, second, token),
        "SHHHV",
        [((EARLY, 128), "H")],
        "early",
        8,
        [pltpu.VMEM((TALL, 2 * NX), BF16), (64, NX), (64, NX), (EARLY, 128), dma_sems(4)],
    )
    (block,) = call(
        fifth_kernel,
        (ids, got, x, own, first, second, early),
        "SVVHHHH",
        [((EARLY + TALL // 2, 128), "H")],
        "fifth",
        8,
        [
            pltpu.VMEM((TALL, 2 * NX), BF16),
            (EARLY + TALL // 2, 128),
            (64, NX),
            (64, NX),
            dma_sems(5),
        ],
    )
    along = [block] + [
        lax.ppermute(
            block,
            "gz",
            [
                (2 * i + core, 2 * ((i + step) % half_layers) + core)
                for i in range(half_layers)
                for core in range(2)
            ],
        )
        for step in range(1, half_layers)
    ]
    across = [
        lax.ppermute(b, "gz", [(i, i ^ 1) for i in range(2 * half_layers)]) for b in along
    ]
    surface, rate = call(
        last_kernel,
        (ids, pairs, count, *along, *across, cells_before, eta, cells_after, cells, y, reach, rest, place, before),
        "SSS" + "H" * 12 + "VHHHH",
        [((32, NY), "V"), ((16, 128), "V")],
        "last",
        24,
        [
            (8, EARLY + TALL // 2, 128),
            (ROWS, NY),
            (512, 128),
            (96, 128, 128),
            (16, 3, 128, 128),
            (16, 128, 128),
            (2 * EARLY + TALL, NY),
            (6, ROWS, NY),
            (3, 64, 128),
            (3, 64, 128),
            (3, 64, 128),
            (16, 3, 128, 128),
            dma_sems(20),
            dma_sems(96 // GROUP),
        ],
    )
    return surface, rate.reshape(2, 4, 2, 128)


def solution(mesh):
    in_specs = (
        P("gx", None),
        P("gx", None),
        P(None, "gx", None, "gz", None),
        P("gx", None, "gz"),
        P("gx", "gz", None, None),
        P("gx", "gz", None),
    )
    out_specs = (P("gx", None), P("gx", None, "gz", None))
    return jax.shard_map(
        per_device, mesh=mesh, in_specs=in_specs, out_specs=out_specs, check_vma=False
    )
```

```python
import functools

import jax
import jax.numpy as jnp
import ml_dtypes
import numpy as np
from jax import lax
from jax.experimental import pallas as pl
from jax.experimental.pallas import tpu as pltpu
from jax.sharding import PartitionSpec as P

TWO_PI = 6.283185307179586
KERNEL_COEF = -5.0 * 21.0 / (16.0 * 3.141592653589793)
NX = 1024
NY = 512
HALF = 512
ROWS = 72
F32 = jnp.float32
BF16 = jnp.bfloat16
NN = (((1,), (0,)), ((), ()))
NT = (((1,), (1,)), ((), ()))
VM = pl.BlockSpec(memory_space=pltpu.VMEM)
SM = pl.BlockSpec(memory_space=pltpu.SMEM)
HB = pl.BlockSpec(memory_space=pltpu.HBM)
GROUP = 8
PAIRS = 96
PART = 32
REST = PAIRS - PART
TALL = 80
EARLY = 2 * ROWS


def parts_of(table):
    high = table.astype(ml_dtypes.bfloat16)
    low = (table - high.astype(np.float64)).astype(ml_dtypes.bfloat16)
    return high, low


@functools.cache
def tables():
    c = np.arange(NY)
    wave = 32 * (c // 64) + c % 32
    is_sine = (c % 64) >= 32
    wave[32] = NY // 2
    is_sine[32] = False
    angle = TWO_PI / NY * ((wave[:, None] * np.arange(NY)[None, :]) % NY)
    norm = np.where((wave == 0) | (wave == NY // 2), 1.0 / NY, 2.0 / NY) ** 0.5
    basis_y = np.where(is_sine[:, None], np.sin(angle), np.cos(angle)) * norm[:, None]
    r = np.arange(HALF)
    m = r % 256
    even = 2 * m
    even[256] = NX // 2
    odd = 2 * m + 1
    wave = np.concatenate([even, odd])
    is_sine = np.concatenate([r > 256, r >= 256])
    angle = TWO_PI / NX * ((np.arange(NX)[:, None] * wave[None, :]) % NX)
    norm = np.where((wave == 0) | (wave == NX // 2), 1.0 / NX, 2.0 / NX) ** 0.5
    basis_x = np.where(is_sine[None, :], np.sin(angle), np.cos(angle)) * norm[None, :]
    n = np.arange(HALF)
    order_gz = 32 * (n % 16) + 4 * (n // 64) + n // 16 % 4
    rows = (np.arange(NX + ROWS) - 16) % NX
    yh, yl = parts_of(basis_y)
    xh, xl = parts_of(basis_x[order_gz])
    return dict(
        y=np.stack([yh, yl]),
        x=np.stack([xh[:, :HALF], xh[:, HALF:], xl[:, :HALF], xl[:, HALF:]]),
        own=np.concatenate(parts_of(basis_x[rows]), axis=1),
    )


def split(value):
    high = value.astype(BF16)
    return high, (value - high.astype(F32)).astype(BF16)


def dot(lhs, rhs, dims):
    return lax.dot_general(lhs, rhs, dims, preferred_element_type=F32)


def data_by_table(value, high, low, dims):
    count = value.shape[0]
    vh, vl = split(value)
    both = dot(jnp.concatenate([vh, vl], 0), high, dims)
    return both[:count] + both[count:] + dot(vh, low, dims)


def table_by_data(high, low, value):
    count = value.shape[0]
    vh, vl = split(value)
    both = dot(high, jnp.concatenate([vh, vl], 0), NT)
    return both[:, :count] + both[:, count:] + dot(low, vh, NT)


def wave_squares(ids_ref):
    share = ids_ref[1]
    c = lax.broadcasted_iota(jnp.int32, (64, NX), 0)
    r = lax.broadcasted_iota(jnp.int32, (64, NX), 1)
    ky = 32 * share + c % 32
    ky = jnp.where((share == 0) & (c == 32), NY // 2, ky)
    m = r % 256
    kx = jnp.where(r == 256, NX // 2, jnp.where(r < HALF, 2 * m, 2 * m + 1))
    kx = kx.astype(F32) * (TWO_PI / NX)
    ky = ky.astype(F32) * (TWO_PI / NY)
    return kx, ky, kx * kx + ky * ky


def to_waves(sums, gaps, x_ref):
    even = data_by_table(sums, x_ref[0], x_ref[2], NN)
    odd = data_by_table(gaps, x_ref[1], x_ref[3], NN)
    return jnp.concatenate([even, odd], 1)


def low_lanes(shape):
    return lax.broadcasted_iota(jnp.int32, shape, 1) < 64


def folded_waves(got_ref, x_ref):
    sums, gaps = [], []
    mask = low_lanes((64, 128))
    for j in range(4):
        first, second = got_ref[2 * j], got_ref[2 * j + 1]
        first_turned = pltpu.roll(first, 64, 1)
        second_turned = pltpu.roll(second, 64, 1)
        sums.append(jnp.where(mask, first + first_turned, second + second_turned))
        gaps.append(jnp.where(mask, first - first_turned, second_turned - second))
    return to_waves(jnp.concatenate(sums, 1), jnp.concatenate(gaps, 1), x_ref)


def from_waves(waves, x_ref):
    even = table_by_data(x_ref[0], x_ref[2], waves[:, :HALF])
    odd = table_by_data(x_ref[1], x_ref[3], waves[:, HALF:])
    return even + odd, even - odd


def by_share(first, second):
    mask = low_lanes(first.shape)
    return (
        jnp.where(mask, first, pltpu.roll(second, 64, 1)),
        jnp.where(mask, pltpu.roll(first, 64, 1), second),
    )


def fetch(source, buffer, sems, place):
    copy = pltpu.make_async_copy(source, buffer, sems.at[place])
    copy.start()
    return copy


def wait_all(copies):
    for copy in copies:
        copy.wait()


def start_kernel(
    ids_ref, phis_hbm, eta_hbm, y_hbm, out_ref, phis_ref, eta_ref, table_ref, block_ref, all_ref,
    sems, out_sems,
):
    first = pl.multiple_of(64 * ids_ref[1], 64)
    rows = pl.multiple_of(8 * (ids_ref[1] // 2), 8)
    copies = [
        fetch(y_hbm.at[:, pl.ds(first, 64), :], table_ref, sems, 0),
        fetch(phis_hbm, phis_ref, sems, 1),
        fetch(eta_hbm.at[pl.ds(rows, 8), :], eta_ref, sems, 2),
    ]
    wait_all(copies)
    coefs = data_by_table(phis_ref[...], table_ref[0], table_ref[1], NT)
    eta = eta_ref[...]
    eta = jnp.where(ids_ref[1] % 2 == 0, eta[:4], eta[4:])
    block_ref[:16] = jnp.concatenate([coefs[:16], coefs[16:]], 1)
    for j in range(4):
        block_ref[16 + 4 * j : 20 + 4 * j] = eta[:, 128 * j : 128 * j + 128]
    all_ref[...] = jnp.broadcast_to(block_ref[...][None], all_ref.shape)
    wait_all([
        fetch(all_ref.at[pl.ds(8 * k, 8)], out_ref.at[pl.ds(8 * k, 8)], out_sems, k)
        for k in range(4)
    ])


def first_kernel(
    ids_ref, got_ref, x_ref, wide_hbm, out_hbm, waves_hbm, out_ref, waves_ref, sems
):
    kx, ky, squares = wave_squares(ids_ref)
    size = jnp.sqrt(squares)
    got = [
        got_ref[pl.ds(512 * half + r, 16, stride=32), :] for half in range(2) for r in range(16)
    ]
    turned = [jnp.concatenate(got[8 * j : 8 * j + 8], 0).T for j in range(4)]
    first, second = jnp.concatenate(turned[:2], 1), jnp.concatenate(turned[2:], 1)
    sums, gaps = first + second, first - second
    sums = jnp.concatenate([sums[:64], sums[64:]], 1)
    gaps = jnp.concatenate([gaps[:64], gaps[64:]], 1)
    waves = to_waves(sums, gaps, x_ref)
    waves_ref[...] = waves
    copies = [fetch(waves_ref, waves_hbm, sems, 8)]
    both = jnp.concatenate([size * waves, squares * waves], 0)
    top, bottom = from_waves(both, x_ref)
    for s in range(8):
        out_ref[s, :64] = top[64 * s : 64 * s + 64]
        out_ref[s, 64:] = bottom[64 * s : 64 * s + 64]
        copies.append(fetch(out_ref.at[s], out_hbm.at[s], sems, s))
    wait_all(copies)


def second_kernel(
    got_ref, gathered_ref, y_ref, below_hbm, above_hbm, out_hbm, eta_hbm, curve_hbm, token_ref,
    out_ref, eta_ref, curve_ref, sems,
):
    pairs = [by_share(got_ref[2 * j], got_ref[2 * j + 1]) for j in range(4)]
    first = jnp.concatenate([p[0] for p in pairs], 1)
    second = jnp.concatenate([p[1] for p in pairs], 1)
    fields = data_by_table(jnp.concatenate([first, second], 0), y_ref[0], y_ref[1], NN)
    columns = []
    for j in range(4):
        block = [
            gathered_ref[pl.ds(512 * half + 16 + 4 * j + q, 16, stride=32), :]
            for half in range(2)
            for q in range(4)
        ]
        columns.append(jnp.concatenate(block, 0))
    eta = jnp.concatenate(columns, 1)
    eta_ref[...] = eta
    curve_ref[...] = 0.5 * eta * fields[128:]
    copies = [fetch(eta_ref, eta_hbm, sems, 8), fetch(curve_ref, curve_hbm, sems, 9)]
    waves = table_by_data(y_ref[0], y_ref[1], -eta * fields[:128])
    token_ref[...] = waves[:8, :128]
    for s in range(8):
        out_ref[s] = waves[64 * s : 64 * s + 64]
        copies.append(fetch(out_ref.at[s], out_hbm.at[s], sems, s))
    wait_all(copies)


def third_kernel(
    ids_ref, got_ref, x_ref, token_ref, out_hbm, waves_hbm, next_ref, out_ref, waves_ref, sems
):
    next_ref[...] = token_ref[...]
    kx, ky, squares = wave_squares(ids_ref)
    size = jnp.sqrt(squares)
    waves = folded_waves(got_ref, x_ref)
    waves_ref[...] = waves
    copies = [fetch(waves_ref, waves_hbm, sems, 8)]
    top, bottom = from_waves(size * waves, x_ref)
    both = jnp.concatenate([top, bottom], 1)
    for s in range(8):
        out_ref[s] = both[64 * s : 64 * s + 64]
        copies.append(fetch(out_ref.at[s], out_hbm.at[s], sems, s))
    wait_all(copies)


def fourth_kernel(
    got_ref, eta_hbm, curve_hbm, y_ref, token_ref, out_hbm, next_ref, out_ref, eta_ref, curve_ref, sems
):
    next_ref[...] = token_ref[...]
    copies = [fetch(eta_hbm, eta_ref, sems, 8), fetch(curve_hbm, curve_ref, sems, 9)]
    pairs = [by_share(got_ref[2 * j], got_ref[2 * j + 1]) for j in range(4)]
    coefs = jnp.concatenate(
        [jnp.concatenate([p[half] for p in pairs], 1) for half in range(2)], 0
    )
    field = data_by_table(coefs, y_ref[0], y_ref[1], NN)
    wait_all(copies)
    waves = table_by_data(y_ref[0], y_ref[1], -eta_ref[...] * (field + curve_ref[...]))
    copies = []
    for s in range(8):
        out_ref[s] = waves[64 * s : 64 * s + 64]
        copies.append(fetch(out_ref.at[s], out_hbm.at[s], sems, s))
    wait_all(copies)


def own_fields(own_ref, fields):
    fh, fl = split(fields)
    oh, ol = own_ref[:, :NX], own_ref[:, NX:]
    return dot(oh, fh, NT) + dot(oh, fl, NT) + dot(ol, fh, NT)


def early_kernel(
    ids_ref, own_hbm, first_hbm, second_hbm, token_ref, out_hbm,
    own_ref, first_ref, second_ref, out_ref, sems,
):
    start = pl.multiple_of(32 * ids_ref[0], 32)
    copies = [
        fetch(first_hbm, first_ref, sems, 1),
        fetch(second_hbm, second_ref, sems, 2),
        fetch(own_hbm.at[pl.ds(start, TALL), :], own_ref, sems, 0),
    ]
    kx, ky, squares = wave_squares(ids_ref)
    size = jnp.sqrt(squares)
    wait_all(copies)
    first = first_ref[...]
    both = first + second_ref[...]
    blocks = []
    for part in (0, HALF):
        speed = kx[:, part : part + 256]
        blocks.append(speed * first[:, part + 256 : part + HALF])
        blocks.append(-speed * first[:, part : part + 256])
    slope_x = jnp.concatenate(blocks, 1)
    speed = ky[:32]
    slope_y = jnp.concatenate([speed * first[32:], -speed * first[:32]], 0)
    rows = own_fields(
        own_ref,
        jnp.concatenate([squares * both, size * squares * first, slope_x, slope_y], 0),
    )
    out_ref[:ROWS] = rows[:ROWS, :128]
    out_ref[ROWS:] = rows[:ROWS, 128:]
    fetch(out_ref, out_hbm, sems, 3).wait()


def fifth_kernel(
    ids_ref, got_ref, x_ref, own_hbm, first_hbm, second_hbm, early_hbm, out_hbm,
    own_ref, out_ref, first_ref, second_ref, sems,
):
    start = pl.multiple_of(32 * ids_ref[0], 32)
    copies = [
        fetch(first_hbm, first_ref, sems, 1),
        fetch(second_hbm, second_ref, sems, 2),
        fetch(own_hbm.at[pl.ds(start, TALL), :], own_ref, sems, 0),
        fetch(early_hbm, out_ref.at[:EARLY], sems, 4),
    ]
    kx, ky, squares = wave_squares(ids_ref)
    size = jnp.sqrt(squares)
    third = folded_waves(got_ref, x_ref)
    wait_all(copies[:3])
    rows = own_fields(own_ref, size * (first_ref[...] + second_ref[...] + third))
    out_ref[EARLY:] = jnp.concatenate([rows[: TALL // 2], rows[TALL // 2 :]], 1)
    wait_all(copies[3:])
    fetch(out_ref, out_hbm, sems, 3).wait()


def own_rows(values):
    pieces = []
    for cx in (1, 2):
        for cy in range(4):
            first = 16 * cx + 4 * cy + 1
            pieces.append(values[first : first + 2])
    return jnp.concatenate(pieces, 0)


def live_mass(ids_ref, mass):
    cell = lax.broadcasted_iota(jnp.int32, (64, 128), 0)
    at_x = 2 * ids_ref[0] - 1 + cell // 16
    at_z = 2 * ids_ref[1] - 1 + cell % 4
    inside = (at_x >= 0) & (at_x < 64) & (at_z >= 0) & (at_z < 16)
    return jnp.where(inside, mass, 0.0)


def pack_kernel(
    count_ref, parts_hbm, own_hbm, low_hbm, high_hbm, parts_ref, own_ref, low_ref, high_ref, sems
):
    fetch(parts_hbm, parts_ref, sems, 3).wait()
    lane = lax.broadcasted_iota(jnp.int32, (2, 128), 1)
    row = lax.broadcasted_iota(jnp.int32, (2, 128), 0)
    for i in range(8):
        for cx in range(2):
            for cy in range(4):
                value = parts_ref[i, cx, cy]
                if i == 7:
                    live = jnp.where(row == 0, count_ref[cx, cy, 0], count_ref[cx, cy, 1])
                    value = jnp.where(lane < live, value, 0.0)
                at = 8 * i + 4 * cx + cy
                own_ref[2 * at : 2 * at + 2] = value
                low_ref[at : at + 1] = value[:1]
                high_ref[at : at + 1] = value[1:]
    wait_all([
        fetch(low_ref, low_hbm, sems, 0),
        fetch(high_ref, high_hbm, sems, 1),
        fetch(own_ref, own_hbm, sems, 2),
    ])


def extend_kernel(
    below_hbm, own_hbm, above_hbm, eta_hbm, wide_hbm, up_hbm, down_hbm,
    below_ref, own_ref, above_ref, eta_ref, wide_ref, up_ref, down_ref, sems,
):
    wait_all([
        fetch(below_hbm, below_ref, sems, 3),
        fetch(own_hbm, own_ref, sems, 4),
        fetch(above_hbm, above_ref, sems, 5),
        fetch(eta_hbm, eta_ref, sems, 6),
    ])
    for i in range(8):
        wide_ref[pl.ds(32 * i, 8, stride=4), :] = below_ref[8 * i : 8 * i + 8]
        wide_ref[pl.ds(32 * i + 1, 8, stride=4), :] = own_ref[pl.ds(16 * i, 8, stride=2), :]
        wide_ref[pl.ds(32 * i + 2, 8, stride=4), :] = own_ref[pl.ds(16 * i + 1, 8, stride=2), :]
        wide_ref[pl.ds(32 * i + 3, 8, stride=4), :] = above_ref[8 * i : 8 * i + 8]
    for i in range(8):
        down_ref[16 * i : 16 * i + 16] = wide_ref[32 * i : 32 * i + 16]
        up_ref[16 * i : 16 * i + 16] = wide_ref[32 * i + 16 : 32 * i + 32]
    for j in range(4):
        up_ref[128 + 16 * j : 144 + 16 * j] = eta_ref[16:, 128 * j : 128 * j + 128]
        down_ref[128 + 24 * j : 152 + 24 * j] = eta_ref[:24, 128 * j : 128 * j + 128]
    wait_all([
        fetch(up_ref, up_hbm, sems, 0),
        fetch(down_ref, down_hbm, sems, 1),
        fetch(wide_ref, wide_hbm, sems, 2),
    ])


def spread_own(values, out_ref):
    columns = jnp.concatenate([own_rows(v) for v in values], 0)
    missing = 128 - columns.shape[0]
    if missing:
        columns = jnp.concatenate([columns, jnp.zeros((missing, 128), F32)], 0)
    columns = columns.T
    for i in range(len(values)):
        for o in range(16):
            k = 16 * i + o
            out_ref[o, i] = jnp.broadcast_to(columns[:, k : k + 1], (128, 128))


def reach_groups(count_ref, part):
    used = jnp.clip(count_ref[0] - part * PART, 0, REST if part else PART)
    return (used + GROUP - 1) // GROUP


def reach_copy(source, target, sems, group):
    return pltpu.make_async_copy(source, target, sems.at[group])


def span_of(ref, group):
    return ref.at[pl.ds(pl.multiple_of(group * GROUP, GROUP), GROUP)]


def reach_channels(ids_ref, cells_ref, chan_ref):
    parts = [cells_ref[64 * i : 64 * i + 64] for i in (0, 1, 2, 6, 7)]
    mass = live_mass(ids_ref, parts[4])
    for i in range(3):
        chan_ref[i] = 0.5 * parts[i]
    chan_ref[3] = parts[3]
    chan_ref[4] = (2.0 * KERNEL_COEF) * mass
    chan_ref[5] = (-2.0 * KERNEL_COEF) * (mass / parts[3])


def reach_pairs(
    part, pairs_ref, count_ref, chan_ref, place_ref, density_ref,
    reach_ref, reach_hbm, sum_ref, reach_sems,
):
    def add_pair(t, carry):
        o = pairs_ref[0, t]
        cell = pairs_ref[1, t]
        place = [chan_ref[i, pl.ds(cell, 1), :] for i in range(3)]
        density, weight, volume = [chan_ref[i, pl.ds(cell, 1), :] for i in range(3, 6)]
        for piece in range(4):
            span = pl.ds(32 * piece, 32)
            gap_x = place_ref[o, 0, span, :] - place[0]
            gap_y = place_ref[o, 1, span, :] - place[1]
            gap_z = place_ref[o, 2, span, :] - place[2]
            square = gap_x * gap_x + gap_y * gap_y + gap_z * gap_z
            reach = jnp.maximum(1.0 - square * lax.rsqrt(jnp.maximum(square, 1e-30)), 0.0)
            reach = reach * reach * reach
            reach_ref[t - part * PART, span, :] = reach * weight
            sum_ref[o, span, :] += reach * ((density - density_ref[o, 0, span, :]) * volume)
        return carry

    def add_group(g, carry):
        start = part * PART + GROUP * g
        stop = jnp.minimum(start + GROUP, count_ref[0])
        lax.fori_loop(start, stop, add_pair, 0)
        reach_copy(span_of(reach_ref, g), span_of(reach_hbm, g), reach_sems, g).start()
        return carry

    lax.fori_loop(0, reach_groups(count_ref, part), add_group, 0)


def reach_end(part, count_ref, reach_ref, reach_hbm, reach_sems):
    def wait_group(g, carry):
        reach_copy(span_of(reach_ref, g), span_of(reach_hbm, g), reach_sems, g).wait()
        return carry

    lax.fori_loop(0, reach_groups(count_ref, part), wait_group, 0)


def reach_kernel(
    ids_ref, pairs_ref, count_ref, wide_hbm, before_hbm, after_hbm, token_ref,
    reach_hbm, place_hbm, density_hbm, sum_hbm, cells_hbm, done_ref,
    wide_ref, before_ref, after_ref, reach_ref, place_ref, density_ref, sum_ref, cells_ref,
    chan_ref, sems, reach_sems,
):
    copies = [
        fetch(wide_hbm, wide_ref, sems, 3),
        fetch(before_hbm.at[pl.ds(0, 128), :], before_ref, sems, 4),
        fetch(after_hbm.at[pl.ds(0, 128), :], after_ref, sems, 5),
    ]
    sum_ref[...] = jnp.zeros_like(sum_ref)
    done_ref[...] = token_ref[...]
    wait_all(copies)
    for i in range(8):
        cells_ref[64 * i : 64 * i + 16] = before_ref[16 * i : 16 * i + 16]
        cells_ref[64 * i + 16 : 64 * i + 48] = wide_ref[32 * i : 32 * i + 32]
        cells_ref[64 * i + 48 : 64 * i + 64] = after_ref[16 * i : 16 * i + 16]
    copies = [fetch(cells_ref, cells_hbm, sems, 2)]
    reach_channels(ids_ref, cells_ref, chan_ref)
    spread_own([chan_ref[i] for i in range(3)], place_ref)
    copies.append(fetch(place_ref, place_hbm, sems, 0))
    spread_own([chan_ref[3]], density_ref)
    copies.append(fetch(density_ref, density_hbm, sems, 6))
    reach_pairs(
        0, pairs_ref, count_ref, chan_ref, place_ref, density_ref,
        reach_ref, reach_hbm, sum_ref, reach_sems,
    )
    copies.append(fetch(sum_ref, sum_hbm, sems, 1))
    reach_end(0, count_ref, reach_ref, reach_hbm, reach_sems)
    wait_all(copies)


def reach_rest_kernel(
    ids_ref, pairs_ref, count_ref, place_hbm, density_hbm, before_hbm, cells_hbm, token_ref,
    reach_hbm, sum_hbm, done_ref,
    reach_ref, place_ref, density_ref, sum_ref, cells_ref, chan_ref, sems, reach_sems,
):
    copies = [
        fetch(cells_hbm, cells_ref, sems, 0),
        fetch(place_hbm, place_ref, sems, 1),
        fetch(density_hbm, density_ref, sems, 2),
        fetch(before_hbm, sum_ref, sems, 3),
    ]
    done_ref[...] = token_ref[...]
    wait_all(copies[:1])
    reach_channels(ids_ref, cells_ref, chan_ref)
    wait_all(copies[1:])
    reach_pairs(
        1, pairs_ref, count_ref, chan_ref, place_ref, density_ref,
        reach_ref, reach_hbm, sum_ref, reach_sems,
    )
    last_copy = fetch(sum_ref, sum_hbm, sems, 4)
    reach_end(1, count_ref, reach_ref, reach_hbm, reach_sems)
    last_copy.wait()


def last_kernel(ids_ref, pairs_ref, count_ref, *refs):
    blocks_hbm, refs = refs[:8], refs[8:]
    (
        before_hbm, eta_hbm, after_hbm, cells_hbm, y_ref, reach_hbm, rest_hbm, place_hbm, sum_hbm, surface_ref, rate_ref,
        blocks, eta_ref, cells_ref, reach_ref, place_ref, sum_ref,
        coef_ref, field_ref, target_ref, speed_ref, half_ref, own_ref, sems, reach_sems,
    ) = refs
    block_copies = [fetch(blocks_hbm[i], blocks.at[i], sems, 4 + i) for i in range(8)]

    for j in range(4):
        lanes = pl.ds(128 * j, 128)
        from_before = before_hbm.at[pl.ds(128 + 16 * j, 16), :]
        from_after = after_hbm.at[pl.ds(128 + 24 * j, 24), :]
        block_copies.append(fetch(from_before, eta_ref.at[pl.ds(0, 16), lanes], sems, 12 + j))
        block_copies.append(fetch(from_after, eta_ref.at[pl.ds(48, 24), lanes], sems, 16 + j))

    def start_group(g, carry):
        reach_copy(span_of(reach_hbm, g), span_of(reach_ref, g), reach_sems, g).start()
        return carry

    def start_rest(g, carry):
        at = g + PART // GROUP
        reach_copy(span_of(rest_hbm, g), span_of(reach_ref, at), reach_sems, at).start()
        return carry

    def wait_group(g, carry):
        reach_copy(span_of(reach_hbm, g), span_of(reach_ref, g), reach_sems, g).wait()
        return carry

    def wait_rest(g, carry):
        at = g + PART // GROUP
        reach_copy(span_of(rest_hbm, g), span_of(reach_ref, at), reach_sems, at).wait()
        return carry

    groups, rest_groups = reach_groups(count_ref, 0), reach_groups(count_ref, 1)
    slab = ids_ref[0]
    layer = ids_ref[1]
    wait_all(block_copies)
    copies = [
        fetch(eta_hbm, eta_ref.at[pl.ds(16, 32), :], sems, 0),
        fetch(cells_hbm, cells_ref, sems, 1),
        fetch(place_hbm, place_ref, sems, 2),
        fetch(sum_hbm, sum_ref, sems, 3),
    ]
    lax.fori_loop(0, groups, start_group, 0)
    lax.fori_loop(0, rest_groups, start_rest, 0)
    for step in range(4):
        share = (layer // 2 + 4 - step) % 4
        lanes = pl.ds(pl.multiple_of(128 * share, 128), 128)
        mine, theirs = blocks.at[step], blocks.at[4 + step]
        for at, size in ((0, ROWS), (ROWS, ROWS), (EARLY, TALL // 2)):
            here = mine[at : at + size, :]
            there = theirs[at : at + size, :]
            first = jnp.where(layer % 2 == 0, here, there)
            second = jnp.where(layer % 2 == 0, there, here)
            first, second = by_share(first, second)
            coef_ref[2 * at : 2 * at + size, lanes] = first
            coef_ref[2 * at + size : 2 * at + 2 * size, lanes] = second
    fields = data_by_table(coef_ref[...], y_ref[0], y_ref[1], NN)
    wait_all(copies[:2])
    parts = [cells_ref[64 * i : 64 * i + 64] for i in range(8)]
    eta = eta_ref[...]
    vertical = (
        fields[4 * ROWS : 5 * ROWS]
        + eta * fields[:ROWS]
        + 0.5 * eta * eta * fields[ROWS : 2 * ROWS]
    )
    surface_ref[...] = vertical[16:48]
    sampled = (fields[2 * ROWS : 3 * ROWS], fields[3 * ROWS : 4 * ROWS], vertical)
    for f in range(3):
        field_ref[2 * f] = sampled[f]
        field_ref[2 * f + 1] = pltpu.roll(sampled[f], NY - 1, 1) - sampled[f]
    row_ids = lax.broadcasted_iota(jnp.int32, (24, 128), 0).astype(F32)

    def sample(cx, carry):
        first_row = pl.multiple_of(16 * cx, 16)
        origin = (32 * slab - 16 + 16 * cx).astype(F32)
        found = [[], [], []]
        place_x = cells_ref[pl.ds(first_row, 16), :] * 8.0 - origin
        place_y = cells_ref[pl.ds(pl.multiple_of(first_row + 64, 16), 16), :] * 64.0
        for cy in range(4):
            for cz in range(4):
                cell = 4 * cy + cz
                along = place_y[cell : cell + 1] - 128.0 * cy
                index = jnp.clip(along.astype(jnp.int32), 0, 127)
                part = along - index.astype(F32)
                index = jnp.broadcast_to(index, (24, 128))
                weight = jnp.maximum(0.0, 1.0 - jnp.abs(place_x[cell : cell + 1] - row_ids))
                weight_next = weight * part
                for f in range(3):
                    here = field_ref[2 * f, pl.ds(first_row, 24), 128 * cy : 128 * cy + 128]
                    step = field_ref[2 * f + 1, pl.ds(first_row, 24), 128 * cy : 128 * cy + 128]
                    here = jnp.take_along_axis(here, index, axis=1)
                    step = jnp.take_along_axis(step, index, axis=1)
                    found[f].append(
                        jnp.sum(weight * here + weight_next * step, axis=0, keepdims=True)
                    )
        for f in range(3):
            target_ref[f, pl.ds(first_row, 16), :] = jnp.concatenate(found[f], 0)
        return carry

    lax.fori_loop(0, 4, sample, 0)
    depth = jnp.exp((parts[2] - 32.0) * (1.0 / 32.0))
    close = jnp.clip(1.0 - parts[0] * (1.0 / 256.0), 0.0, 1.0)
    close = close * close
    for i in range(3):
        half_ref[i] = 0.5 * parts[i]
        speed = parts[3 + i]
        speed_ref[i] = speed + close * (target_ref[i] * depth - speed)
    spread_own([speed_ref[i] for i in range(3)], own_ref)
    wait_all(copies[2:])

    def add_pair(t, carry):
        o = pairs_ref[0, t]
        cell = pairs_ref[1, t]
        place = [half_ref[i, pl.ds(cell, 1), :] for i in range(3)]
        speed = [speed_ref[i, pl.ds(cell, 1), :] for i in range(3)]
        for piece in range(4):
            span = pl.ds(32 * piece, 32)
            approach = 0.0
            for i in range(3):
                approach = approach + (own_ref[o, i, span, :] - speed[i]) * (
                    place_ref[o, i, span, :] - place[i]
                )
            sum_ref[o, span, :] += reach_ref[t, span, :] * approach
        return carry

    def add_group(g, carry):
        wait_group(g, 0)
        stop = jnp.minimum(GROUP * g + GROUP, count_ref[0])
        return lax.fori_loop(GROUP * g, stop, add_pair, carry)

    def add_rest(g, carry):
        wait_rest(g, 0)
        start = PART + GROUP * g
        stop = jnp.minimum(start + GROUP, count_ref[0])
        return lax.fori_loop(start, stop, add_pair, carry)

    lax.fori_loop(0, groups, add_group, 0)
    lax.fori_loop(0, rest_groups, add_rest, 0)
    ones = jnp.ones((8, 384), BF16)
    rates = []
    for o in range(16):
        total = sum_ref[o]
        high, rest = split(total)
        middle, last = split(total - high.astype(F32))
        rates.append(dot(ones, jnp.concatenate([high, middle, last], 1), NT)[:1])
    mass = own_rows(parts[7])
    rate_ref[...] = jnp.where(mass > 0.0, jnp.concatenate(rates, 0), 0.0)


def call(kernel, args, kinds, outs, name, vmem, scratch):
    specs = dict(S=SM, H=HB, V=VM)
    args = [
        pltpu.with_memory_space_constraint(a, pltpu.HBM) if k == "H" else a
        for a, k in zip(args, kinds, strict=True)
    ]
    return pl.pallas_call(
        kernel,
        out_shape=[
            pltpu.HBM(s, F32) if k == "H" else jax.ShapeDtypeStruct(s, F32) for s, k in outs
        ],
        in_specs=[specs[k] for k in kinds],
        out_specs=[specs[k] for _, k in outs],
        scratch_shapes=[pltpu.VMEM(s, F32) if isinstance(s, tuple) else s for s in scratch],
        compiler_params=pltpu.CompilerParams(vmem_limit_bytes=vmem * 1024 * 1024),
        name=name,
    )(*args)


def dma_sems(count):
    return pltpu.SemaphoreType.DMA((count,))


def passed(values, axis, by):
    size = lax.axis_size(axis)
    return lax.ppermute(values, axis, [(i, (i + by) % size) for i in range(size)])


def swap(block, axis):
    return lax.all_to_all(block, axis, split_axis=0, concat_axis=0, tiled=True)


def per_device(eta, phis, particles, cell_count, pair_cells, pair_count):
    slab = lax.axis_index("gx")
    layer = lax.axis_index("gz")
    ids = jnp.stack([slab, layer]).astype(jnp.int32)
    table = tables()
    y = jnp.asarray(table["y"])
    x = jnp.asarray(table["x"])
    own = jnp.asarray(table["own"])

    half_layers = lax.axis_size("gz") // 2

    own_cells, low, high = call(
        pack_kernel, (cell_count, particles), "SH",
        [((128, 128), "H"), ((64, 128), "H"), ((64, 128), "H")], "pack", 4,
        [(8, 2, 4, 2, 128), (128, 128), (64, 128), (64, 128), dma_sems(4)],
    )
    below = passed(high, "gz", 1)
    above = passed(low, "gz", -1)
    wide, up, down = call(
        extend_kernel, (below, own_cells, above, eta), "HHHH",
        [((256, 128), "H"), ((192, 128), "H"), ((224, 128), "H")], "extend", 4,
        [
            (64, 128),
            (128, 128),
            (64, 128),
            (32, NY),
            (256, 128),
            (192, 128),
            (224, 128),
            dma_sems(7),
        ],
    )
    cells_before = passed(up, "gx", 1)
    cells_after = passed(down, "gx", -1)
    pairs = pair_cells.reshape(2, 96)
    count = pair_count.reshape(1)

    (block,) = call(
        start_kernel, (ids, phis, eta, y), "SHHH", [((32, 32, 128), "H")], "start", 4,
        [
            (32, NY),
            (8, NY),
            pltpu.VMEM((2, 64, NY), BF16),
            (32, 128),
            (32, 32, 128),
            dma_sems(3),
            dma_sems(4),
        ],
    )
    gathered = swap(block, "gx").reshape(1024, 128)
    block, first = call(
        first_kernel,
        (ids, gathered, x, wide),
        "SVVH",
        [((8, 128, 128), "H"), ((64, NX), "H")],
        "first",
        8,
        [(8, 128, 128), (64, NX), dma_sems(9)],
    )
    got = swap(block, "gz")
    block, eta_part, curve, token = call(
        second_kernel,
        (got, gathered, y, cells_before, cells_after),
        "VVVHH",
        [((8, 64, 128), "H"), ((128, NY), "H"), ((128, NY), "H"), ((8, 128), "V")],
        "second",
        8,
        [(8, 64, 128), (128, NY), (128, NY), dma_sems(10)],
    )
    got = swap(block, "gz")
    reach, place, density, before, cells, token = call(
        reach_kernel,
        (ids, pairs, count, wide, cells_before, cells_after, token),
        "SSSHHHV",
        [
            ((PART, 128, 128), "H"),
            ((16, 3, 128, 128), "H"),
            ((16, 1, 128, 128), "H"),
            ((16, 128, 128), "H"),
            ((512, 128), "H"),
            ((8, 128), "V"),
        ],
        "reach",
        16,
        [
            (256, 128),
            (128, 128),
            (128, 128),
            (PART, 128, 128),
            (16, 3, 128, 128),
            (16, 1, 128, 128),
            (16, 128, 128),
            (512, 128),
            (6, 64, 128),
            dma_sems(7),
            dma_sems(PART // GROUP),
        ],
    )
    block, second, token = call(
        third_kernel,
        (ids, got, x, token),
        "SVVV",
        [((8, 64, 128), "H"), ((64, NX), "H"), ((8, 128), "V")],
        "third",
        8,
        [(8, 64, 128), (64, NX), dma_sems(9)],
    )
    got = swap(block, "gz")
    rest, before, token = call(
        reach_rest_kernel,
        (ids, pairs, count, place, density, before, cells, token),
        "SSSHHHHV",
        [((REST, 128, 128), "H"), ((16, 128, 128), "H"), ((8, 128), "V")],
        "rest",
        16,
        [
            (REST, 128, 128),
            (16, 3, 128, 128),
            (16, 1, 128, 128),
            (16, 128, 128),
            (512, 128),
            (6, 64, 128),
            dma_sems(5),
            dma_sems(REST // GROUP),
        ],
    )
    block, token = call(
        fourth_kernel,
        (got, eta_part, curve, y, token),
        "VHHVV",
        [((8, 64, 128), "H"), ((8, 128), "V")],
        "fourth",
        8,
        [(8, 64, 128), (128, NY), (128, NY), dma_sems(10)],
    )
    got = swap(block, "gz")
    (early,) = call(
        early_kernel,
        (ids, own, first, second, token),
        "SHHHV",
        [((EARLY, 128), "H")],
        "early",
        8,
        [pltpu.VMEM((TALL, 2 * NX), BF16), (64, NX), (64, NX), (EARLY, 128), dma_sems(4)],
    )
    (block,) = call(
        fifth_kernel,
        (ids, got, x, own, first, second, early),
        "SVVHHHH",
        [((EARLY + TALL // 2, 128), "H")],
        "fifth",
        8,
        [
            pltpu.VMEM((TALL, 2 * NX), BF16),
            (EARLY + TALL // 2, 128),
            (64, NX),
            (64, NX),
            dma_sems(5),
        ],
    )
    along = [block] + [
        lax.ppermute(
            block,
            "gz",
            [
                (2 * i + core, 2 * ((i + step) % half_layers) + core)
                for i in range(half_layers)
                for core in range(2)
            ],
        )
        for step in range(1, half_layers)
    ]
    across = [
        lax.ppermute(b, "gz", [(i, i ^ 1) for i in range(2 * half_layers)]) for b in along
    ]
    surface, rate = call(
        last_kernel,
        (ids, pairs, count, *along, *across, cells_before, eta, cells_after, cells, y, reach, rest, place, before),
        "SSS" + "H" * 12 + "VHHHH",
        [((32, NY), "V"), ((16, 128), "V")],
        "last",
        24,
        [
            (8, EARLY + TALL // 2, 128),
            (ROWS, NY),
            (512, 128),
            (96, 128, 128),
            (16, 3, 128, 128),
            (16, 128, 128),
            (2 * EARLY + TALL, NY),
            (6, ROWS, NY),
            (3, 64, 128),
            (3, 64, 128),
            (3, 64, 128),
            (16, 3, 128, 128),
            dma_sems(20),
            dma_sems(96 // GROUP),
        ],
    )
    return surface, rate.reshape(2, 4, 2, 128)


def solution(mesh):
    in_specs = (
        P("gx", None),
        P("gx", None),
        P(None, "gx", None, "gz", None),
        P("gx", None, "gz"),
        P("gx", "gz", None, None),
        P("gx", "gz", None),
    )
    out_specs = (P("gx", None), P("gx", None, "gz", None))
    return jax.shard_map(
        per_device, mesh=mesh, in_specs=in_specs, out_specs=out_specs, check_vma=False
    )
```
